32 devices in a mesh: orb: 8 (over y, x, core), band: 4 (over z).
Axes of the slice: x: 2, y: 2, z: 4, core: 2. Of those that a mesh axis runs over, the one named last changes fastest.
Arguments:
- blocks: float32 [192, 32, 64, 64], P('orb'), may hold values from -0.125 to 0.125
- columns: int32 [192, 32], P('orb'), may hold values from 0 to 191, as said below
- counts: int32 [192], P('orb'), may hold values from 8 to 32
- vectors: float32 [12288, 1536], P('orb', 'band'), may hold values from -6 to 6
Outputs:
- filtered: float32 [12288, 1536], P('orb', 'band')
- gram: float32 [1536, 1536], P('band', 'orb')
The draws below stay inside these ranges and needn't reach their ends.
Inputs may be any that keep to these rules, and one draw needn't show every extreme that they name: `columns`: block column indices of row r lie within 24 block rows of r, counted cyclically modulo 192, are distinct within a row, and slot 0 holds r itself.
All inputs are finite; a program needn't handle non-finite values.
Results may differ from the reference program's by a relative error of at most 0.000088.
Values sent between devices are 32-bit elements; how exact they have to be, the bound alone decides.
No kernel may reach another device: no remote copies, remote signals or barrier semaphores. Data moves between devices by JAX's collectives and lax.ppermute only.
A program may use at most 192 MiB of HBM per device.

```python
import jax
import jax.numpy as jnp
from jax import lax

BLOCK = 64
BANDS = 1536
SLOTS = 32
ROWS_DEV = 24
NBLK = 192
NORDER = 12288


def draw_columns(key, part):
    key = jax.random.fold_in(key, 11)
    reach = ROWS_DEV
    width = 2 * reach + 1
    rowids = jnp.arange(NBLK, dtype=jnp.int32)[:, None]
    offsets = jnp.arange(width, dtype=jnp.int32)[None, :] - reach
    target = (rowids + offsets) % NBLK
    scores = jax.random.randint(key, (NBLK, width), 0, 2 ** 20) * (width + 1) + (offsets + reach)
    scores = jnp.where(offsets == 0, -1, scores)
    order = jnp.argsort(scores, axis=1)[:, :SLOTS]
    return jnp.take_along_axis(target, order, axis=1).astype(jnp.int32)


def draw_counts(key, part):
    key = jax.random.fold_in(key, 23)
    first_key, second_key = jax.random.split(key)
    base = jax.random.randint(first_key, (NBLK,), SLOTS // 4, SLOTS + 1)
    start = jax.random.randint(second_key, (), 0, NBLK)
    rowids = jnp.arange(NBLK, dtype=jnp.int32)
    dense = (rowids - start) % NBLK < NBLK // 4
    base = jnp.where(dense, SLOTS, base)
    base = jnp.where(rowids == (start + NBLK // 2) % NBLK, SLOTS // 4, base)
    return base.astype(jnp.int32)


def block_scale(own_key, dims, pieces, smallest, high):
    factor_of, own = 1.0, jax.random.fold_in(own_key, 6)
    for dim, parts in pieces:
        heights = jnp.exp(jax.random.uniform(jax.random.fold_in(own, dim), (parts,), jnp.float32, smallest / len(pieces), high / len(pieces)))
        factor_of = factor_of * jnp.repeat(heights, dims[dim] // parts).reshape([-1 if axis == dim else 1 for axis in range(len(dims))])
    return factor_of


def bell_draw(stream_key, extent, scale, most, pieces=(), kind=jnp.bfloat16):
    level = block_scale(stream_key, extent, pieces, -0.22, 0.18) if pieces else 1.0
    values = jax.random.normal(stream_key, extent, jnp.float32) * scale * level
    return jnp.minimum(jnp.maximum(values, -most), most).astype(kind)


def setup_inputs(seed: int = 0) -> dict:
    seeds = jax.random.split(jax.random.key(seed), 5)
    blocks = bell_draw(seeds[0], (NBLK, SLOTS, BLOCK, BLOCK), (SLOTS * BLOCK) ** -0.5, 0.125, ((0, 8),), jnp.float32)
    columns = draw_columns(jax.random.fold_in(seeds[4], 71), 0)
    counts = draw_counts(jax.random.fold_in(seeds[4], 71), 0)
    vectors = bell_draw(seeds[3], (NORDER, BANDS), 1.0, 6.0, ((0, 8), (1, 4)), jnp.float32)
    return {"blocks": blocks, "columns": columns, "counts": counts, "vectors": vectors}


def apply_hamiltonian(blocks, columns, counts, vec):
    stacked = vec.reshape(NBLK, BLOCK, BANDS)
    live = (jnp.arange(SLOTS, dtype=jnp.int32)[None, :] < counts[:, None]).astype(jnp.float32)

    def one_row(item):
        blk, col, alive = item
        picked = stacked[col]
        return jnp.einsum("kij,kjm->im", blk * alive[:, None, None], picked, precision=lax.Precision.HIGHEST)

    out = lax.map(one_row, (blocks, columns, live))
    return out.reshape(NORDER, BANDS)


def reference(blocks, columns, counts, vectors):
    first = (apply_hamiltonian(blocks, columns, counts, vectors) - 0.1 * vectors) / 0.9
    filtered = 2.0 * (apply_hamiltonian(blocks, columns, counts, first) - 0.1 * first) / 0.9 - vectors
    gram = jnp.dot(filtered.T, filtered, precision=lax.Precision.HIGHEST, preferred_element_type=jnp.float32) / NORDER
    return filtered, gram
```

```python
import functools

import jax
import jax.numpy as jnp
from jax import lax
from jax.experimental import pallas as pl
from jax.experimental.pallas import tpu as pltpu
from jax.sharding import PartitionSpec as P

GROUP = 4
LANES = 128
VMEM = 40 * 1024 * 1024


def split(x):
    hi = x.astype(jnp.bfloat16)
    lo = (x - hi.astype(jnp.float32)).astype(jnp.bfloat16)
    return hi, lo


def densify_kernel(slot_ref, blocks_ref, hi_ref, lo_ref, *, spread):
    blk = blocks_ref.shape[2]
    step = pl.program_id(0)

    def one_row(i, carry):
        row = step * GROUP + i
        start = pl.multiple_of(i * blk, blk)
        for pair in range(spread // 2):
            left = slot_ref[row, 2 * pair]
            right = slot_ref[row, 2 * pair + 1]
            lblk = jnp.where(left >= 0, blocks_ref[i, jnp.maximum(left, 0)], 0.0)
            rblk = jnp.where(right >= 0, blocks_ref[i, jnp.maximum(right, 0)], 0.0)
            hi, lo = split(jnp.concatenate([lblk, rblk], axis=1))
            hi_ref[pl.ds(start, blk), pl.ds(pair * 2 * blk, 2 * blk)] = hi
            lo_ref[pl.ds(start, blk), pl.ds(pair * 2 * blk, 2 * blk)] = lo
        return carry

    lax.fori_loop(0, GROUP, one_row, 0)


def densify(slot_of, blocks):
    rows, slots, blk, _ = blocks.shape
    spread = slot_of.shape[1]
    shape = jax.ShapeDtypeStruct((rows * blk, spread * blk), jnp.bfloat16)
    out = pl.BlockSpec((GROUP * blk, spread * blk), lambda g, _: (g, 0))
    return pl.pallas_call(
        functools.partial(densify_kernel, spread=spread),
        grid_spec=pltpu.PrefetchScalarGridSpec(
            num_scalar_prefetch=1,
            grid=(rows // GROUP,),
            in_specs=[pl.BlockSpec((GROUP, slots, blk, blk), lambda g, _: (g, 0, 0, 0))],
            out_specs=[out, out],
        ),
        out_shape=[shape, shape],
        compiler_params=pltpu.CompilerParams(vmem_limit_bytes=VMEM),
        cost_estimate=pl.CostEstimate(flops=0, bytes_accessed=60_000_000, transcendentals=0),
    )(slot_of, blocks)


def apply_kernel(hi_ref, lo_ref, before_ref, own_ref, after_ref, *rest, second):
    old_ref = rest[0] if second else None
    out_ref, parts = rest[-2:]
    step = pl.program_id(0)
    rows, width = own_ref.shape
    tall, wide = hi_ref.shape

    @pl.when(step == 0)
    def _():
        for place, ref in enumerate((before_ref, own_ref, after_ref)):
            hi, lo = split(ref[...])
            parts[pl.ds(place * rows, rows), pl.ds(0, width)] = hi
            parts[pl.ds(place * rows, rows), pl.ds(width, width)] = lo

    start = pl.multiple_of(step * tall, tall)
    both = jnp.dot(hi_ref[...], parts[pl.ds(start, wide), :], preferred_element_type=jnp.float32)
    rest_ = jnp.dot(
        lo_ref[...], parts[pl.ds(start, wide), pl.ds(0, width)], preferred_element_type=jnp.float32
    )
    product = both[:, :width] + (both[:, width:] + rest_)
    own = own_ref[pl.ds(start, tall), :]
    if second:
        out_ref[...] = 2.0 * (product - 0.1 * own) / 0.9 - old_ref[...]
    else:
        out_ref[...] = (product - 0.1 * own) / 0.9


def apply_step(hi, lo, before, own, after, old=None):
    rows, width = own.shape
    wide = hi.shape[1]
    tall = wide - 2 * rows
    steps = rows // tall
    band = pl.BlockSpec((tall, wide), lambda g: (g, 0))
    whole = pl.BlockSpec((rows, width), lambda g: (0, 0))
    piece = pl.BlockSpec((tall, width), lambda g: (g, 0))
    second = old is not None
    return pl.pallas_call(
        functools.partial(apply_kernel, second=second),
        grid=(steps,),
        in_specs=[band, band, whole, whole, whole] + ([piece] if second else []),
        out_specs=piece,
        out_shape=jax.ShapeDtypeStruct((rows, width), jnp.float32),
        scratch_shapes=[pltpu.VMEM((3 * rows, 2 * width), jnp.bfloat16)],
        compiler_params=pltpu.CompilerParams(vmem_limit_bytes=VMEM),
        cost_estimate=pl.CostEstimate(
            flops=8 * rows * wide * width, bytes_accessed=4 * rows * wide, transcendentals=0
        ),
    )(hi, lo, before, own, after, *([old] if second else []))


def slot_table(columns, counts):
    rows, slots = columns.shape
    total = rows * lax.axis_size("orb")
    spread = GROUP + 2 * rows
    ids = jnp.arange(rows, dtype=jnp.int32)
    offset = lax.axis_index("orb") * rows - rows
    place = (columns - offset) % total - (ids // GROUP * GROUP)[:, None]
    number = jnp.arange(slots, dtype=jnp.int32)
    place = jnp.where(number[None, :] < counts[:, None], place, -1)
    hit = place[:, :, None] == jnp.arange(spread, dtype=jnp.int32)[None, None, :]
    return jnp.max(jnp.where(hit, number[None, :, None], -1), axis=1)


def neighbours(x):
    size = lax.axis_size("orb")
    up = [(i, (i + 1) % size) for i in range(size)]
    down = [(j, i) for i, j in up]
    return lax.ppermute(x, "orb", up), lax.ppermute(x, "orb", down)


def after_that(x, done):
    return lax.optimization_barrier((x, done))[0]


def body(blocks, columns, counts, vectors):
    rows, width = vectors.shape
    order_total = rows * lax.axis_size("orb")
    cuts = [(c, min(c + LANES, width)) for c in range(0, width, LANES)]
    hi, lo = densify(slot_table(columns, counts), blocks)
    old = [vectors[:, a:b] for a, b in cuts]
    halo, done = [], None
    for x in old:
        x = x if done is None else after_that(x, done)
        halo.append(neighbours(x))
        done = halo[-1]
    first = [apply_step(hi, lo, h[0], x, h[1]) for x, h in zip(old, halo)]
    halo = []
    for x in first:
        x = after_that(x, done)
        halo.append(neighbours(x))
        done = halo[-1]
    filtered = jnp.concatenate(
        [apply_step(hi, lo, h[0], x, h[1], v) for x, h, v in zip(first, halo, old)], axis=1
    )
    partial_gram = jnp.dot(
        filtered.T,
        lax.all_gather(filtered, "band", axis=1, tiled=True),
        precision=lax.Precision.HIGH,
        preferred_element_type=jnp.float32,
    )
    gram = lax.psum_scatter(partial_gram, "orb", scatter_dimension=1, tiled=True)
    return (filtered, gram / order_total)


def solution(mesh):
    placed = (P("orb", None, None, None), P("orb", None), P("orb"), P("orb", "band"))
    return jax.shard_map(
        body,
        mesh=mesh,
        in_specs=placed,
        out_specs=(P("orb", "band"), P("band", "orb")),
        check_vma=False,
    )
```

```python
import functools

import jax
import jax.numpy as jnp
from jax import lax
from jax.experimental import pallas as pl
from jax.experimental.pallas import tpu as pltpu
from jax.sharding import PartitionSpec as P

GROUP = 4
LANES = 128
VMEM = 40 * 1024 * 1024


def split(x):
    hi = x.astype(jnp.bfloat16)
    lo = (x - hi.astype(jnp.float32)).astype(jnp.bfloat16)
    return hi, lo


def densify_kernel(slot_ref, blocks_ref, hi_ref, lo_ref, *, spread):
    blk = blocks_ref.shape[2]
    step = pl.program_id(0)

    def one_row(i, carry):
        row = step * GROUP + i
        start = pl.multiple_of(i * blk, blk)
        for pair in range(spread // 2):
            left = slot_ref[row, 2 * pair]
            right = slot_ref[row, 2 * pair + 1]
            lblk = jnp.where(left >= 0, blocks_ref[i, jnp.maximum(left, 0)], 0.0)
            rblk = jnp.where(right >= 0, blocks_ref[i, jnp.maximum(right, 0)], 0.0)
            hi, lo = split(jnp.concatenate([lblk, rblk], axis=1))
            hi_ref[pl.ds(start, blk), pl.ds(pair * 2 * blk, 2 * blk)] = hi
            lo_ref[pl.ds(start, blk), pl.ds(pair * 2 * blk, 2 * blk)] = lo
        return carry

    lax.fori_loop(0, GROUP, one_row, 0)


def densify(slot_of, blocks):
    rows, slots, blk, _ = blocks.shape
    spread = slot_of.shape[1]
    shape = jax.ShapeDtypeStruct((rows * blk, spread * blk), jnp.bfloat16)
    out = pl.BlockSpec((GROUP * blk, spread * blk), lambda g, _: (g, 0))
    return pl.pallas_call(
        functools.partial(densify_kernel, spread=spread),
        grid_spec=pltpu.PrefetchScalarGridSpec(
            num_scalar_prefetch=1,
            grid=(rows // GROUP,),
            in_specs=[pl.BlockSpec((GROUP, slots, blk, blk), lambda g, _: (g, 0, 0, 0))],
            out_specs=[out, out],
        ),
        out_shape=[shape, shape],
        compiler_params=pltpu.CompilerParams(vmem_limit_bytes=VMEM),
        cost_estimate=pl.CostEstimate(flops=0, bytes_accessed=60_000_000, transcendentals=0),
    )(slot_of, blocks)


def apply_kernel(hi_ref, lo_ref, before_ref, own_ref, after_ref, *rest, second):
    old_ref = rest[0] if second else None
    out_ref, parts = rest[-2:]
    step = pl.program_id(0)
    rows, width = own_ref.shape
    tall, wide = hi_ref.shape

    @pl.when(step == 0)
    def _():
        for place, ref in enumerate((before_ref, own_ref, after_ref)):
            hi, lo = split(ref[...])
            parts[pl.ds(place * rows, rows), pl.ds(0, width)] = hi
            parts[pl.ds(place * rows, rows), pl.ds(width, width)] = lo

    start = pl.multiple_of(step * tall, tall)
    both = jnp.dot(hi_ref[...], parts[pl.ds(start, wide), :], preferred_element_type=jnp.float32)
    rest_ = jnp.dot(
        lo_ref[...], parts[pl.ds(start, wide), pl.ds(0, width)], preferred_element_type=jnp.float32
    )
    product = both[:, :width] + (both[:, width:] + rest_)
    own = own_ref[pl.ds(start, tall), :]
    if second:
        out_ref[...] = 2.0 * (product - 0.1 * own) / 0.9 - old_ref[...]
    else:
        out_ref[...] = (product - 0.1 * own) / 0.9


def apply_step(hi, lo, before, own, after, old=None):
    rows, width = own.shape
    wide = hi.shape[1]
    tall = wide - 2 * rows
    steps = rows // tall
    band = pl.BlockSpec((tall, wide), lambda g: (g, 0))
    whole = pl.BlockSpec((rows, width), lambda g: (0, 0))
    piece = pl.BlockSpec((tall, width), lambda g: (g, 0))
    second = old is not None
    return pl.pallas_call(
        functools.partial(apply_kernel, second=second),
        grid=(steps,),
        in_specs=[band, band, whole, whole, whole] + ([piece] if second else []),
        out_specs=piece,
        out_shape=jax.ShapeDtypeStruct((rows, width), jnp.float32),
        scratch_shapes=[pltpu.VMEM((3 * rows, 2 * width), jnp.bfloat16)],
        compiler_params=pltpu.CompilerParams(vmem_limit_bytes=VMEM),
        cost_estimate=pl.CostEstimate(
            flops=8 * rows * wide * width, bytes_accessed=4 * rows * wide, transcendentals=0
        ),
    )(hi, lo, before, own, after, *([old] if second else []))


def slot_table(columns, counts):
    rows, slots = columns.shape
    total = rows * lax.axis_size("orb")
    spread = GROUP + 2 * rows
    ids = jnp.arange(rows, dtype=jnp.int32)
    offset = lax.axis_index("orb") * rows - rows
    place = (columns - offset) % total - (ids // GROUP * GROUP)[:, None]
    number = jnp.arange(slots, dtype=jnp.int32)
    place = jnp.where(number[None, :] < counts[:, None], place, -1)
    hit = place[:, :, None] == jnp.arange(spread, dtype=jnp.int32)[None, None, :]
    return jnp.max(jnp.where(hit, number[None, :, None], -1), axis=1)


def neighbours(x):
    size = lax.axis_size("orb")
    up = [(i, (i + 1) % size) for i in range(size)]
    down = [(j, i) for i, j in up]
    return lax.ppermute(x, "orb", up), lax.ppermute(x, "orb", down)


def after_that(x, *done):
    return lax.optimization_barrier((x, done))[0]


def prep_kernel(band_ref, *refs):
    ins, (hi_ref, lo_ref, thi_ref, tlo_ref) = refs[:4], refs[4:]
    for place, ref in enumerate(ins):
        band = band_ref[place]
        x = ref[...]
        hi_ref[band], lo_ref[band] = split(x)
        thi_ref[band], tlo_ref[band] = split(x.T)


def prep(bands, parts):
    rows, width = parts[0].shape
    plain = jax.ShapeDtypeStruct((4, rows, width), jnp.bfloat16)
    turned = jax.ShapeDtypeStruct((4, width, rows), jnp.bfloat16)
    return pl.pallas_call(
        prep_kernel,
        in_specs=[pl.BlockSpec(memory_space=pltpu.SMEM)] + [pl.BlockSpec(memory_space=pltpu.VMEM)] * 4,
        out_specs=[pl.BlockSpec(memory_space=pltpu.VMEM)] * 4,
        out_shape=[plain, plain, turned, turned],
        compiler_params=pltpu.CompilerParams(vmem_limit_bytes=VMEM),
        cost_estimate=pl.CostEstimate(flops=0, bytes_accessed=32 * rows * width, transcendentals=0),
    )(bands, *parts)


def product_kernel(target_ref, thi_ref, tlo_ref, *rest):
    *ins, out_ref = rest
    count = len(ins) // 2
    four, width, rows = thi_ref.shape
    thi = thi_ref[...].reshape(four * width, rows)
    tlo = tlo_ref[...].reshape(four * width, rows)
    his = jnp.concatenate([ref[0] for ref in ins[:count]], axis=1)
    both = jnp.concatenate([his] + [ref[0] for ref in ins[count:]], axis=1)
    size = his.shape[1]
    big = jnp.dot(thi, both, preferred_element_type=jnp.float32)
    small = jnp.dot(tlo, his, preferred_element_type=jnp.float32)
    out_ref[0] = big[:, :size] + (big[:, size:] + small)


def products(targets, thi, tlo, his, los):
    four, width, rows = thi.shape
    size = sum(x.shape[2] for x in his)
    whole = pl.BlockSpec((four, width, rows), lambda g, t: (0, 0, 0))
    picked = [pl.BlockSpec((1, rows, x.shape[2]), lambda g, t: (t[g], 0, 0)) for x in his]
    return pl.pallas_call(
        product_kernel,
        grid_spec=pltpu.PrefetchScalarGridSpec(
            num_scalar_prefetch=1,
            grid=(targets.shape[0],),
            in_specs=[whole, whole] + picked + picked,
            out_specs=pl.BlockSpec((1, four * width, size), lambda g, t: (g, 0, 0)),
        ),
        out_shape=jax.ShapeDtypeStruct((targets.shape[0], four * width, size), jnp.float32),
        compiler_params=pltpu.CompilerParams(vmem_limit_bytes=VMEM),
        cost_estimate=pl.CostEstimate(
            flops=targets.shape[0] * 8 * four * width * rows * size,
            bytes_accessed=8 * four * width * rows,
            transcendentals=0,
        ),
    )(targets, thi, tlo, *his, *los)


def linear(chip, core, z):
    return (chip * 2 + core) * 4 + z


def send(x, pairs):
    return lax.ppermute(x, ("orb", "band"), pairs)


def mirrored(pairs):
    out = []
    for chip in range(4):
        for a, b in pairs:
            out.append((linear(chip, 0, a), linear(chip, 0, b)))
            out.append((linear(chip, 1, 3 - a), linear(chip, 1, 3 - b)))
    return out


def gather_bands(x):
    return [x] + [send(x, mirrored([(source, 2)])) for source in (0, 1, 3)]


def over_chips(flip):
    return [
        (linear(chip, core, 2 - core), linear(chip ^ flip, core, 2 - core))
        for chip in range(4)
        for core in range(2)
    ]


class GramPlan:
    def __init__(self):
        orb, self.z = lax.axis_index("orb"), lax.axis_index("band")
        self.chip, self.core = orb // 2, orb % 2
        order = jnp.asarray([[2, 0, 1, 3], [1, 3, 2, 0]], jnp.int32)
        self.bands = order[self.core]
        self.holder = self.z == 2 - self.core
        self.his, self.los = [], []

    def add_chunk(self, parts):
        hi, lo, thi, tlo = prep(self.bands, parts)
        self.his.append(hi)
        self.los.append(lo)
        far = jnp.stack([self.chip ^ 2, self.chip ^ 3])
        near = jnp.stack([self.chip, self.chip ^ 1])
        theirs = products(far, thi, tlo, self.his, self.los)
        got = send(theirs, over_chips(2))
        ours = products(near, thi, tlo, self.his, self.los)
        return got, ours

    def reduce(self, got, ours):
        got_x = send(got[1] + ours[1], over_chips(1))
        total = got[0] + ours[0] + got_x
        total = total.reshape(4, total.shape[0] // 4, total.shape[1])
        piece = jnp.where(self.holder, lax.dynamic_index_in_dim(total, self.z, 0, False), 0.0)
        for z in (0, 1, 3):
            goal = jnp.where(self.core == 0, z, 3 - z)
            moved = lax.dynamic_index_in_dim(total, goal, 0, False)
            piece = piece + send(moved, mirrored([(2, z)]))
        swap = [(linear(q, c, z), linear(q, 1 - c, z)) for q in range(4) for c in range(2) for z in range(4)]
        piece = piece + send(piece, swap)
        turn = [(linear(q, c, z), linear(z, c, q)) for q in range(4) for c in range(2) for z in range(4)]
        return piece, send(piece, turn).T

    def assemble(self, pieces, widths):
        rows = []
        for r in range(len(widths)):
            row = [pieces[r][0]]
            start = sum(widths[:r])
            for c in range(r + 1, len(widths)):
                row.append(pieces[c][1][start : start + widths[r], :])
            rows.append(jnp.concatenate(row, axis=1))
        gram = jnp.concatenate(rows, axis=0)
        half = gram.shape[1] // 2
        return jnp.where(self.core == 0, gram[:, :half], gram[:, half:])


def simple_gram(filtered):
    partial_gram = jnp.dot(
        filtered.T,
        lax.all_gather(filtered, "band", axis=1, tiled=True),
        precision=lax.Precision.HIGH,
        preferred_element_type=jnp.float32,
    )
    return lax.psum_scatter(partial_gram, "orb", scatter_dimension=1, tiled=True)


def body(blocks, columns, counts, vectors, by_symmetry):
    rows, width = vectors.shape
    order_total = rows * lax.axis_size("orb")
    widths = [min(LANES, width - c) for c in range(0, width, LANES)]
    starts = [sum(widths[:c]) for c in range(len(widths))]
    hi, lo = densify(slot_table(columns, counts), blocks)
    old = [vectors[:, a : a + w] for a, w in zip(starts, widths)]
    count = len(widths)
    halos, first, filtered = {}, [], []
    order = [("v", 0)]
    for c in range(count):
        if c + 1 < count:
            order.append(("v", c + 1))
        order.append(("f", c))
    done = None
    for kind, c in order:
        if kind == "v":
            x = old[c]
        else:
            first.append(apply_step(hi, lo, halos["v", c][0], old[c], halos["v", c][1]))
            x = first[c]
        if done is not None:
            x = after_that(x, *done)
        halos[kind, c] = neighbours(x)
        done = halos[kind, c] if done is not None else halos[kind, c] + (hi,)
    for c in range(count):
        h = halos["f", c]
        filtered.append(apply_step(hi, lo, h[0], first[c], h[1], old[c]))
    if by_symmetry:
        plan = GramPlan()
        partial = [plan.add_chunk(gather_bands(x)) for x in filtered]
        gram = plan.assemble([plan.reduce(*p) for p in partial], widths)
    else:
        gram = simple_gram(jnp.concatenate(filtered, axis=1))
    return (jnp.concatenate(filtered, axis=1), gram / order_total)


def solution(mesh):
    placed = (P("orb", None, None, None), P("orb", None), P("orb"), P("orb", "band"))
    by_symmetry = mesh.shape["orb"] == 8 and mesh.shape["band"] == 4
    return jax.shard_map(
        functools.partial(body, by_symmetry=by_symmetry),
        mesh=mesh,
        in_specs=placed,
        out_specs=(P("orb", "band"), P("band", "orb")),
        check_vma=False,
    )
```

```python
import functools

import jax
import jax.numpy as jnp
from jax import lax
from jax.experimental import pallas as pl
from jax.experimental.pallas import tpu as pltpu
from jax.sharding import PartitionSpec as P

GROUP = 4
LANES = 128
MIB = 1024 * 1024


def split(x):
    hi = x.astype(jnp.bfloat16)
    lo = (x - hi.astype(jnp.float32)).astype(jnp.bfloat16)
    return hi, lo


def folds(rows, width):
    count = LANES // width if LANES % width == 0 else 1
    return count if rows % (count * 256) == 0 else 1


def fold(x, count):
    return jnp.concatenate(jnp.split(x, count, axis=0), axis=1) if count > 1 else x


def unfold(x, count):
    return jnp.concatenate(jnp.split(x, count, axis=1), axis=0) if count > 1 else x


def densify_kernel(slot_ref, blocks_ref, hi_ref, lo_ref, *, spread, reach):
    blk = blocks_ref.shape[2]
    step = pl.program_id(0)
    tile = (blk, 2 * blk)
    shift = lax.broadcasted_iota(jnp.int32, tile, 1) - lax.broadcasted_iota(jnp.int32, tile, 0)

    def one_row(i, carry):
        row = step * GROUP + i
        start = pl.multiple_of(i * blk, blk)
        for pair in range(spread // 2):
            left = slot_ref[row, 2 * pair]
            right = slot_ref[row, 2 * pair + 1]
            lblk = jnp.where(left >= 0, blocks_ref[i, jnp.maximum(left, 0)], 0.0)
            rblk = jnp.where(right >= 0, blocks_ref[i, jnp.maximum(right, 0)], 0.0)
            both = jnp.concatenate([lblk, rblk], axis=1)
            if reach <= 2 * pair + 1 and 2 * pair < reach + GROUP:
                both = both - jnp.where(shift == (reach + i - 2 * pair) * blk, 0.1, 0.0)
            hi, lo = split(both / 0.9)
            hi_ref[pl.ds(start, blk), pl.ds(pair * 2 * blk, 2 * blk)] = hi
            lo_ref[pl.ds(start, blk), pl.ds(pair * 2 * blk, 2 * blk)] = lo
        return carry

    lax.fori_loop(0, GROUP, one_row, 0)


def densify(slot_of, blocks):
    rows, slots, blk, _ = blocks.shape
    spread = slot_of.shape[1]
    shape = jax.ShapeDtypeStruct((rows * blk, spread * blk), jnp.bfloat16)
    out = pl.BlockSpec((GROUP * blk, spread * blk), lambda g, _: (g, 0))
    return pl.pallas_call(
        functools.partial(densify_kernel, spread=spread, reach=rows),
        grid_spec=pltpu.PrefetchScalarGridSpec(
            num_scalar_prefetch=1,
            grid=(rows // GROUP,),
            in_specs=[pl.BlockSpec((GROUP, slots, blk, blk), lambda g, _: (g, 0, 0, 0))],
            out_specs=[out, out],
        ),
        out_shape=[shape, shape],
        compiler_params=pltpu.CompilerParams(vmem_limit_bytes=20 * MIB),
        cost_estimate=pl.CostEstimate(flops=0, bytes_accessed=60_000_000, transcendentals=0),
    )(slot_of, blocks)


def apply_kernel(hi_ref, lo_ref, before_ref, own_ref, after_ref, *rest, second, count):
    old_ref = rest[0] if second else None
    out_ref, parts = rest[-2:]
    step = pl.program_id(0)
    rows, width = own_ref.shape[0] * count, own_ref.shape[1] // count
    tall, wide = hi_ref.shape
    short = rows // count

    @pl.when(step == 0)
    def _():
        for place, ref in enumerate((before_ref, own_ref, after_ref)):
            for k in range(count):
                hi, lo = split(ref[:, pl.ds(k * width, width)])
                there = pl.ds(place * rows + k * short, short)
                parts[there, pl.ds(0, width)] = hi
                parts[there, pl.ds(width, width)] = lo

    start = pl.multiple_of(step * tall, tall)
    both = jnp.dot(hi_ref[...], parts[pl.ds(start, wide), :], preferred_element_type=jnp.float32)
    other = jnp.dot(
        lo_ref[...], parts[pl.ds(start, wide), pl.ds(0, width)], preferred_element_type=jnp.float32
    )
    product = both[:, :width] + (both[:, width:] + other)
    for k in range(count):

        @pl.when((step * tall) // short == k)
        def _():
            there = pl.ds(pl.multiple_of(step * tall - k * short, tall), tall)
            lanes = pl.ds(k * width, width)
            if second:
                out_ref[there, lanes] = 2.0 * product - old_ref[there, lanes]
            else:
                out_ref[there, lanes] = product


def apply_step(hi, lo, before, own, after, count, old=None):
    short, lanes = own.shape
    rows, width = short * count, lanes // count
    wide = hi.shape[1]
    tall = wide - 2 * rows
    band = pl.BlockSpec((tall, wide), lambda g: (g, 0))
    whole = pl.BlockSpec((short, lanes), lambda g: (0, 0))
    second = old is not None
    return pl.pallas_call(
        functools.partial(apply_kernel, second=second, count=count),
        grid=(rows // tall,),
        in_specs=[band, band, whole, whole, whole] + ([whole] if second else []),
        out_specs=whole,
        out_shape=jax.ShapeDtypeStruct((short, lanes), jnp.float32),
        scratch_shapes=[pltpu.VMEM((3 * rows, 2 * width), jnp.bfloat16)],
        compiler_params=pltpu.CompilerParams(vmem_limit_bytes=22 * MIB),
        cost_estimate=pl.CostEstimate(
            flops=8 * rows * wide * width, bytes_accessed=4 * rows * wide, transcendentals=0
        ),
    )(hi, lo, before, own, after, *([old] if second else []))


def slot_table(columns, counts):
    rows, slots = columns.shape
    total = rows * lax.axis_size("orb")
    spread = GROUP + 2 * rows
    ids = jnp.arange(rows, dtype=jnp.int32)
    offset = lax.axis_index("orb") * rows - rows
    place = (columns - offset) % total - (ids // GROUP * GROUP)[:, None]
    number = jnp.arange(slots, dtype=jnp.int32)
    place = jnp.where(number[None, :] < counts[:, None], place, -1)
    hit = place[:, :, None] == jnp.arange(spread, dtype=jnp.int32)[None, None, :]
    return jnp.max(jnp.where(hit, number[None, :, None], -1), axis=1)


def neighbours(x):
    size = lax.axis_size("orb")
    up = [(i, (i + 1) % size) for i in range(size)]
    down = [(j, i) for i, j in up]
    return lax.ppermute(x, "orb", up), lax.ppermute(x, "orb", down)


def after_that(x, *done):
    return lax.optimization_barrier((x, done))[0]


def prep_kernel(band_ref, *refs, count):
    ins, (hi_ref, lo_ref, thi_ref, tlo_ref) = refs[:4], refs[4:]
    for place, ref in enumerate(ins):
        band = band_ref[place]
        short, width = ref.shape[0], ref.shape[1] // count
        for k in range(count):
            x = ref[:, pl.ds(k * width, width)]
            there = pl.ds(k * short, short)
            hi_ref[band, there, :], lo_ref[band, there, :] = split(x)
            thi_ref[band, :, there], tlo_ref[band, :, there] = split(x.T)


def prep(bands, parts, count):
    short, lanes = parts[0].shape
    rows, width = short * count, lanes // count
    plain = jax.ShapeDtypeStruct((4, rows, width), jnp.bfloat16)
    turned = jax.ShapeDtypeStruct((4, width, rows), jnp.bfloat16)
    return pl.pallas_call(
        functools.partial(prep_kernel, count=count),
        in_specs=[pl.BlockSpec(memory_space=pltpu.SMEM)] + [pl.BlockSpec(memory_space=pltpu.VMEM)] * 4,
        out_specs=[pl.BlockSpec(memory_space=pltpu.VMEM)] * 4,
        out_shape=[plain, plain, turned, turned],
        compiler_params=pltpu.CompilerParams(vmem_limit_bytes=16 * MIB),
        cost_estimate=pl.CostEstimate(flops=0, bytes_accessed=32 * rows * width, transcendentals=0),
    )(bands, *parts)


def product_kernel(target_ref, *refs, shapes):
    refs, out_ref = list(refs[:-1]), refs[-1]
    start = 0
    for columns in shapes:
        thi_ref, tlo_ref = refs[:2]
        ins, refs = refs[2 : 2 + 2 * columns], refs[2 + 2 * columns :]
        four, width, rows = thi_ref.shape
        thi = thi_ref[...].reshape(four * width, rows)
        tlo = tlo_ref[...].reshape(four * width, rows)
        his = jnp.concatenate([ref[0] for ref in ins[:columns]], axis=1)
        los = jnp.concatenate([ref[0] for ref in ins[columns:]], axis=1)
        total = jnp.dot(thi, los, preferred_element_type=jnp.float32)
        total += jnp.dot(tlo, his, preferred_element_type=jnp.float32)
        total += jnp.dot(thi, his, preferred_element_type=jnp.float32)
        out_ref[0, :, pl.ds(start, his.shape[1])] = total
        start += his.shape[1]


def products(targets, chunks, lines):
    ins, specs, shapes, size, flops = [], [], [], 0, 0
    for line in lines:
        hi, lo, thi, tlo = chunks[line]
        four, width, rows = thi.shape
        ins += [thi, tlo]
        specs += [pl.BlockSpec((four, width, rows), lambda g, t: (0, 0, 0))] * 2
        for part in (0, 1):
            for c in range(line + 1):
                x = chunks[c][part]
                ins.append(x)
                specs.append(pl.BlockSpec((1, rows, x.shape[2]), lambda g, t: (t[g], 0, 0)))
        wide = sum(chunks[c][0].shape[2] for c in range(line + 1))
        shapes.append(line + 1)
        size += wide
        flops += 6 * four * width * rows * wide
    return pl.pallas_call(
        functools.partial(product_kernel, shapes=shapes),
        grid_spec=pltpu.PrefetchScalarGridSpec(
            num_scalar_prefetch=1,
            grid=(targets.shape[0],),
            in_specs=specs,
            out_specs=pl.BlockSpec((1, four * width, size), lambda g, t: (g, 0, 0)),
        ),
        out_shape=jax.ShapeDtypeStruct((targets.shape[0], four * width, size), jnp.float32),
        compiler_params=pltpu.CompilerParams(vmem_limit_bytes=28 * MIB),
        cost_estimate=pl.CostEstimate(
            flops=targets.shape[0] * flops, bytes_accessed=8_000_000, transcendentals=0
        ),
    )(targets, *ins)


def linear(chip, core, z):
    return (chip * 2 + core) * 4 + z


def send(x, pairs):
    return lax.ppermute(x, ("orb", "band"), pairs)


def mirrored(pairs):
    out = []
    for chip in range(4):
        for a, b in pairs:
            out.append((linear(chip, 0, a), linear(chip, 0, b)))
            out.append((linear(chip, 1, 3 - a), linear(chip, 1, 3 - b)))
    return out


def gather_bands(x):
    return [x] + [send(x, mirrored([(source, 2)])) for source in (0, 1, 3)]


def over_chips(flip):
    return [
        (linear(chip, core, 2 - core), linear(chip ^ flip, core, 2 - core))
        for chip in range(4)
        for core in range(2)
    ]


class GramPlan:
    def __init__(self, rows, widths, counts):
        orb, self.z = lax.axis_index("orb"), lax.axis_index("band")
        self.chip, self.core = orb // 2, orb % 2
        order = jnp.asarray([[2, 0, 1, 3], [1, 3, 2, 0]], jnp.int32)
        self.bands = order[self.core]
        self.holder = self.z == 2 - self.core
        self.widths, self.counts = widths, counts
        self.chunks = []

    def add(self, parts):
        self.chunks.append(prep(self.bands, parts, self.counts[len(self.chunks)]))

    def far(self, lines, flip):
        targets = jnp.stack([self.chip ^ flip, self.chip ^ 3])
        theirs = products(targets, self.chunks, lines)
        return send(theirs, over_chips(flip)), theirs

    def near(self, lines, flip, theirs):
        targets = after_that(jnp.stack([self.chip, self.chip ^ flip ^ 3]), theirs)
        return products(targets, self.chunks, lines)

    def total(self, got, ours, flip):
        last = send(got[1] + ours[1], over_chips(flip ^ 3))
        out = got[0] + ours[0] + last
        return out.reshape(4, out.shape[0] // 4, out.shape[1])

    def finish(self, totals):
        total = jnp.concatenate(
            [jnp.pad(t, ((0, 0), (0, 0), (0, totals[0].shape[2] - t.shape[2]))) for t in totals], axis=1
        )
        piece = jnp.where(self.holder, lax.dynamic_index_in_dim(total, self.z, 0, False), 0.0)
        for z in (0, 1, 3):
            goal = jnp.where(self.core == 0, z, 3 - z)
            moved = lax.dynamic_index_in_dim(total, goal, 0, False)
            piece = piece + send(moved, mirrored([(2, z)]))
        swap = [(linear(q, c, z), linear(q, 1 - c, z)) for q in range(4) for c in range(2) for z in range(4)]
        piece = piece + send(piece, swap)
        w0, w1, w2, w3 = self.widths
        high = piece[:w0]
        own = [high[:, :w0], high[:, w0:], piece[w0 : w0 + w2, : w0 + w1 + w2], piece[w0 + w2 :]]
        half = w1 // 2
        small = jnp.where(self.core == 0, own[1][:half, :w0], own[1][half:, :w0])
        turn = [[(linear(q, c, z), linear(z, c, q)) for q in range(4) for z in range(4)] for c in range(2)]
        small = send(small, turn[0] + turn[1])
        large = send(piece[w0:], turn[1])
        first = jnp.concatenate([own[0], own[1][:, :w0], own[2][:, :w0], own[3][:, :w0]], axis=0)
        middle = [small.T, own[1][:, w0:], own[2][:, w0 : w0 + w1], own[3][:, w0 : w0 + w1]]
        left = [x if x is middle[0] else x[:, :half] for x in middle]
        right = [x if x is middle[0] else x[:, half:] for x in middle]
        left = jnp.concatenate([first, jnp.concatenate(left, axis=0)], axis=1)
        turned = large.T
        second = [turned[: w0 + w1, :w2], own[2][:, w0 + w1 :], own[3][:, w0 + w1 : w0 + w1 + w2]]
        third = [turned[: w0 + w1 + w2, w2:], own[3][:, w0 + w1 + w2 :]]
        right = jnp.concatenate(
            [jnp.concatenate(x, axis=0) for x in (right, second, third)], axis=1
        )
        return jnp.where(self.core == 0, left, right)


def simple_gram(filtered):
    partial_gram = jnp.dot(
        filtered.T,
        lax.all_gather(filtered, "band", axis=1, tiled=True),
        precision=lax.Precision.HIGH,
        preferred_element_type=jnp.float32,
    )
    return lax.psum_scatter(partial_gram, "orb", scatter_dimension=1, tiled=True)


def in_turn(hi, lo, old, counts, rows):
    first, filtered = [], []
    for x, count in zip(old, counts):
        before, after = neighbours(x)
        first.append(apply_step(hi, lo, before, x, after, count))
    for x, v, count in zip(first, old, counts):
        before, after = neighbours(x)
        filtered.append(apply_step(hi, lo, before, x, after, count, v))
    return filtered, simple_gram(
        jnp.concatenate([unfold(x, count) for x, count in zip(filtered, counts)], axis=1)
    )


def by_symmetry(hi, lo, old, counts, rows, widths):
    def one(x, halo, c, v=None):
        return apply_step(hi, lo, halo[0], x, halo[1], counts[c], v)

    plan = GramPlan(rows, widths, counts)
    v0, v1, v2, v3 = old
    hv0 = neighbours(v0)
    hv1 = neighbours(after_that(v1, hi, *hv0))
    f0 = one(v0, hv0, 0)
    hf0 = neighbours(f0)
    f1 = one(v1, hv1, 1)
    hv2 = neighbours(after_that(v2, f1, *hf0))
    g0 = one(f0, hf0, 0, v0)
    z0 = gather_bands(g0)
    f1 = after_that(f1, g0)
    hf1 = neighbours(f1)
    f2 = one(after_that(v2, g0), hv2, 2)
    hv3 = neighbours(after_that(v3, f2, *hf1))
    g1 = one(after_that(f1, f2), hf1, 1, v1)
    z1 = gather_bands(g1)
    f2 = after_that(f2, g1)
    hf2 = neighbours(f2)
    f3 = one(after_that(v3, g1), hv3, 3)
    hf3 = neighbours(f3)
    z0[0] = after_that(z0[0], f3)
    plan.add(z0)
    g2 = one(after_that(f2, plan.chunks[0][0]), hf2, 2, v2)
    z2 = gather_bands(g2)
    g3 = one(after_that(f3, g2), hf3, 3, v3)
    z3 = gather_bands(g3)
    z1[0] = after_that(z1[0], g3)
    plan.add(z1)
    got_a, theirs = plan.far([0, 1], 2)
    ours_a = plan.near([0, 1], 2, theirs)
    z2[0] = after_that(z2[0], ours_a)
    plan.add(z2)
    got_b, theirs = plan.far([2], 1)
    ours_b = plan.near([2], 1, theirs)
    z3[0] = after_that(z3[0], ours_b)
    plan.add(z3)
    got_c, theirs = plan.far([3], 1)
    ours_c = plan.near([3], 1, theirs)
    totals = [plan.total(got_a, ours_a, 2), plan.total(got_b, ours_b, 1), plan.total(got_c, ours_c, 1)]
    return [g0, g1, g2, after_that(g3, ours_c)], plan.finish(totals)


def body(blocks, columns, counts, vectors, symmetric):
    rows, width = vectors.shape
    order_total = rows * lax.axis_size("orb")
    if symmetric:
        widths = [LANES, LANES, LANES // 2, LANES // 2]
    else:
        widths = [min(LANES, width - c) for c in range(0, width, LANES)]
    counts_of = [folds(rows, w) for w in widths]
    slot_of = slot_table(columns, counts)
    hi, lo = densify(slot_of, blocks)
    old = []
    for c, (w, count) in enumerate(zip(widths, counts_of)):
        start = sum(widths[:c])
        source = after_that(vectors, slot_of) if c else vectors
        old.append(fold(source[:, start : start + w], count))
    if symmetric:
        filtered, gram = by_symmetry(hi, lo, old, counts_of, rows, widths)
    else:
        filtered, gram = in_turn(hi, lo, old, counts_of, rows)
    filtered = jnp.concatenate([unfold(x, n) for x, n in zip(filtered, counts_of)], axis=1)
    return (filtered, gram / order_total)


def solution(mesh):
    placed = (P("orb", None, None, None), P("orb", None), P("orb"), P("orb", "band"))
    return jax.shard_map(
        lambda blocks, columns, counts, vectors: body(
            blocks,
            columns,
            counts,
            vectors,
            mesh.shape["orb"] == 8 and mesh.shape["band"] == 4 and vectors.shape[1] == 3 * LANES,
        ),
        mesh=mesh,
        in_specs=placed,
        out_specs=(P("orb", "band"), P("band", "orb")),
        check_vma=False,
    )
```

```python
import functools

import jax
import jax.numpy as jnp
from jax import lax
from jax.experimental import pallas as pl
from jax.experimental.pallas import tpu as pltpu
from jax.sharding import PartitionSpec as P

GROUP = 4
LANES = 128
MIB = 1024 * 1024
APPLY_MIB = 14


def split(x):
    hi = x.astype(jnp.bfloat16)
    lo = (x - hi.astype(jnp.float32)).astype(jnp.bfloat16)
    return hi, lo


def densify_kernel(slot_ref, blocks_ref, hi_ref, lo_ref, *, spread, reach):
    blk = blocks_ref.shape[2]
    step = pl.program_id(0)
    tile = (blk, 2 * blk)
    shift = lax.broadcasted_iota(jnp.int32, tile, 1) - lax.broadcasted_iota(jnp.int32, tile, 0)

    def one_row(i, carry):
        row = step * GROUP + i
        start = pl.multiple_of(i * blk, blk)
        for pair in range(spread // 2):
            left = slot_ref[row, 2 * pair]
            right = slot_ref[row, 2 * pair + 1]
            lblk = jnp.where(left >= 0, blocks_ref[i, jnp.maximum(left, 0)], 0.0)
            rblk = jnp.where(right >= 0, blocks_ref[i, jnp.maximum(right, 0)], 0.0)
            both = jnp.concatenate([lblk, rblk], axis=1)
            if reach <= 2 * pair + 1 and 2 * pair < reach + GROUP:
                both = both - jnp.where(shift == (reach + i - 2 * pair) * blk, 0.1, 0.0)
            hi, lo = split(both / 0.9)
            hi_ref[pl.ds(start, blk), pl.ds(pair * 2 * blk, 2 * blk)] = hi
            lo_ref[pl.ds(start, blk), pl.ds(pair * 2 * blk, 2 * blk)] = lo
        return carry

    lax.fori_loop(0, GROUP, one_row, 0)


def densify(slot_of, blocks):
    rows, slots, blk, _ = blocks.shape
    spread = slot_of.shape[1]
    shape = pltpu.VMEM((rows * blk, spread * blk), jnp.bfloat16)
    out = pl.BlockSpec((GROUP * blk, spread * blk), lambda g, _: (g, 0))
    return pl.pallas_call(
        functools.partial(densify_kernel, spread=spread, reach=rows),
        grid_spec=pltpu.PrefetchScalarGridSpec(
            num_scalar_prefetch=1,
            grid=(rows // GROUP,),
            in_specs=[pl.BlockSpec((GROUP, slots, blk, blk), lambda g, _: (g, 0, 0, 0))],
            out_specs=[out, out],
        ),
        out_shape=[shape, shape],
        compiler_params=pltpu.CompilerParams(vmem_limit_bytes=20 * MIB),
        cost_estimate=pl.CostEstimate(flops=0, bytes_accessed=60_000_000, transcendentals=0),
    )(slot_of, blocks)


def apply_kernel(hi_ref, lo_ref, before_ref, own_ref, after_ref, *rest, second):
    old_ref = rest[0] if second else None
    out_ref, parts = rest[-2:]
    rows, width = own_ref.shape
    wide = hi_ref.shape[1]
    tall = wide - 2 * rows
    for place, ref in enumerate((before_ref, own_ref, after_ref)):
        there = pl.ds(place * rows, rows)
        parts[there, pl.ds(0, width)], parts[there, pl.ds(width, width)] = split(ref[...])

    def one_group(step, carry):
        start = pl.multiple_of(step * tall, tall)
        here = pl.ds(start, tall)
        reached = pl.ds(start, wide)
        both = jnp.dot(hi_ref[here, :], parts[reached, :], preferred_element_type=jnp.float32)
        other = jnp.dot(
            lo_ref[here, :], parts[reached, pl.ds(0, width)], preferred_element_type=jnp.float32
        )
        product = both[:, :width] + (both[:, width:] + other)
        if second:
            product = 2.0 * product - old_ref[here, :]
        out_ref[here, :] = product
        return carry

    lax.fori_loop(0, rows // tall, one_group, 0)


def apply_step(hi, lo, before, own, after, old=None):
    rows, width = own.shape
    wide = hi.shape[1]
    second = old is not None
    hi, lo = (pltpu.with_memory_space_constraint(x, pltpu.VMEM) for x in (hi, lo))
    vmem = pl.BlockSpec(memory_space=pltpu.VMEM)
    return pl.pallas_call(
        functools.partial(apply_kernel, second=second),
        in_specs=[vmem] * (6 if second else 5),
        out_specs=vmem,
        out_shape=jax.ShapeDtypeStruct((rows, width), jnp.float32),
        scratch_shapes=[pltpu.VMEM((3 * rows, 2 * width), jnp.bfloat16)],
        compiler_params=pltpu.CompilerParams(vmem_limit_bytes=APPLY_MIB * MIB),
        cost_estimate=pl.CostEstimate(
            flops=8 * rows * wide * width, bytes_accessed=4 * rows * wide, transcendentals=0
        ),
    )(hi, lo, before, own, after, *([old] if second else []))


def slot_table(columns, counts):
    rows, slots = columns.shape
    total = rows * lax.axis_size("orb")
    spread = GROUP + 2 * rows
    ids = jnp.arange(rows, dtype=jnp.int32)
    offset = lax.axis_index("orb") * rows - rows
    place = (columns - offset) % total - (ids // GROUP * GROUP)[:, None]
    number = jnp.arange(slots, dtype=jnp.int32)
    place = jnp.where(number[None, :] < counts[:, None], place, -1)
    hit = place[:, :, None] == jnp.arange(spread, dtype=jnp.int32)[None, None, :]
    return jnp.max(jnp.where(hit, number[None, :, None], -1), axis=1)


def neighbours(x):
    size = lax.axis_size("orb")
    up = [(i, (i + 1) % size) for i in range(size)]
    down = [(j, i) for i, j in up]
    return lax.ppermute(x, "orb", up), lax.ppermute(x, "orb", down)


def after_that(x, *done):
    return lax.optimization_barrier((x, done))[0]


def prep_kernel(band_ref, *refs):
    ins, (hi_ref, lo_ref, thi_ref, tlo_ref) = refs[:4], refs[4:]
    for place, ref in enumerate(ins):
        band = band_ref[place]
        x = ref[...]
        hi_ref[band], lo_ref[band] = split(x)
        thi_ref[band], tlo_ref[band] = split(x.T)


def prep(bands, parts):
    rows, width = parts[0].shape
    plain = jax.ShapeDtypeStruct((4, rows, width), jnp.bfloat16)
    turned = jax.ShapeDtypeStruct((4, width, rows), jnp.bfloat16)
    return pl.pallas_call(
        prep_kernel,
        in_specs=[pl.BlockSpec(memory_space=pltpu.SMEM)] + [pl.BlockSpec(memory_space=pltpu.VMEM)] * 4,
        out_specs=[pl.BlockSpec(memory_space=pltpu.VMEM)] * 4,
        out_shape=[plain, plain, turned, turned],
        compiler_params=pltpu.CompilerParams(vmem_limit_bytes=16 * MIB),
        cost_estimate=pl.CostEstimate(flops=0, bytes_accessed=32 * rows * width, transcendentals=0),
    )(bands, *parts)


def product_kernel(target_ref, thi_ref, tlo_ref, *refs):
    ins, out_ref = refs[:-1], refs[-1]
    columns = len(ins) // 2
    count, width, rows = thi_ref.shape
    thi = thi_ref[...].reshape(count * width, rows)
    tlo = tlo_ref[...].reshape(count * width, rows)
    his = jnp.concatenate([ref[0] for ref in ins[:columns]], axis=1)
    los = jnp.concatenate([ref[0] for ref in ins[columns:]], axis=1)
    small = jnp.dot(thi, los, preferred_element_type=jnp.float32)
    small += jnp.dot(tlo, his, preferred_element_type=jnp.float32)
    out_ref[0] = small + jnp.dot(thi, his, preferred_element_type=jnp.float32)


def products(targets, chunks, half=None):
    _, _, thi, tlo = chunks[-1]
    four, width, rows = thi.shape
    count = four if half is None else four // 2
    place = half or 0
    size = sum(chunk[0].shape[2] for chunk in chunks)
    left = pl.BlockSpec((count, width, rows), lambda g, t: (place, 0, 0))
    right = [pl.BlockSpec((1, rows, chunk[0].shape[2]), lambda g, t: (t[g], 0, 0)) for chunk in chunks]
    return pl.pallas_call(
        product_kernel,
        grid_spec=pltpu.PrefetchScalarGridSpec(
            num_scalar_prefetch=1,
            grid=(targets.shape[0],),
            in_specs=[left, left] + right + right,
            out_specs=pl.BlockSpec((1, count * width, size), lambda g, t: (g, 0, 0)),
        ),
        out_shape=jax.ShapeDtypeStruct((targets.shape[0], count * width, size), jnp.float32),
        compiler_params=pltpu.CompilerParams(vmem_limit_bytes=24 * MIB),
        cost_estimate=pl.CostEstimate(
            flops=targets.shape[0] * 6 * count * width * rows * size,
            bytes_accessed=8_000_000,
            transcendentals=0,
        ),
    )(targets, thi, tlo, *[c[0] for c in chunks], *[c[1] for c in chunks])


def middle_kernel(got_a, ours_a, got_b, ours_b, send_a, keep_a, send_b, keep_b):
    for got, ours, send_ref, keep in ((got_a, ours_a, send_a, keep_a), (got_b, ours_b, send_b, keep_b)):
        keep[...] = got[0] + ours[0]
        send_ref[...] = got[1] + ours[1]


def middle(*parts):
    shape = jax.ShapeDtypeStruct(parts[0].shape[1:], jnp.float32)
    vmem = pl.BlockSpec(memory_space=pltpu.VMEM)
    return pl.pallas_call(
        middle_kernel,
        in_specs=[vmem] * 4,
        out_specs=[vmem] * 4,
        out_shape=[shape] * 4,
        compiler_params=pltpu.CompilerParams(vmem_limit_bytes=12 * MIB),
        cost_estimate=pl.CostEstimate(flops=0, bytes_accessed=5_000_000, transcendentals=0),
    )(*parts)


def pick_kernel(goal_ref, *refs):
    ins, outs, sums = refs[:-5], refs[-5:-1], refs[-1]
    half = len(ins) // 2
    rows = sums.shape[1]
    for place in range(4):
        keep, got = (ins[0], ins[1]) if half == 1 or place < 2 else (ins[2], ins[3])
        start = (place if half == 1 else place % 2) * rows
        sums[place] = keep[pl.ds(start, rows), :] + got[pl.ds(start, rows), :]
    for k, out in enumerate(outs):
        out[...] = sums[goal_ref[k]]
    outs[3][...] = jnp.where(goal_ref[4] > 0, outs[3][...], 0.0)


def pick(goals, *parts):
    rows, size = parts[0].shape[0] * len(parts) // 8, parts[0].shape[1]
    shape = jax.ShapeDtypeStruct((rows, size), jnp.float32)
    vmem = pl.BlockSpec(memory_space=pltpu.VMEM)
    return pl.pallas_call(
        pick_kernel,
        in_specs=[pl.BlockSpec(memory_space=pltpu.SMEM)] + [vmem] * len(parts),
        out_specs=[vmem] * 4,
        out_shape=[shape] * 4,
        scratch_shapes=[pltpu.VMEM((4, rows, size), jnp.float32)],
        compiler_params=pltpu.CompilerParams(vmem_limit_bytes=12 * MIB),
        cost_estimate=pl.CostEstimate(flops=0, bytes_accessed=3_000_000, transcendentals=0),
    )(goals, *parts)


def assemble_kernel(core_ref, e0_ref, e1_ref, turn_ref, own_ref, other_ref, ta_ref, tb_ref, out_ref, *, scale):
    w = e0_ref.shape[0]
    low = own_ref[...] + other_ref[...]
    turned = (ta_ref[...] + tb_ref[...]).T
    first = jnp.concatenate([e0_ref[...], turn_ref[...].T, turned[:w]], axis=1)
    second = jnp.concatenate([e1_ref[...], turned[w:]], axis=1)
    half = out_ref.shape[1]
    is_first = core_ref[0] == 0
    for k, x in enumerate((first, second, low)):
        out_ref[pl.ds(k * w, w), :] = jnp.where(is_first, x[:, :half], x[:, half:]) * scale


def assemble(core, parts, order):
    w = parts[0].shape[0]
    vmem = pl.BlockSpec(memory_space=pltpu.VMEM)
    return pl.pallas_call(
        functools.partial(assemble_kernel, scale=1.0 / order),
        in_specs=[pl.BlockSpec(memory_space=pltpu.SMEM)] + [vmem] * len(parts),
        out_specs=vmem,
        out_shape=jax.ShapeDtypeStruct((3 * w, 3 * w // 2), jnp.float32),
        compiler_params=pltpu.CompilerParams(vmem_limit_bytes=12 * MIB),
        cost_estimate=pl.CostEstimate(flops=0, bytes_accessed=2_000_000, transcendentals=0),
    )(core[None], *parts)


def linear(chip, core, z):
    return (chip * 2 + core) * 4 + z


def send(x, pairs):
    return lax.ppermute(x, ("orb", "band"), pairs)


def mirrored(pairs):
    out = []
    for chip in range(4):
        for a, b in pairs:
            out.append((linear(chip, 0, a), linear(chip, 0, b)))
            out.append((linear(chip, 1, 3 - a), linear(chip, 1, 3 - b)))
    return out


def gather_bands(x):
    return [x] + [send(x, mirrored([(source, 2)])) for source in (0, 1, 3)]


def over_chips(flip):
    return [
        (linear(chip, core, 2 - core), linear(chip ^ flip, core, 2 - core))
        for chip in range(4)
        for core in range(2)
    ]


EVERY = [(q, c, z) for q in range(4) for c in range(2) for z in range(4)]
SWAP = [(linear(q, c, z), linear(q, 1 - c, z)) for q, c, z in EVERY]
TURN = [(linear(q, c, z), linear(z, c, q)) for q, c, z in EVERY]
TURN_UP = [[(linear(q, c, z), linear(z, 1, q)) for q, c, z in EVERY if c == core] for core in range(2)]


def simple_gram(filtered):
    partial_gram = jnp.dot(
        filtered.T,
        lax.all_gather(filtered, "band", axis=1, tiled=True),
        precision=lax.Precision.HIGH,
        preferred_element_type=jnp.float32,
    )
    return lax.psum_scatter(partial_gram, "orb", scatter_dimension=1, tiled=True)


def in_turn(hi, lo, old, order):
    first, filtered = [], []
    for x in old:
        before, after = neighbours(x)
        first.append(apply_step(hi, lo, before, x, after))
    for x, v in zip(first, old):
        before, after = neighbours(x)
        filtered.append(apply_step(hi, lo, before, x, after, v))
    filtered = jnp.concatenate(filtered, axis=1)
    return filtered, simple_gram(filtered) / order


def by_symmetry(hi, lo, old, order):
    def one(x, halo, v=None):
        return apply_step(hi, lo, halo[0], x, halo[1], v)

    orb, z = lax.axis_index("orb"), lax.axis_index("band")
    chip, core = orb // 2, orb % 2
    bands = jnp.asarray([[2, 0, 1, 3], [1, 3, 2, 0]], jnp.int32)[core]
    holder = (z == 2 - core).astype(jnp.int32)
    goals = jnp.stack([jnp.where(core == 0, k, 3 - k) for k in (0, 1, 3)] + [z, holder]).astype(jnp.int32)
    far_y = jnp.stack([chip ^ 2, chip ^ 3])
    far_x = jnp.stack([chip ^ 1, chip ^ 3])
    near_y = jnp.stack([chip, chip ^ 1])
    near_x = jnp.stack([chip, chip ^ 2])

    def deliver(parts):
        moved = pick(goals, *parts)
        piece = moved[3]
        for k, x in zip((0, 1, 3), moved):
            piece = piece + send(x, mirrored([(2, k)]))
        return piece

    v0, v1, v2 = old
    hv = [neighbours(x) for x in old]
    f0 = one(v0, hv[0])
    hf0 = neighbours(f0)
    f1 = one(v1, hv[1])
    hf1 = neighbours(f1)
    f2 = one(v2, hv[2])
    hf2 = neighbours(f2)
    g0 = one(f0, hf0, v0)
    z0 = gather_bands(g0)
    g1 = one(after_that(f1, g0), hf1, v1)
    z1 = gather_bands(g1)
    chunks = [prep(bands, [after_that(z0[0], g1)] + z0[1:])]
    far0 = products(far_y, chunks)
    got0 = send(far0, over_chips(2))
    g2 = one(after_that(f2, far0), hf2, v2)
    z2 = gather_bands(g2)
    ours0 = products(after_that(near_y, g2), chunks)
    filtered = jnp.concatenate([g0, g1, after_that(g2, ours0)], axis=1)
    chunks.append(prep(bands, [after_that(z1[0], filtered)] + z1[1:]))
    far1 = products(far_y, chunks)
    got1 = send(far1, over_chips(2))
    ours1 = products(after_that(near_y, far1), chunks)
    last0 = send(after_that(got0, ours1)[1] + ours0[1], over_chips(1))
    chunks.append(prep(bands, [after_that(z2[0], ours1)] + z2[1:]))
    far2y = products(far_y, chunks, 0)
    got2y = send(far2y, over_chips(2))
    far2x = products(after_that(far_x, far2y), chunks, 1)
    got2x = send(far2x, over_chips(1))
    last1 = send(after_that(got1, far2x)[1] + ours1[1], over_chips(1))
    ours2y = products(after_that(near_y, far2x), chunks, 0)
    ours2x = products(after_that(near_x, ours2y), chunks, 1)
    send2y, keep2y, send2x, keep2x = middle(got2y, ours2y, got2x, ours2x)
    last2y = send(send2y, over_chips(1))
    last2x = send(send2x, over_chips(2))
    early = deliver(
        [
            jnp.concatenate([got0[0] + ours0[0], got1[0] + ours1[0]], axis=1),
            jnp.concatenate([last0, last1], axis=1),
        ]
    )
    early = early + send(early, SWAP)
    w = v0.shape[1]
    early_turn = send(early[:, w : 2 * w], TURN)
    piece = deliver([keep2y, last2y, keep2x, last2x])
    other = send(piece, SWAP)
    turned = [send(piece[:, : 2 * w], TURN_UP[k]) for k in (0, 1)]
    gram = assemble(
        core, [early[:, :w], early[:, w:], early_turn, piece, other, *turned], order
    )
    return filtered, gram


def body(blocks, columns, counts, vectors, symmetric):
    rows, width = vectors.shape
    order = rows * lax.axis_size("orb")
    slot_of = slot_table(columns, counts)
    hi, lo = densify(slot_of, blocks)
    later = after_that(vectors, slot_of)
    old = [
        (later if c else vectors)[:, c : min(c + LANES, width)] for c in range(0, width, LANES)
    ]
    return (by_symmetry if symmetric else in_turn)(hi, lo, old, order)


def solution(mesh):
    placed = (P("orb", None, None, None), P("orb", None), P("orb"), P("orb", "band"))

    def whole(blocks, columns, counts, vectors):
        symmetric = (
            mesh.shape["orb"] == 8 and mesh.shape["band"] == 4 and vectors.shape[1] == 3 * LANES
        )
        return body(blocks, columns, counts, vectors, symmetric)

    return jax.shard_map(
        whole,
        mesh=mesh,
        in_specs=placed,
        out_specs=(P("orb", "band"), P("band", "orb")),
        check_vma=False,
    )
```

```python
import functools

import jax
import jax.numpy as jnp
from jax import lax
from jax.experimental import pallas as pl
from jax.experimental.pallas import tpu as pltpu
from jax.sharding import PartitionSpec as P

GROUP = 4
LANES = 128
MIB = 1024 * 1024
APPLY_MIB = 14


def split(x):
    hi = x.astype(jnp.bfloat16)
    lo = (x - hi.astype(jnp.float32)).astype(jnp.bfloat16)
    return hi, lo


def densify_kernel(slot_ref, blocks_ref, hi_ref, lo_ref, *, spread, reach):
    blk = blocks_ref.shape[2]
    step = pl.program_id(0)
    tile = (blk, 2 * blk)
    shift = lax.broadcasted_iota(jnp.int32, tile, 1) - lax.broadcasted_iota(jnp.int32, tile, 0)

    def one_row(i, carry):
        row = step * GROUP + i
        start = pl.multiple_of(i * blk, blk)
        for pair in range(spread // 2):
            left = slot_ref[row, 2 * pair]
            right = slot_ref[row, 2 * pair + 1]
            lblk = jnp.where(left >= 0, blocks_ref[i, jnp.maximum(left, 0)], 0.0)
            rblk = jnp.where(right >= 0, blocks_ref[i, jnp.maximum(right, 0)], 0.0)
            both = jnp.concatenate([lblk, rblk], axis=1)
            if reach <= 2 * pair + 1 and 2 * pair < reach + GROUP:
                both = both - jnp.where(shift == (reach + i - 2 * pair) * blk, 0.1, 0.0)
            hi, lo = split(both / 0.9)
            hi_ref[pl.ds(start, blk), pl.ds(pair * 2 * blk, 2 * blk)] = hi
            lo_ref[pl.ds(start, blk), pl.ds(pair * 2 * blk, 2 * blk)] = lo
        return carry

    lax.fori_loop(0, GROUP, one_row, 0)


def densify(slot_of, blocks):
    rows, slots, blk, _ = blocks.shape
    spread = slot_of.shape[1]
    shape = pltpu.VMEM((rows * blk, spread * blk), jnp.bfloat16)
    out = pl.BlockSpec((GROUP * blk, spread * blk), lambda g, _: (g, 0))
    return pl.pallas_call(
        functools.partial(densify_kernel, spread=spread, reach=rows),
        grid_spec=pltpu.PrefetchScalarGridSpec(
            num_scalar_prefetch=1,
            grid=(rows // GROUP,),
            in_specs=[pl.BlockSpec((GROUP, slots, blk, blk), lambda g, _: (g, 0, 0, 0))],
            out_specs=[out, out],
        ),
        out_shape=[shape, shape],
        compiler_params=pltpu.CompilerParams(vmem_limit_bytes=20 * MIB),
        cost_estimate=pl.CostEstimate(flops=0, bytes_accessed=60_000_000, transcendentals=0),
    )(slot_of, blocks)


def apply_kernel(hi_ref, lo_ref, before_ref, own_ref, after_ref, *rest, second):
    old_ref = rest[0] if second else None
    out_ref, parts = rest[-2:]
    rows, width = own_ref.shape
    wide = hi_ref.shape[1]
    tall = wide - 2 * rows
    for place, ref in enumerate((before_ref, own_ref, after_ref)):
        there = pl.ds(place * rows, rows)
        parts[there, pl.ds(0, width)], parts[there, pl.ds(width, width)] = split(ref[...])

    def one_group(step, carry):
        start = pl.multiple_of(step * tall, tall)
        here = pl.ds(start, tall)
        reached = pl.ds(start, wide)
        both = jnp.dot(hi_ref[here, :], parts[reached, :], preferred_element_type=jnp.float32)
        other = jnp.dot(
            lo_ref[here, :], parts[reached, pl.ds(0, width)], preferred_element_type=jnp.float32
        )
        product = both[:, :width] + (both[:, width:] + other)
        if second:
            product = 2.0 * product - old_ref[here, :]
        out_ref[here, :] = product
        return carry

    lax.fori_loop(0, rows // tall, one_group, 0)


def apply_step(hi, lo, before, own, after, old=None):
    rows, width = own.shape
    wide = hi.shape[1]
    second = old is not None
    hi, lo = (pltpu.with_memory_space_constraint(x, pltpu.VMEM) for x in (hi, lo))
    vmem = pl.BlockSpec(memory_space=pltpu.VMEM)
    return pl.pallas_call(
        functools.partial(apply_kernel, second=second),
        in_specs=[vmem] * (6 if second else 5),
        out_specs=vmem,
        out_shape=jax.ShapeDtypeStruct((rows, width), jnp.float32),
        scratch_shapes=[pltpu.VMEM((3 * rows, 2 * width), jnp.bfloat16)],
        compiler_params=pltpu.CompilerParams(vmem_limit_bytes=APPLY_MIB * MIB),
        cost_estimate=pl.CostEstimate(
            flops=8 * rows * wide * width, bytes_accessed=4 * rows * wide, transcendentals=0
        ),
    )(hi, lo, before, own, after, *([old] if second else []))


def slot_table(columns, counts):
    rows, slots = columns.shape
    total = rows * lax.axis_size("orb")
    spread = GROUP + 2 * rows
    ids = jnp.arange(rows, dtype=jnp.int32)
    offset = lax.axis_index("orb") * rows - rows
    place = (columns - offset) % total - (ids // GROUP * GROUP)[:, None]
    number = jnp.arange(slots, dtype=jnp.int32)
    place = jnp.where(number[None, :] < counts[:, None], place, -1)
    hit = place[:, :, None] == jnp.arange(spread, dtype=jnp.int32)[None, None, :]
    return jnp.max(jnp.where(hit, number[None, :, None], -1), axis=1)


def neighbours(x):
    size = lax.axis_size("orb")
    up = [(i, (i + 1) % size) for i in range(size)]
    down = [(j, i) for i, j in up]
    return lax.ppermute(x, "orb", up), lax.ppermute(x, "orb", down)


def after_that(x, *done):
    return lax.optimization_barrier((x, done))[0]


def prep_kernel(band_ref, *refs):
    ins, (hi_ref, lo_ref, thi_ref, tlo_ref) = refs[:4], refs[4:]
    for place, ref in enumerate(ins):
        band = band_ref[place]
        x = ref[...]
        hi_ref[band], lo_ref[band] = split(x)
        thi_ref[band], tlo_ref[band] = split(x.T)


def prep(bands, parts):
    rows, width = parts[0].shape
    plain = jax.ShapeDtypeStruct((4, rows, width), jnp.bfloat16)
    turned = jax.ShapeDtypeStruct((4, width, rows), jnp.bfloat16)
    return pl.pallas_call(
        prep_kernel,
        in_specs=[pl.BlockSpec(memory_space=pltpu.SMEM)] + [pl.BlockSpec(memory_space=pltpu.VMEM)] * 4,
        out_specs=[pl.BlockSpec(memory_space=pltpu.VMEM)] * 4,
        out_shape=[plain, plain, turned, turned],
        compiler_params=pltpu.CompilerParams(vmem_limit_bytes=16 * MIB),
        cost_estimate=pl.CostEstimate(flops=0, bytes_accessed=32 * rows * width, transcendentals=0),
    )(bands, *parts)


def product_kernel(target_ref, *refs, shapes):
    *ins, out_a, out_b = refs
    step = pl.program_id(0)
    parts = []
    for columns in shapes:
        left, ins = ins[:2], ins[2:]
        right, ins = ins[: 2 * columns], ins[2 * columns :]
        count, width, rows = left[0].shape
        thi, tlo = (ref[...].reshape(count * width, rows) for ref in left)
        his = jnp.concatenate([ref[0] for ref in right[:columns]], axis=1)
        los = jnp.concatenate([ref[0] for ref in right[columns:]], axis=1)
        small = jnp.dot(thi, los, preferred_element_type=jnp.float32)
        small += jnp.dot(tlo, his, preferred_element_type=jnp.float32)
        parts.append(small + jnp.dot(thi, his, preferred_element_type=jnp.float32))
    total = jnp.concatenate(parts, axis=1)

    @pl.when(step < 2)
    def _():
        out_a[0] = total

    @pl.when(step >= 2)
    def _():
        out_b[0] = total


def products(targets, chunks, lines):
    ins, specs, shapes, size, flops = [], [], [], 0, 0
    for line in lines:
        _, _, thi, tlo = chunks[line]
        four, width, rows = thi.shape
        ins += [thi, tlo]
        specs += [pl.BlockSpec((four // 2, width, rows), lambda g, t: (g // 2, 0, 0))] * 2
        for part in (0, 1):
            for c in range(line + 1):
                x = chunks[c][part]
                ins.append(x)
                specs.append(pl.BlockSpec((1, rows, x.shape[2]), lambda g, t: (t[g], 0, 0)))
        wide = sum(chunks[c][0].shape[2] for c in range(line + 1))
        shapes.append(line + 1)
        size += wide
        flops += 12 * four * width * rows * wide
    tall = four // 2 * width
    shape = jax.ShapeDtypeStruct((2, tall, size), jnp.float32)
    return pl.pallas_call(
        functools.partial(product_kernel, shapes=shapes),
        grid_spec=pltpu.PrefetchScalarGridSpec(
            num_scalar_prefetch=1,
            grid=(4,),
            in_specs=specs,
            out_specs=[
                pl.BlockSpec((1, tall, size), lambda g, t: (jnp.minimum(g, 1), 0, 0)),
                pl.BlockSpec((1, tall, size), lambda g, t: (jnp.maximum(g - 2, 0), 0, 0)),
            ],
        ),
        out_shape=[shape, shape],
        compiler_params=pltpu.CompilerParams(vmem_limit_bytes=24 * MIB),
        cost_estimate=pl.CostEstimate(flops=flops, bytes_accessed=8_000_000, transcendentals=0),
    )(targets, *ins)


def middle_kernel(got_a, ours_a, got_b, ours_b, send_a, keep_a, send_b, keep_b):
    for got, ours, send_ref, keep in ((got_a, ours_a, send_a, keep_a), (got_b, ours_b, send_b, keep_b)):
        keep[...] = got[0] + ours[0]
        send_ref[...] = got[1] + ours[1]


def middle(*parts):
    shape = jax.ShapeDtypeStruct(parts[0].shape[1:], jnp.float32)
    vmem = pl.BlockSpec(memory_space=pltpu.VMEM)
    return pl.pallas_call(
        middle_kernel,
        in_specs=[vmem] * 4,
        out_specs=[vmem] * 4,
        out_shape=[shape] * 4,
        compiler_params=pltpu.CompilerParams(vmem_limit_bytes=12 * MIB),
        cost_estimate=pl.CostEstimate(flops=0, bytes_accessed=5_000_000, transcendentals=0),
    )(*parts)


def pick_kernel(goal_ref, *refs):
    ins, outs, sums = refs[:8], refs[8:12], refs[12]
    rows = sums.shape[1] // 2
    for batch in range(2):
        for band in range(4):
            keep, got = ins[4 * batch + band // 2 * 2 : 4 * batch + band // 2 * 2 + 2]
            there = pl.ds(band % 2 * rows, rows)
            sums[band, pl.ds(batch * rows, rows), :] = keep[there, :] + got[there, :]
    for k, out in enumerate(outs):
        out[...] = sums[goal_ref[k]]
    outs[3][...] = jnp.where(goal_ref[4] > 0, outs[3][...], 0.0)


def pick(goals, *parts):
    rows, size = parts[0].shape
    shape = jax.ShapeDtypeStruct((rows, size), jnp.float32)
    vmem = pl.BlockSpec(memory_space=pltpu.VMEM)
    return pl.pallas_call(
        pick_kernel,
        in_specs=[pl.BlockSpec(memory_space=pltpu.SMEM)] + [vmem] * len(parts),
        out_specs=[vmem] * 4,
        out_shape=[shape] * 4,
        scratch_shapes=[pltpu.VMEM((4, rows, size), jnp.float32)],
        compiler_params=pltpu.CompilerParams(vmem_limit_bytes=12 * MIB),
        cost_estimate=pl.CostEstimate(flops=0, bytes_accessed=3_000_000, transcendentals=0),
    )(goals, *parts)


def assemble_kernel(core_ref, piece_ref, turn_e_ref, turn_l_ref, out_ref, *, scale):
    w = turn_e_ref.shape[0]
    early, last = piece_ref[:w, :], piece_ref[w:, :]
    turned = turn_l_ref[...].T
    first = jnp.concatenate([early[:, :w], turn_e_ref[...].T, turned[:w]], axis=1)
    second = jnp.concatenate([early[:, w:], turned[w:]], axis=1)
    half = out_ref.shape[1]
    is_first = core_ref[0] == 0
    for k, x in enumerate((first, second, last)):
        out_ref[pl.ds(k * w, w), :] = jnp.where(is_first, x[:, :half], x[:, half:]) * scale


def assemble(core, parts, order):
    w = parts[0].shape[0] // 2
    vmem = pl.BlockSpec(memory_space=pltpu.VMEM)
    return pl.pallas_call(
        functools.partial(assemble_kernel, scale=1.0 / order),
        in_specs=[pl.BlockSpec(memory_space=pltpu.SMEM)] + [vmem] * len(parts),
        out_specs=vmem,
        out_shape=jax.ShapeDtypeStruct((3 * w, 3 * w // 2), jnp.float32),
        compiler_params=pltpu.CompilerParams(vmem_limit_bytes=12 * MIB),
        cost_estimate=pl.CostEstimate(flops=0, bytes_accessed=2_000_000, transcendentals=0),
    )(core, *parts)


def linear(chip, core, z):
    return (chip * 2 + core) * 4 + z


def send(x, pairs):
    return lax.ppermute(x, ("orb", "band"), pairs)


def mirrored(pairs):
    out = []
    for chip in range(4):
        for a, b in pairs:
            out.append((linear(chip, 0, a), linear(chip, 0, b)))
            out.append((linear(chip, 1, 3 - a), linear(chip, 1, 3 - b)))
    return out


def gather_bands(x):
    return [x] + [send(x, mirrored([(source, 2)])) for source in (0, 1, 3)]


def over_chips(flip):
    return [
        (linear(chip, core, 2 - core), linear(chip ^ flip, core, 2 - core))
        for chip in range(4)
        for core in range(2)
    ]


EVERY = [(q, c, z) for q in range(4) for c in range(2) for z in range(4)]
SWAP = [(linear(q, c, z), linear(q, 1 - c, z)) for q, c, z in EVERY]
TURN = [(linear(q, c, z), linear(z, c, q)) for q, c, z in EVERY]
TURN_UP = [pair for pair in TURN if pair[0] // 4 % 2 == 1]


def simple_gram(filtered):
    partial_gram = jnp.dot(
        filtered.T,
        lax.all_gather(filtered, "band", axis=1, tiled=True),
        precision=lax.Precision.HIGH,
        preferred_element_type=jnp.float32,
    )
    return lax.psum_scatter(partial_gram, "orb", scatter_dimension=1, tiled=True)


def in_turn(hi, lo, old, order):
    first, filtered = [], []
    for x in old:
        before, after = neighbours(x)
        first.append(apply_step(hi, lo, before, x, after))
    for x, v in zip(first, old):
        before, after = neighbours(x)
        filtered.append(apply_step(hi, lo, before, x, after, v))
    filtered = jnp.concatenate(filtered, axis=1)
    return filtered, simple_gram(filtered) / order


def index_tables():
    orb, z = lax.axis_index("orb"), lax.axis_index("band")
    chip, core = orb >> 1, orb & 1
    bands = jnp.stack([b + core * (3 - 2 * b) for b in (2, 0, 1, 3)])
    holder = (z == 2 - core).astype(jnp.int32)
    goals = jnp.stack([k + core * (3 - 2 * k) for k in (0, 1, 3)] + [z, holder])
    far = jnp.stack([chip ^ 2, chip ^ 3, chip ^ 1, chip ^ 3])
    near = jnp.stack([chip, chip ^ 1, chip, chip ^ 2])
    return bands, goals, far, near, core[None]


def by_symmetry(hi, lo, old, order, tables):
    def one(x, halo, v=None):
        return apply_step(hi, lo, halo[0], x, halo[1], v)

    bands, goals, far, near, core = tables

    def across(parts, order):
        return [send(x, over_chips(flip)) for x, flip in zip(parts, order)]

    v0, v1, v2 = old
    hv = [neighbours(x) for x in old]
    f0 = one(v0, hv[0])
    hf0 = neighbours(f0)
    f1 = one(v1, hv[1])
    hf1 = neighbours(f1)
    f2 = one(v2, hv[2])
    hf2 = neighbours(f2)
    g0 = one(f0, hf0, v0)
    z0 = gather_bands(g0)
    g1 = one(after_that(f1, g0), hf1, v1)
    z1 = gather_bands(g1)
    chunks = [prep(bands, [after_that(z0[0], g1)] + z0[1:])]
    g2 = one(after_that(f2, chunks[0][0]), hf2, v2)
    z2 = gather_bands(g2)
    chunks.append(prep(bands, [after_that(z1[0], g2)] + z1[1:]))
    theirs_e = products(far, chunks, (0, 1))
    got_e = across(theirs_e, (2, 1))
    ours_e = products(after_that(near, theirs_e[0]), chunks, (0, 1))
    chunks.append(prep(bands, [after_that(z2[0], ours_e[0])] + z2[1:]))
    theirs_l = products(far, chunks, (2,))
    got_l = across(theirs_l, (2, 1))
    got_e[0] = after_that(got_e[0], theirs_l[0])
    send_ey, keep_ey, send_ex, keep_ex = middle(got_e[0], ours_e[0], got_e[1], ours_e[1])
    last_e = across((send_ey, send_ex), (1, 2))
    ours_l = products(after_that(near, keep_ey), chunks, (2,))
    send_ly, keep_ly, send_lx, keep_lx = middle(got_l[0], ours_l[0], got_l[1], ours_l[1])
    last_l = across((send_ly, send_lx), (1, 2))
    filtered = jnp.concatenate([g0, g1, after_that(g2, keep_ly)], axis=1)
    moved = pick(goals, keep_ey, last_e[0], keep_ex, last_e[1], keep_ly, last_l[0], keep_lx, last_l[1])
    piece = moved[3]
    for k, x in zip((0, 1, 3), moved):
        piece = piece + send(x, mirrored([(2, k)]))
    piece = piece + send(piece, SWAP)
    w = v0.shape[1]
    turn_e = send(piece[:w, w : 2 * w], TURN)
    turn_l = send(piece[w:, : 2 * w], TURN_UP)
    return filtered, assemble(core, [piece, turn_e, turn_l], order)


def body(blocks, columns, counts, vectors, symmetric):
    rows, width = vectors.shape
    order = rows * lax.axis_size("orb")
    slot_of = slot_table(columns, counts)
    later = vectors
    if symmetric:
        tables = index_tables()
        slot_of, tables, later = lax.optimization_barrier((slot_of, tables, vectors))
    old = [
        (later if c else vectors)[:, c : min(c + LANES, width)] for c in range(0, width, LANES)
    ]
    hi, lo = densify(slot_of, blocks)
    if symmetric:
        return by_symmetry(hi, lo, old, order, tables)
    return in_turn(hi, lo, old, order)


def solution(mesh):
    placed = (P("orb", None, None, None), P("orb", None), P("orb"), P("orb", "band"))

    def whole(blocks, columns, counts, vectors):
        symmetric = (
            mesh.shape["orb"] == 8 and mesh.shape["band"] == 4 and vectors.shape[1] == 3 * LANES
        )
        return body(blocks, columns, counts, vectors, symmetric)

    return jax.shard_map(
        whole,
        mesh=mesh,
        in_specs=placed,
        out_specs=(P("orb", "band"), P("band", "orb")),
        check_vma=False,
    )
```

```python
import functools

import jax
import jax.numpy as jnp
from jax import lax
from jax.experimental import pallas as pl
from jax.experimental.pallas import tpu as pltpu
from jax.sharding import PartitionSpec as P

GROUP = 4
LANES = 128
MIB = 1024 * 1024
APPLY_MIB = 14


def split(x):
    hi = x.astype(jnp.bfloat16)
    lo = (x - hi.astype(jnp.float32)).astype(jnp.bfloat16)
    return hi, lo


def densify_kernel(slot_ref, blocks_ref, hi_ref, lo_ref, *, spread, reach):
    blk = blocks_ref.shape[2]
    step = pl.program_id(0)
    tile = (blk, 2 * blk)
    shift = lax.broadcasted_iota(jnp.int32, tile, 1) - lax.broadcasted_iota(jnp.int32, tile, 0)

    def one_row(i, carry):
        row = step * GROUP + i
        start = pl.multiple_of(i * blk, blk)
        for pair in range(spread // 2):
            left = slot_ref[row, 2 * pair]
            right = slot_ref[row, 2 * pair + 1]
            lblk = jnp.where(left >= 0, blocks_ref[i, jnp.maximum(left, 0)], 0.0)
            rblk = jnp.where(right >= 0, blocks_ref[i, jnp.maximum(right, 0)], 0.0)
            both = jnp.concatenate([lblk, rblk], axis=1)
            if reach <= 2 * pair + 1 and 2 * pair < reach + GROUP:
                both = both - jnp.where(shift == (reach + i - 2 * pair) * blk, 0.1, 0.0)
            hi, lo = split(both / 0.9)
            hi_ref[pl.ds(start, blk), pl.ds(pair * 2 * blk, 2 * blk)] = hi
            lo_ref[pl.ds(start, blk), pl.ds(pair * 2 * blk, 2 * blk)] = lo
        return carry

    lax.fori_loop(0, GROUP, one_row, 0)


def densify(slot_of, blocks):
    rows, slots, blk, _ = blocks.shape
    spread = slot_of.shape[1]
    shape = pltpu.VMEM((rows * blk, spread * blk), jnp.bfloat16)
    out = pl.BlockSpec((GROUP * blk, spread * blk), lambda g, _: (g, 0))
    return pl.pallas_call(
        functools.partial(densify_kernel, spread=spread, reach=rows),
        grid_spec=pltpu.PrefetchScalarGridSpec(
            num_scalar_prefetch=1,
            grid=(rows // GROUP,),
            in_specs=[pl.BlockSpec((GROUP, slots, blk, blk), lambda g, _: (g, 0, 0, 0))],
            out_specs=[out, out],
        ),
        out_shape=[shape, shape],
        compiler_params=pltpu.CompilerParams(vmem_limit_bytes=20 * MIB),
        cost_estimate=pl.CostEstimate(flops=0, bytes_accessed=60_000_000, transcendentals=0),
    )(slot_of, blocks)


def apply_kernel(core_ref, hi_ref, lo_ref, near_ref, far_ref, own_ref, *rest, second, turned):
    inside_ref, across_ref = (far_ref, near_ref) if turned else (near_ref, far_ref)
    old_ref = rest[0] if second else None
    out_ref, parts = rest[-2:]
    rows, width = own_ref.shape
    wide = hi_ref.shape[1]
    tall = wide - 2 * rows
    core = core_ref[0]
    for place, ref in ((1, own_ref), (2 - 2 * core, inside_ref), (2 * core, across_ref)):
        there = pl.ds(pl.multiple_of(place * rows, rows), rows)
        parts[there, pl.ds(0, width)], parts[there, pl.ds(width, width)] = split(ref[...])

    def one_group(step, carry):
        start = pl.multiple_of(step * tall, tall)
        here = pl.ds(start, tall)
        reached = pl.ds(start, wide)
        both = jnp.dot(hi_ref[here, :], parts[reached, :], preferred_element_type=jnp.float32)
        other = jnp.dot(
            lo_ref[here, :], parts[reached, pl.ds(0, width)], preferred_element_type=jnp.float32
        )
        product = both[:, :width] + (both[:, width:] + other)
        if second:
            product = 2.0 * product - old_ref[here, :]
        out_ref[here, :] = product
        return carry

    lax.fori_loop(0, rows // tall, one_group, 0)


def apply_step(core, hi, lo, halo, own, old=None, turned=False):
    rows, width = own.shape
    wide = hi.shape[1]
    second = old is not None
    hi, lo = (pltpu.with_memory_space_constraint(x, pltpu.VMEM) for x in (hi, lo))
    vmem = pl.BlockSpec(memory_space=pltpu.VMEM)
    return pl.pallas_call(
        functools.partial(apply_kernel, second=second, turned=turned),
        in_specs=[pl.BlockSpec(memory_space=pltpu.SMEM)] + [vmem] * (6 if second else 5),
        out_specs=vmem,
        out_shape=jax.ShapeDtypeStruct((rows, width), jnp.float32),
        scratch_shapes=[pltpu.VMEM((3 * rows, 2 * width), jnp.bfloat16)],
        compiler_params=pltpu.CompilerParams(vmem_limit_bytes=APPLY_MIB * MIB),
        cost_estimate=pl.CostEstimate(
            flops=8 * rows * wide * width, bytes_accessed=4 * rows * wide, transcendentals=0
        ),
    )(core, hi, lo, *(halo[::-1] if turned else halo), own, *([old] if second else []))


def slot_table(columns, counts):
    rows, slots = columns.shape
    total = rows * lax.axis_size("orb")
    spread = GROUP + 2 * rows
    ids = jnp.arange(rows, dtype=jnp.int32)
    offset = lax.axis_index("orb") * rows - rows
    place = (columns - offset) % total - (ids // GROUP * GROUP)[:, None]
    number = jnp.arange(slots, dtype=jnp.int32)
    place = jnp.where(number[None, :] < counts[:, None], place, -1)
    hit = place[:, :, None] == jnp.arange(spread, dtype=jnp.int32)[None, None, :]
    return jnp.max(jnp.where(hit, number[None, :, None], -1), axis=1)


def neighbours(x):
    size = lax.axis_size("orb")
    inside = [(i, i ^ 1) for i in range(size)]
    across = [(i, (i + 1 if i % 2 else i - 1) % size) for i in range(size)]
    return lax.ppermute(x, "orb", inside), lax.ppermute(x, "orb", across)


def after_that(x, *done):
    return lax.optimization_barrier((x, done))[0]


def prep_kernel(band_ref, *refs):
    ins, (hi_ref, lo_ref, thi_ref, tlo_ref) = refs[:4], refs[4:]
    for place, ref in enumerate(ins):
        band = band_ref[place]
        x = ref[...]
        hi_ref[band], lo_ref[band] = split(x)
        thi_ref[band], tlo_ref[band] = split(x.T)


def prep(bands, parts):
    rows, width = parts[0].shape
    plain = pltpu.VMEM((4, rows, width), jnp.bfloat16)
    turned = pltpu.VMEM((4, width, rows), jnp.bfloat16)
    return pl.pallas_call(
        prep_kernel,
        in_specs=[pl.BlockSpec(memory_space=pltpu.SMEM)] + [pl.BlockSpec(memory_space=pltpu.VMEM)] * 4,
        out_specs=[pl.BlockSpec(memory_space=pltpu.VMEM)] * 4,
        out_shape=[plain, plain, turned, turned],
        compiler_params=pltpu.CompilerParams(vmem_limit_bytes=16 * MIB),
        cost_estimate=pl.CostEstimate(flops=0, bytes_accessed=32 * rows * width, transcendentals=0),
    )(bands, *parts)


def product_kernel(target_ref, *refs, shapes, place):
    *ins, out_ref = refs
    target = target_ref[place]
    start = 0
    for columns in shapes:
        left, ins = ins[:2], ins[2:]
        right, ins = ins[: 2 * columns], ins[2 * columns :]
        count, width, rows = left[0].shape
        thi, tlo = (ref[...].reshape(count * width, rows) for ref in left)
        his = jnp.concatenate([ref[target] for ref in right[:columns]], axis=1)
        los = jnp.concatenate([ref[target] for ref in right[columns:]], axis=1)
        total = jnp.dot(thi, los, preferred_element_type=jnp.float32)
        total += jnp.dot(tlo, his, preferred_element_type=jnp.float32)
        total += jnp.dot(thi, his, preferred_element_type=jnp.float32)
        out_ref[:, pl.ds(start, his.shape[1])] = total
        start += his.shape[1]


def products(targets, place, chunks, lines):
    ins, shapes, size, flops = [], [], 0, 0
    for line in lines:
        _, _, thi, tlo = chunks[line]
        four, width, rows = thi.shape
        ins += [thi, tlo]
        for part in (0, 1):
            ins += [chunks[c][part] for c in range(line + 1)]
        wide = sum(chunks[c][0].shape[2] for c in range(line + 1))
        shapes.append(line + 1)
        size += wide
        flops += 6 * four * width * rows * wide
    ins = [pltpu.with_memory_space_constraint(x, pltpu.VMEM) for x in ins]
    vmem = pl.BlockSpec(memory_space=pltpu.VMEM)
    return pl.pallas_call(
        functools.partial(product_kernel, shapes=shapes, place=place),
        in_specs=[pl.BlockSpec(memory_space=pltpu.SMEM)] + [vmem] * len(ins),
        out_specs=vmem,
        out_shape=jax.ShapeDtypeStruct((four * width, size), jnp.float32),
        compiler_params=pltpu.CompilerParams(vmem_limit_bytes=16 * MIB),
        cost_estimate=pl.CostEstimate(flops=flops, bytes_accessed=8_000_000, transcendentals=0),
    )(targets, *ins)


def sum_kernel(*refs):
    *ins, out_ref = refs
    out_ref[...] = (ins[0][...] + ins[1][...]) + (ins[2][...] + ins[3][...])


def sum_parts(*parts):
    vmem = pl.BlockSpec(memory_space=pltpu.VMEM)
    return pl.pallas_call(
        sum_kernel,
        in_specs=[vmem] * 4,
        out_specs=vmem,
        out_shape=jax.ShapeDtypeStruct(parts[0].shape, jnp.float32),
        compiler_params=pltpu.CompilerParams(vmem_limit_bytes=12 * MIB),
        cost_estimate=pl.CostEstimate(flops=0, bytes_accessed=4_000_000, transcendentals=0),
    )(*parts)


def pick_kernel(goal_ref, early_ref, *refs):
    ins, outs = refs[:4], refs[4:]
    rows = early_ref.shape[0] // 4
    for k, out in enumerate(outs):
        there = pl.ds(pl.multiple_of(goal_ref[k] * rows, rows), rows)
        x, y, u, v = (ref[there, :] for ref in ins)
        late = (x + y) + (u + v)
        early = early_ref[there, :]
        if k == 3:
            early, late = (jnp.where(goal_ref[4] > 0, x, 0.0) for x in (early, late))
        out[pl.ds(0, rows), :] = early
        out[pl.ds(rows, rows), :] = late


def pick(goals, early, *parts):
    rows, size = parts[0].shape
    shape = jax.ShapeDtypeStruct((rows // 2, size), jnp.float32)
    vmem = pl.BlockSpec(memory_space=pltpu.VMEM)
    return pl.pallas_call(
        pick_kernel,
        in_specs=[pl.BlockSpec(memory_space=pltpu.SMEM)] + [vmem] * 5,
        out_specs=[vmem] * 4,
        out_shape=[shape] * 4,
        compiler_params=pltpu.CompilerParams(vmem_limit_bytes=12 * MIB),
        cost_estimate=pl.CostEstimate(flops=0, bytes_accessed=3_000_000, transcendentals=0),
    )(goals, early, *parts)


def assemble_kernel(core_ref, piece_ref, turn_e_ref, turn_l_ref, out_ref, *, scale):
    w = turn_e_ref.shape[0]
    early, last = piece_ref[:w, :], piece_ref[w:, :]
    turned = turn_l_ref[...].T
    first = jnp.concatenate([early[:, :w], turn_e_ref[...].T, turned[:w]], axis=1)
    second = jnp.concatenate([early[:, w:], turned[w:]], axis=1)
    half = out_ref.shape[1]
    is_first = core_ref[0] == 0
    for k, x in enumerate((first, second, last)):
        out_ref[pl.ds(k * w, w), :] = jnp.where(is_first, x[:, :half], x[:, half:]) * scale


def assemble(core, parts, order):
    w = parts[0].shape[0] // 2
    vmem = pl.BlockSpec(memory_space=pltpu.VMEM)
    return pl.pallas_call(
        functools.partial(assemble_kernel, scale=1.0 / order),
        in_specs=[pl.BlockSpec(memory_space=pltpu.SMEM)] + [vmem] * len(parts),
        out_specs=vmem,
        out_shape=jax.ShapeDtypeStruct((3 * w, 3 * w // 2), jnp.float32),
        compiler_params=pltpu.CompilerParams(vmem_limit_bytes=12 * MIB),
        cost_estimate=pl.CostEstimate(flops=0, bytes_accessed=2_000_000, transcendentals=0),
    )(core, *parts)


def linear(chip, core, z):
    return (chip * 2 + core) * 4 + z


def send(x, pairs):
    return lax.ppermute(x, ("orb", "band"), pairs)


def mirrored(pairs):
    out = []
    for chip in range(4):
        for a, b in pairs:
            out.append((linear(chip, 0, a), linear(chip, 0, b)))
            out.append((linear(chip, 1, 3 - a), linear(chip, 1, 3 - b)))
    return out


def gather_bands(x):
    return [x] + [send(x, mirrored([(source, 2)])) for source in (0, 1, 3)]


def over_chips(flip):
    return [
        (linear(chip, core, 2 - core), linear(chip ^ flip, core, 2 - core))
        for chip in range(4)
        for core in range(2)
    ]


FLIPS = (3, 1, 2, 0)
EVERY = [(q, c, z) for q in range(4) for c in range(2) for z in range(4)]
SWAP = [(linear(q, c, z), linear(q, 1 - c, z)) for q, c, z in EVERY]
TURN = [(linear(q, c, z), linear(z, c, q)) for q, c, z in EVERY]
TURN_UP = [pair for pair in TURN if pair[0] // 4 % 2 == 1]


def simple_gram(filtered):
    partial_gram = jnp.dot(
        filtered.T,
        lax.all_gather(filtered, "band", axis=1, tiled=True),
        precision=lax.Precision.HIGH,
        preferred_element_type=jnp.float32,
    )
    return lax.psum_scatter(partial_gram, "orb", scatter_dimension=1, tiled=True)


def in_turn(hi, lo, old, order):
    core = (lax.axis_index("orb") & 1)[None]
    first = [apply_step(core, hi, lo, neighbours(x), x) for x in old]
    filtered = [apply_step(core, hi, lo, neighbours(x), x, v) for x, v in zip(first, old)]
    filtered = jnp.concatenate(filtered, axis=1)
    return filtered, simple_gram(filtered) / order


def index_tables():
    orb, z = lax.axis_index("orb"), lax.axis_index("band")
    chip, core = orb >> 1, orb & 1
    bands = jnp.stack([b + core * (3 - 2 * b) for b in (2, 0, 1, 3)])
    holder = (z == 2 - core).astype(jnp.int32)
    goals = jnp.stack([k + core * (3 - 2 * k) for k in (0, 1, 3)] + [z, holder])
    targets = jnp.stack([chip ^ flip for flip in FLIPS])
    return bands, goals, targets, core[None]


def by_symmetry(hi, lo, old, order, tables):
    bands, goals, targets, core = tables

    def one(x, halo, v=None, turned=False):
        return apply_step(core, hi, lo, halo, x, v, turned)

    def over_all_chips(chunks, lines, first_after):
        parts, before = [], first_after
        for k, flip in enumerate(FLIPS):
            parts.append(products(after_that(targets, before), k, chunks, lines))
            before = parts[-1]
        return [send(x, over_chips(flip)) if flip else x for x, flip in zip(parts, FLIPS)], before

    v0, v1, v2 = old
    hv = [neighbours(x) for x in old]
    f0 = one(v0, hv[0])
    hf0 = neighbours(f0)
    f1 = one(v1, hv[1])
    hf1 = neighbours(f1)
    f2 = one(v2, hv[2])
    hf2 = neighbours(f2)
    g0 = one(f0, hf0, v0)
    z0 = gather_bands(g0)
    g1 = one(after_that(f1, g0), hf1, v1)
    z1 = gather_bands(g1)
    chunks = [prep(bands, [after_that(z0[0], g1)] + z0[1:])]
    g2 = one(after_that(f2, chunks[0][0]), hf2, v2, turned=True)
    z2 = gather_bands(g2)
    chunks.append(prep(bands, [after_that(z1[0], g2)] + z1[1:]))
    early, last = over_all_chips(chunks, (0, 1), g2)
    chunks.append(prep(bands, [after_that(z2[0], last)] + z2[1:]))
    late, last = over_all_chips(chunks, (2,), chunks[2][0])
    early[3] = after_that(early[3], last)
    moved = pick(goals, sum_parts(*early), *late)
    piece = moved[3]
    for k, x in zip((0, 1, 3), moved):
        piece = piece + send(x, mirrored([(2, k)]))
    filtered = jnp.concatenate([g0, g1, after_that(g2, last)], axis=1)
    piece = piece + send(piece, SWAP)
    w = v0.shape[1]
    turn_e = send(piece[:w, w : 2 * w], TURN)
    turn_l = send(piece[w:, : 2 * w], TURN_UP)
    return filtered, assemble(core, [piece, turn_e, turn_l], order)


def body(blocks, columns, counts, vectors, symmetric):
    rows, width = vectors.shape
    order = rows * lax.axis_size("orb")
    slot_of = slot_table(columns, counts)
    later = vectors
    if symmetric:
        tables = index_tables()
        slot_of, tables, later = lax.optimization_barrier((slot_of, tables, vectors))
    old = [
        (later if c else vectors)[:, c : min(c + LANES, width)] for c in range(0, width, LANES)
    ]
    hi, lo = densify(slot_of, blocks)
    if symmetric:
        return by_symmetry(hi, lo, old, order, tables)
    return in_turn(hi, lo, old, order)


def solution(mesh):
    placed = (P("orb", None, None, None), P("orb", None), P("orb"), P("orb", "band"))

    def whole(blocks, columns, counts, vectors):
        symmetric = (
            mesh.shape["orb"] == 8 and mesh.shape["band"] == 4 and vectors.shape[1] == 3 * LANES
        )
        return body(blocks, columns, counts, vectors, symmetric)

    return jax.shard_map(
        whole,
        mesh=mesh,
        in_specs=placed,
        out_specs=(P("orb", "band"), P("band", "orb")),
        check_vma=False,
    )
```

```python
import functools

import jax
import jax.numpy as jnp
from jax import lax
from jax.experimental import pallas as pl
from jax.experimental.pallas import tpu as pltpu
from jax.sharding import PartitionSpec as P

GROUP = 4
LANES = 128
MIB = 1024 * 1024
APPLY_MIB = 14


def split(x):
    hi = x.astype(jnp.bfloat16)
    lo = (x - hi.astype(jnp.float32)).astype(jnp.bfloat16)
    return hi, lo


def densify_kernel(slot_ref, blocks_ref, hi_ref, lo_ref, *, spread, reach):
    blk = blocks_ref.shape[2]
    step = pl.program_id(0)
    tile = (blk, 2 * blk)
    shift = lax.broadcasted_iota(jnp.int32, tile, 1) - lax.broadcasted_iota(jnp.int32, tile, 0)

    def one_row(i, carry):
        row = step * GROUP + i
        start = pl.multiple_of(i * blk, blk)
        for pair in range(spread // 2):
            left = slot_ref[row, 2 * pair]
            right = slot_ref[row, 2 * pair + 1]
            lblk = jnp.where(left >= 0, blocks_ref[i, jnp.maximum(left, 0)], 0.0)
            rblk = jnp.where(right >= 0, blocks_ref[i, jnp.maximum(right, 0)], 0.0)
            both = jnp.concatenate([lblk, rblk], axis=1)
            if reach <= 2 * pair + 1 and 2 * pair < reach + GROUP:
                both = both - jnp.where(shift == (reach + i - 2 * pair) * blk, 0.1, 0.0)
            hi, lo = split(both / 0.9)
            hi_ref[pl.ds(start, blk), pl.ds(pair * 2 * blk, 2 * blk)] = hi
            lo_ref[pl.ds(start, blk), pl.ds(pair * 2 * blk, 2 * blk)] = lo
        return carry

    lax.fori_loop(0, GROUP, one_row, 0)


def densify(slot_of, blocks):
    rows, slots, blk, _ = blocks.shape
    spread = slot_of.shape[1]
    shape = pltpu.VMEM((rows * blk, spread * blk), jnp.bfloat16)
    out = pl.BlockSpec((GROUP * blk, spread * blk), lambda g, _: (g, 0))
    return pl.pallas_call(
        functools.partial(densify_kernel, spread=spread, reach=rows),
        grid_spec=pltpu.PrefetchScalarGridSpec(
            num_scalar_prefetch=1,
            grid=(rows // GROUP,),
            in_specs=[pl.BlockSpec((GROUP, slots, blk, blk), lambda g, _: (g, 0, 0, 0))],
            out_specs=[out, out],
        ),
        out_shape=[shape, shape],
        compiler_params=pltpu.CompilerParams(vmem_limit_bytes=20 * MIB),
        cost_estimate=pl.CostEstimate(flops=0, bytes_accessed=60_000_000, transcendentals=0),
    )(slot_of, blocks)


def apply_kernel(core_ref, hi_ref, lo_ref, near_ref, far_ref, own_ref, *rest, second, turned):
    inside_ref, across_ref = (far_ref, near_ref) if turned else (near_ref, far_ref)
    old_ref = rest[0] if second else None
    out_ref, parts = rest[-2:]
    rows, width = own_ref.shape
    wide = hi_ref.shape[1]
    tall = wide - 2 * rows
    core = core_ref[0]
    for place, ref in ((1, own_ref), (2 - 2 * core, inside_ref), (2 * core, across_ref)):
        there = pl.ds(pl.multiple_of(place * rows, rows), rows)
        parts[there, pl.ds(0, width)], parts[there, pl.ds(width, width)] = split(ref[...])

    def one_group(step, carry):
        start = pl.multiple_of(step * tall, tall)
        here = pl.ds(start, tall)
        reached = pl.ds(start, wide)
        both = jnp.dot(hi_ref[here, :], parts[reached, :], preferred_element_type=jnp.float32)
        other = jnp.dot(
            lo_ref[here, :], parts[reached, pl.ds(0, width)], preferred_element_type=jnp.float32
        )
        product = both[:, :width] + (both[:, width:] + other)
        if second:
            product = 2.0 * product - old_ref[here, :]
        out_ref[here, :] = product
        return carry

    lax.fori_loop(0, rows // tall, one_group, 0)


def apply_step(core, hi, lo, halo, own, old=None, turned=False):
    rows, width = own.shape
    wide = hi.shape[1]
    second = old is not None
    hi, lo = (pltpu.with_memory_space_constraint(x, pltpu.VMEM) for x in (hi, lo))
    vmem = pl.BlockSpec(memory_space=pltpu.VMEM)
    return pl.pallas_call(
        functools.partial(apply_kernel, second=second, turned=turned),
        in_specs=[pl.BlockSpec(memory_space=pltpu.SMEM)] + [vmem] * (6 if second else 5),
        out_specs=vmem,
        out_shape=jax.ShapeDtypeStruct((rows, width), jnp.float32),
        scratch_shapes=[pltpu.VMEM((3 * rows, 2 * width), jnp.bfloat16)],
        compiler_params=pltpu.CompilerParams(vmem_limit_bytes=APPLY_MIB * MIB),
        cost_estimate=pl.CostEstimate(
            flops=8 * rows * wide * width, bytes_accessed=4 * rows * wide, transcendentals=0
        ),
    )(core, hi, lo, *(halo[::-1] if turned else halo), own, *([old] if second else []))


def slot_table(columns, counts):
    rows, slots = columns.shape
    total = rows * lax.axis_size("orb")
    spread = GROUP + 2 * rows
    ids = jnp.arange(rows, dtype=jnp.int32)
    offset = lax.axis_index("orb") * rows - rows
    place = (columns - offset) % total - (ids // GROUP * GROUP)[:, None]
    number = jnp.arange(slots, dtype=jnp.int32)
    place = jnp.where(number[None, :] < counts[:, None], place, -1)
    hit = place[:, :, None] == jnp.arange(spread, dtype=jnp.int32)[None, None, :]
    return jnp.max(jnp.where(hit, number[None, :, None], -1), axis=1)


def neighbours(x):
    size = lax.axis_size("orb")
    inside = [(i, i ^ 1) for i in range(size)]
    across = [(i, (i + 1 if i % 2 else i - 1) % size) for i in range(size)]
    return lax.ppermute(x, "orb", inside), lax.ppermute(x, "orb", across)


def after_that(x, *done):
    return lax.optimization_barrier((x, done))[0]


def store_parts(band_ref, ins, outs):
    hi_ref, lo_ref, thi_ref, tlo_ref = outs
    for place, ref in enumerate(ins):
        x = ref[...]
        width = x.shape[1]
        there = pl.ds(pl.multiple_of(band_ref[place] * width, width), width)
        hi_ref[:, there], lo_ref[:, there] = split(x)
        thi_ref[there, :], tlo_ref[there, :] = split(x.T)


def block_row(target, turned, right):
    rows = turned[0][0].shape[0] // 4
    there = pl.ds(pl.multiple_of(target * rows, rows), rows)
    thi = jnp.concatenate([hi[there, :] for hi, lo in turned], axis=0)
    tlo = jnp.concatenate([lo[there, :] for hi, lo in turned], axis=0)
    hi_ref, lo_ref = right
    total = jnp.dot(thi, lo_ref[...], preferred_element_type=jnp.float32)
    total += jnp.dot(tlo, hi_ref[...], preferred_element_type=jnp.float32)
    return total + jnp.dot(thi, hi_ref[...], preferred_element_type=jnp.float32)


def chunk_kernel(band_ref, target_ref, *refs, before, places, upper):
    ins, refs = refs[:4], refs[4:]
    olds, refs = [refs[4 * k : 4 * k + 4] for k in range(before)], refs[4 * before :]
    old_products, refs = (refs[: len(places)], refs[len(places) :]) if upper else ((), refs)
    new, outs = refs[:4], refs[4:]
    store_parts(band_ref, ins, new)
    turned = [x[2:] for x in olds] + [new[2:]]
    for k, place in enumerate(places):
        total = block_row(target_ref[place], turned, new[:2])
        if upper:
            high = old_products[k].shape[0]
            outs[k][pl.ds(0, high), :] = old_products[k][...]
            outs[k][pl.ds(high, total.shape[0]), :] = total
        else:
            outs[k][...] = total


def chunk(bands, targets, parts, olds, places, old_products=()):
    rows, width = parts[0].shape
    plain = pltpu.VMEM((rows, 4 * width), jnp.bfloat16)
    turned = pltpu.VMEM((4 * width, rows), jnp.bfloat16)
    high = width * (len(olds) + 1) + (old_products[0].shape[0] if old_products else 0)
    product = jax.ShapeDtypeStruct((high, 4 * width), jnp.float32)
    olds = [pltpu.with_memory_space_constraint(x, pltpu.VMEM) for old in olds for x in old]
    ins = [*parts, *olds, *old_products]
    vmem, smem = pl.BlockSpec(memory_space=pltpu.VMEM), pl.BlockSpec(memory_space=pltpu.SMEM)
    out = pl.pallas_call(
        functools.partial(
            chunk_kernel, before=len(olds) // 4, places=places, upper=bool(old_products)
        ),
        in_specs=[smem, smem] + [vmem] * len(ins),
        out_specs=[vmem] * (4 + len(places)),
        out_shape=[plain, plain, turned, turned] + [product] * len(places),
        compiler_params=pltpu.CompilerParams(vmem_limit_bytes=18 * MIB),
        cost_estimate=pl.CostEstimate(
            flops=24 * len(places) * high * width * rows, bytes_accessed=8_000_000, transcendentals=0
        ),
    )(bands, targets, *ins)
    return out[:4], list(out[4:])


def product_kernel(target_ref, *refs, place):
    out_ref = refs[-1]
    out_ref[...] = block_row(target_ref[place], [refs[k : k + 2] for k in range(2, len(refs) - 1, 2)], refs[:2])


def product(targets, place, chunks):
    rows, wide = chunks[-1][0].shape
    ins = [*chunks[-1][:2]] + [x for c in chunks for x in c[2:]]
    ins = [pltpu.with_memory_space_constraint(x, pltpu.VMEM) for x in ins]
    high = wide // 4 * len(chunks)
    vmem = pl.BlockSpec(memory_space=pltpu.VMEM)
    return pl.pallas_call(
        functools.partial(product_kernel, place=place),
        in_specs=[pl.BlockSpec(memory_space=pltpu.SMEM)] + [vmem] * len(ins),
        out_specs=vmem,
        out_shape=jax.ShapeDtypeStruct((high, wide), jnp.float32),
        compiler_params=pltpu.CompilerParams(vmem_limit_bytes=16 * MIB),
        cost_estimate=pl.CostEstimate(
            flops=6 * high * wide * rows, bytes_accessed=4_000_000, transcendentals=0
        ),
    )(targets, *ins)


def sum_kernel(*refs):
    *ins, out_ref = refs
    out_ref[...] = (ins[0][...] + ins[1][...]) + (ins[2][...] + ins[3][...])


def sum_parts(*parts):
    vmem = pl.BlockSpec(memory_space=pltpu.VMEM)
    return pl.pallas_call(
        sum_kernel,
        in_specs=[vmem] * 4,
        out_specs=vmem,
        out_shape=jax.ShapeDtypeStruct(parts[0].shape, jnp.float32),
        compiler_params=pltpu.CompilerParams(vmem_limit_bytes=12 * MIB),
        cost_estimate=pl.CostEstimate(flops=0, bytes_accessed=4_000_000, transcendentals=0),
    )(*parts)


def pick_kernel(goal_ref, early_ref, *refs):
    ins, outs = refs[:4], refs[4:]
    rows, width = early_ref.shape[0], early_ref.shape[1] // 4
    for k, out in enumerate(outs):
        there = pl.ds(pl.multiple_of(goal_ref[k] * width, width), width)
        x, y, u, v = (ref[:, there] for ref in ins)
        late = (x + y) + (u + v)
        early = early_ref[:, there]
        if k == 3:
            early, late = (jnp.where(goal_ref[4] > 0, x, 0.0) for x in (early, late))
        out[pl.ds(0, rows), :] = early
        out[pl.ds(rows, rows), :] = late


def pick(goals, early, *late):
    rows, size = early.shape
    shape = jax.ShapeDtypeStruct((2 * rows, size // 4), jnp.float32)
    vmem = pl.BlockSpec(memory_space=pltpu.VMEM)
    return pl.pallas_call(
        pick_kernel,
        in_specs=[pl.BlockSpec(memory_space=pltpu.SMEM)] + [vmem] * 5,
        out_specs=[vmem] * 4,
        out_shape=[shape] * 4,
        compiler_params=pltpu.CompilerParams(vmem_limit_bytes=12 * MIB),
        cost_estimate=pl.CostEstimate(flops=0, bytes_accessed=3_000_000, transcendentals=0),
    )(goals, early, *late)


def assemble_kernel(core_ref, piece_ref, turn_e_ref, turn_l_ref, out_ref, *, scale):
    w = piece_ref.shape[1]
    first = jnp.concatenate([piece_ref[:w, :], turn_e_ref[...].T, turn_l_ref[:w, :].T], axis=0)
    second = jnp.concatenate([piece_ref[w : 3 * w, :], turn_l_ref[w:, :].T], axis=0)
    last = piece_ref[3 * w :, :]
    half = out_ref.shape[0]
    is_first = core_ref[0] == 0
    for k, x in enumerate((first, second, last)):
        out_ref[:, pl.ds(k * w, w)] = jnp.where(is_first, x[:half], x[half:]) * scale


def assemble(core, parts, order):
    w = parts[0].shape[1]
    vmem = pl.BlockSpec(memory_space=pltpu.VMEM)
    return pl.pallas_call(
        functools.partial(assemble_kernel, scale=1.0 / order),
        in_specs=[pl.BlockSpec(memory_space=pltpu.SMEM)] + [vmem] * len(parts),
        out_specs=vmem,
        out_shape=jax.ShapeDtypeStruct((3 * w // 2, 3 * w), jnp.float32),
        compiler_params=pltpu.CompilerParams(vmem_limit_bytes=12 * MIB),
        cost_estimate=pl.CostEstimate(flops=0, bytes_accessed=2_000_000, transcendentals=0),
    )(core, *parts).T


def linear(chip, core, z):
    return (chip * 2 + core) * 4 + z


def send(x, pairs):
    return lax.ppermute(x, ("orb", "band"), pairs)


def mirrored(pairs):
    out = []
    for chip in range(4):
        for a, b in pairs:
            out.append((linear(chip, 0, a), linear(chip, 0, b)))
            out.append((linear(chip, 1, 3 - a), linear(chip, 1, 3 - b)))
    return out


def gather_bands(x):
    return [x] + [send(x, mirrored([(source, 2)])) for source in (0, 1, 3)]


def over_chips(flip):
    return [
        (linear(chip, core, 2 - core), linear(chip ^ flip, core, 2 - core))
        for chip in range(4)
        for core in range(2)
    ]


FLIPS = (3, 1, 2, 0)
ALL = (0, 1, 2, 3)
EVERY = [(q, c, z) for q in range(4) for c in range(2) for z in range(4)]
SWAP = [(linear(q, c, z), linear(q, 1 - c, z)) for q, c, z in EVERY]
TURN = [(linear(q, c, z), linear(z, c, q)) for q, c, z in EVERY]
TURN_UP = [pair for pair in TURN if pair[0] // 4 % 2 == 1]


def simple_gram(filtered):
    partial_gram = jnp.dot(
        filtered.T,
        lax.all_gather(filtered, "band", axis=1, tiled=True),
        precision=lax.Precision.HIGH,
        preferred_element_type=jnp.float32,
    )
    return lax.psum_scatter(partial_gram, "orb", scatter_dimension=1, tiled=True)


def in_turn(hi, lo, old, order):
    core = (lax.axis_index("orb") & 1)[None]
    first = [apply_step(core, hi, lo, neighbours(x), x) for x in old]
    filtered = [apply_step(core, hi, lo, neighbours(x), x, v) for x, v in zip(first, old)]
    filtered = jnp.concatenate(filtered, axis=1)
    return filtered, simple_gram(filtered) / order


def index_tables():
    orb, z = lax.axis_index("orb"), lax.axis_index("band")
    chip, core = orb >> 1, orb & 1
    bands = jnp.stack([b + core * (3 - 2 * b) for b in (2, 0, 1, 3)])
    holder = (z == 2 - core).astype(jnp.int32)
    goals = jnp.stack([k + core * (3 - 2 * k) for k in (0, 1, 3)] + [z, holder])
    targets = jnp.stack([chip ^ flip for flip in FLIPS])
    return bands, goals, targets, core[None]


def by_symmetry(hi, lo, old, order, tables):
    bands, goals, targets, core = tables

    def one(x, halo, v=None, turned=False):
        return apply_step(core, hi, lo, halo, x, v, turned)

    v0, v1, v2 = old
    hv = [neighbours(x) for x in old]
    f0 = one(v0, hv[0])
    hf0 = neighbours(f0)
    f1 = one(v1, hv[1])
    hf1 = neighbours(f1)
    f2 = one(v2, hv[2])
    hf2 = neighbours(f2)
    g0 = one(f0, hf0, v0)
    z0 = gather_bands(g0)
    g1 = one(after_that(f1, g0), hf1, v1)
    z1 = gather_bands(g1)
    c0, upper = chunk(bands, targets, [after_that(z0[0], g1)] + z0[1:], [], ALL)
    g2 = one(after_that(f2, upper[0]), hf2, v2, turned=True)
    z2 = gather_bands(g2)
    c1, early = chunk(bands, targets, [after_that(z1[0], g2)] + z1[1:], [c0], ALL, upper)
    early = [send(x, over_chips(flip)) if flip else x for x, flip in zip(early, FLIPS)]
    c2, late = chunk(bands, targets, [after_that(z2[0], c1[0])] + z2[1:], [c0, c1], (0,))
    for k in (1, 2):
        late.append(product(after_that(targets, late[-1]), k, [c0, c1, c2]))
    last = late[-1]
    late = [send(x, over_chips(flip)) for x, flip in zip(late, FLIPS)]
    early_sum = sum_parts(after_that(early[0], last), *early[1:])
    late.append(product(after_that(targets, early_sum, late[0]), 3, [c0, c1, c2]))
    moved = pick(goals, early_sum, *late)
    piece = moved[3]
    for k, x in zip((0, 1, 3), moved):
        piece = piece + send(x, mirrored([(2, k)]))
    filtered = jnp.concatenate([g0, g1, after_that(g2, late[3])], axis=1)
    piece = piece + send(piece, SWAP)
    w = v0.shape[1]
    turn_e = send(piece[w : 2 * w], TURN)
    turn_l = send(piece[3 * w : 5 * w], TURN_UP)
    return filtered, assemble(core, [piece, turn_e, turn_l], order)


def body(blocks, columns, counts, vectors, symmetric):
    rows, width = vectors.shape
    order = rows * lax.axis_size("orb")
    slot_of = slot_table(columns, counts)
    later = vectors
    if symmetric:
        tables = index_tables()
        slot_of, tables, later = lax.optimization_barrier((slot_of, tables, vectors))
    old = [
        (later if c else vectors)[:, c : min(c + LANES, width)] for c in range(0, width, LANES)
    ]
    hi, lo = densify(slot_of, blocks)
    if symmetric:
        return by_symmetry(hi, lo, old, order, tables)
    return in_turn(hi, lo, old, order)


def solution(mesh):
    placed = (P("orb", None, None, None), P("orb", None), P("orb"), P("orb", "band"))

    def whole(blocks, columns, counts, vectors):
        symmetric = (
            mesh.shape["orb"] == 8 and mesh.shape["band"] == 4 and vectors.shape[1] == 3 * LANES
        )
        return body(blocks, columns, counts, vectors, symmetric)

    return jax.shard_map(
        whole,
        mesh=mesh,
        in_specs=placed,
        out_specs=(P("orb", "band"), P("band", "orb")),
        check_vma=False,
    )
```

```python
import functools

import jax
import jax.numpy as jnp
from jax import lax
from jax.experimental import pallas as pl
from jax.experimental.pallas import tpu as pltpu
from jax.sharding import PartitionSpec as P

GROUP = 4
LANES = 128
MIB = 1024 * 1024
APPLY_MIB = 10


def split(x):
    hi = x.astype(jnp.bfloat16)
    lo = (x - hi.astype(jnp.float32)).astype(jnp.bfloat16)
    return hi, lo


def densify_kernel(slot_ref, blocks_ref, hi_ref, lo_ref, *, spread, reach):
    blk = blocks_ref.shape[2]
    step = pl.program_id(0)
    tile = (blk, 2 * blk)
    shift = lax.broadcasted_iota(jnp.int32, tile, 1) - lax.broadcasted_iota(jnp.int32, tile, 0)

    def one_row(i, carry):
        row = step * GROUP + i
        start = pl.multiple_of(i * blk, blk)
        for pair in range(spread // 2):
            left = slot_ref[row, 2 * pair]
            right = slot_ref[row, 2 * pair + 1]
            lblk = jnp.where(left >= 0, blocks_ref[i, jnp.maximum(left, 0)], 0.0)
            rblk = jnp.where(right >= 0, blocks_ref[i, jnp.maximum(right, 0)], 0.0)
            both = jnp.concatenate([lblk, rblk], axis=1)
            if reach <= 2 * pair + 1 and 2 * pair < reach + GROUP:
                both = both - jnp.where(shift == (reach + i - 2 * pair) * blk, 0.1, 0.0)
            hi, lo = split(both / 0.9)
            hi_ref[pl.ds(start, blk), pl.ds(pair * 2 * blk, 2 * blk)] = hi
            lo_ref[pl.ds(start, blk), pl.ds(pair * 2 * blk, 2 * blk)] = lo
        return carry

    lax.fori_loop(0, GROUP, one_row, 0)


def densify(slot_of, blocks):
    rows, slots, blk, _ = blocks.shape
    spread = slot_of.shape[1]
    shape = pltpu.VMEM((rows * blk, spread * blk), jnp.bfloat16)
    out = pl.BlockSpec((GROUP * blk, spread * blk), lambda g, _: (g, 0))
    return pl.pallas_call(
        functools.partial(densify_kernel, spread=spread, reach=rows),
        grid_spec=pltpu.PrefetchScalarGridSpec(
            num_scalar_prefetch=1,
            grid=(rows // GROUP,),
            in_specs=[pl.BlockSpec((GROUP, slots, blk, blk), lambda g, _: (g, 0, 0, 0))],
            out_specs=[out, out],
        ),
        out_shape=[shape, shape],
        compiler_params=pltpu.CompilerParams(vmem_limit_bytes=20 * MIB),
        cost_estimate=pl.CostEstimate(flops=0, bytes_accessed=60_000_000, transcendentals=0),
    )(slot_of, blocks)


def apply_kernel(core_ref, hi_ref, lo_ref, near_ref, far_ref, own_ref, *rest, second, turned):
    inside_ref, across_ref = (far_ref, near_ref) if turned else (near_ref, far_ref)
    old_ref = rest[0] if second else None
    out_ref, parts = rest[-2:]
    rows, width = own_ref.shape
    wide = hi_ref.shape[1]
    tall = wide - 2 * rows
    core = core_ref[0]
    for place, ref in ((1, own_ref), (2 - 2 * core, inside_ref), (2 * core, across_ref)):
        there = pl.ds(pl.multiple_of(place * rows, rows), rows)
        parts[there, pl.ds(0, width)], parts[there, pl.ds(width, width)] = split(ref[...])

    def one_group(step, carry):
        start = pl.multiple_of(step * tall, tall)
        here = pl.ds(start, tall)
        reached = pl.ds(start, wide)
        both = jnp.dot(hi_ref[here, :], parts[reached, :], preferred_element_type=jnp.float32)
        other = jnp.dot(
            lo_ref[here, :], parts[reached, pl.ds(0, width)], preferred_element_type=jnp.float32
        )
        product = both[:, :width] + (both[:, width:] + other)
        if second:
            product = 2.0 * product - old_ref[here, :]
        out_ref[here, :] = product
        return carry

    lax.fori_loop(0, rows // tall, one_group, 0)


def apply_step(core, hi, lo, halo, own, old=None, turned=False):
    rows, width = own.shape
    wide = hi.shape[1]
    second = old is not None
    hi, lo = (pltpu.with_memory_space_constraint(x, pltpu.VMEM) for x in (hi, lo))
    vmem = pl.BlockSpec(memory_space=pltpu.VMEM)
    return pl.pallas_call(
        functools.partial(apply_kernel, second=second, turned=turned),
        in_specs=[pl.BlockSpec(memory_space=pltpu.SMEM)] + [vmem] * (6 if second else 5),
        out_specs=vmem,
        out_shape=jax.ShapeDtypeStruct((rows, width), jnp.float32),
        scratch_shapes=[pltpu.VMEM((3 * rows, 2 * width), jnp.bfloat16)],
        compiler_params=pltpu.CompilerParams(vmem_limit_bytes=APPLY_MIB * MIB),
        cost_estimate=pl.CostEstimate(
            flops=8 * rows * wide * width, bytes_accessed=4 * rows * wide, transcendentals=0
        ),
    )(core, hi, lo, *(halo[::-1] if turned else halo), own, *([old] if second else []))


def slot_table(columns, counts):
    rows, slots = columns.shape
    total = rows * lax.axis_size("orb")
    spread = GROUP + 2 * rows
    ids = jnp.arange(rows, dtype=jnp.int32)
    offset = lax.axis_index("orb") * rows - rows
    place = (columns - offset) % total - (ids // GROUP * GROUP)[:, None]
    number = jnp.arange(slots, dtype=jnp.int32)
    place = jnp.where(number[None, :] < counts[:, None], place, -1)
    hit = place[:, :, None] == jnp.arange(spread, dtype=jnp.int32)[None, None, :]
    return jnp.max(jnp.where(hit, number[None, :, None], -1), axis=1)


def neighbours(x):
    size = lax.axis_size("orb")
    inside = [(i, i ^ 1) for i in range(size)]
    across = [(i, (i + 1 if i % 2 else i - 1) % size) for i in range(size)]
    return lax.ppermute(x, "orb", inside), lax.ppermute(x, "orb", across)


def after_that(x, *done):
    return lax.optimization_barrier((x, done))[0]


def store_parts(band_ref, ins, outs):
    hi_ref, lo_ref, thi_ref, tlo_ref = outs
    for place, ref in enumerate(ins):
        x = ref[...]
        width = x.shape[1]
        there = pl.ds(pl.multiple_of(band_ref[place] * width, width), width)
        hi_ref[:, there], lo_ref[:, there] = split(x)
        thi_ref[there, :], tlo_ref[there, :] = split(x.T)


def block_row(target, turned, right):
    rows = turned[0][0].shape[0] // 4
    there = pl.ds(pl.multiple_of(target * rows, rows), rows)
    thi = jnp.concatenate([hi[there, :] for hi, lo in turned], axis=0)
    tlo = jnp.concatenate([lo[there, :] for hi, lo in turned], axis=0)
    hi_ref, lo_ref = right
    total = jnp.dot(thi, lo_ref[...], preferred_element_type=jnp.float32)
    total += jnp.dot(tlo, hi_ref[...], preferred_element_type=jnp.float32)
    return total + jnp.dot(thi, hi_ref[...], preferred_element_type=jnp.float32)


def chunk_kernel(band_ref, target_ref, *refs, before, places, upper):
    ins, refs = refs[:4], refs[4:]
    olds, refs = [refs[4 * k : 4 * k + 4] for k in range(before)], refs[4 * before :]
    old_products, refs = (refs[: len(places)], refs[len(places) :]) if upper else ((), refs)
    new, outs = refs[:4], refs[4:]
    store_parts(band_ref, ins, new)
    turned = [x[2:] for x in olds] + [new[2:]]
    for k, place in enumerate(places):
        total = block_row(target_ref[place], turned, new[:2])
        if upper:
            high = old_products[k].shape[0]
            outs[k][pl.ds(0, high), :] = old_products[k][...]
            outs[k][pl.ds(high, total.shape[0]), :] = total
        else:
            outs[k][...] = total


def chunk(bands, targets, parts, olds, places, old_products=()):
    rows, width = parts[0].shape
    plain = pltpu.VMEM((rows, 4 * width), jnp.bfloat16)
    turned = pltpu.VMEM((4 * width, rows), jnp.bfloat16)
    high = width * (len(olds) + 1) + (old_products[0].shape[0] if old_products else 0)
    product = jax.ShapeDtypeStruct((high, 4 * width), jnp.float32)
    olds = [pltpu.with_memory_space_constraint(x, pltpu.VMEM) for old in olds for x in old]
    ins = [*parts, *olds, *old_products]
    vmem, smem = pl.BlockSpec(memory_space=pltpu.VMEM), pl.BlockSpec(memory_space=pltpu.SMEM)
    out = pl.pallas_call(
        functools.partial(
            chunk_kernel, before=len(olds) // 4, places=places, upper=bool(old_products)
        ),
        in_specs=[smem, smem] + [vmem] * len(ins),
        out_specs=[vmem] * (4 + len(places)),
        out_shape=[plain, plain, turned, turned] + [product] * len(places),
        compiler_params=pltpu.CompilerParams(vmem_limit_bytes=14 * MIB),
        cost_estimate=pl.CostEstimate(
            flops=24 * len(places) * high * width * rows, bytes_accessed=8_000_000, transcendentals=0
        ),
    )(bands, targets, *ins)
    return out[:4], list(out[4:])


def product_kernel(target_ref, *refs, place):
    out_ref = refs[-1]
    out_ref[...] = block_row(target_ref[place], [refs[k : k + 2] for k in range(2, len(refs) - 1, 2)], refs[:2])


def product(targets, place, chunks):
    rows, wide = chunks[-1][0].shape
    ins = [*chunks[-1][:2]] + [x for c in chunks for x in c[2:]]
    ins = [pltpu.with_memory_space_constraint(x, pltpu.VMEM) for x in ins]
    high = wide // 4 * len(chunks)
    vmem = pl.BlockSpec(memory_space=pltpu.VMEM)
    return pl.pallas_call(
        functools.partial(product_kernel, place=place),
        in_specs=[pl.BlockSpec(memory_space=pltpu.SMEM)] + [vmem] * len(ins),
        out_specs=vmem,
        out_shape=jax.ShapeDtypeStruct((high, wide), jnp.float32),
        compiler_params=pltpu.CompilerParams(vmem_limit_bytes=16 * MIB),
        cost_estimate=pl.CostEstimate(
            flops=6 * high * wide * rows, bytes_accessed=4_000_000, transcendentals=0
        ),
    )(targets, *ins)


def pick_kernel(goal_ref, *refs):
    ins, outs = refs[:4], refs[4:]
    width = ins[0].shape[1] // 4
    for k, out in enumerate(outs):
        there = pl.ds(pl.multiple_of(goal_ref[k] * width, width), width)
        x, y, u, v = (ref[:, there] for ref in ins)
        total = (x + y) + (u + v)
        out[...] = jnp.where(goal_ref[4] > 0, total, 0.0) if k == 3 else total


def pick(goals, parts):
    rows, size = parts[0].shape
    shape = jax.ShapeDtypeStruct((rows, size // 4), jnp.float32)
    vmem = pl.BlockSpec(memory_space=pltpu.VMEM)
    return pl.pallas_call(
        pick_kernel,
        in_specs=[pl.BlockSpec(memory_space=pltpu.SMEM)] + [vmem] * 4,
        out_specs=[vmem] * 4,
        out_shape=[shape] * 4,
        compiler_params=pltpu.CompilerParams(vmem_limit_bytes=8 * MIB),
        cost_estimate=pl.CostEstimate(flops=0, bytes_accessed=3_000_000, transcendentals=0),
    )(goals, *parts)


def assemble_kernel(core_ref, piece_ref, turn_e_ref, turn_l_ref, out_ref, *, scale):
    w = piece_ref.shape[1]
    first = jnp.concatenate([piece_ref[:w, :], turn_e_ref[...].T, turn_l_ref[:w, :].T], axis=0)
    second = jnp.concatenate([piece_ref[w : 3 * w, :], turn_l_ref[w:, :].T], axis=0)
    last = piece_ref[3 * w :, :]
    half = out_ref.shape[0]
    is_first = core_ref[0] == 0
    for k, x in enumerate((first, second, last)):
        out_ref[:, pl.ds(k * w, w)] = jnp.where(is_first, x[:half], x[half:]) * scale


def assemble(core, parts, order):
    w = parts[0].shape[1]
    vmem = pl.BlockSpec(memory_space=pltpu.VMEM)
    return pl.pallas_call(
        functools.partial(assemble_kernel, scale=1.0 / order),
        in_specs=[pl.BlockSpec(memory_space=pltpu.SMEM)] + [vmem] * len(parts),
        out_specs=vmem,
        out_shape=jax.ShapeDtypeStruct((3 * w // 2, 3 * w), jnp.float32),
        compiler_params=pltpu.CompilerParams(vmem_limit_bytes=12 * MIB),
        cost_estimate=pl.CostEstimate(flops=0, bytes_accessed=2_000_000, transcendentals=0),
    )(core, *parts).T


def linear(chip, core, z):
    return (chip * 2 + core) * 4 + z


def send(x, pairs):
    return lax.ppermute(x, ("orb", "band"), pairs)


def mirrored(pairs):
    out = []
    for chip in range(4):
        for a, b in pairs:
            out.append((linear(chip, 0, a), linear(chip, 0, b)))
            out.append((linear(chip, 1, 3 - a), linear(chip, 1, 3 - b)))
    return out


def gather_bands(x):
    return [x] + [send(x, mirrored([(source, 2)])) for source in (0, 1, 3)]


def over_chips(flip):
    return [
        (linear(chip, core, 2 - core), linear(chip ^ flip, core, 2 - core))
        for chip in range(4)
        for core in range(2)
    ]


FLIPS = (3, 1, 2, 0)
ALL = (0, 1, 2, 3)
EVERY = [(q, c, z) for q in range(4) for c in range(2) for z in range(4)]
SWAP = [(linear(q, c, z), linear(q, 1 - c, z)) for q, c, z in EVERY]
TURN = [(linear(q, c, z), linear(z, c, q)) for q, c, z in EVERY]
TURN_UP = [pair for pair in TURN if pair[0] // 4 % 2 == 1]


def simple_gram(filtered):
    partial_gram = jnp.dot(
        filtered.T,
        lax.all_gather(filtered, "band", axis=1, tiled=True),
        precision=lax.Precision.HIGH,
        preferred_element_type=jnp.float32,
    )
    return lax.psum_scatter(partial_gram, "orb", scatter_dimension=1, tiled=True)


def in_turn(hi, lo, old, order):
    core = (lax.axis_index("orb") & 1)[None]
    first = [apply_step(core, hi, lo, neighbours(x), x) for x in old]
    filtered = [apply_step(core, hi, lo, neighbours(x), x, v) for x, v in zip(first, old)]
    filtered = jnp.concatenate(filtered, axis=1)
    return filtered, simple_gram(filtered) / order


def index_tables():
    orb, z = lax.axis_index("orb"), lax.axis_index("band")
    chip, core = orb >> 1, orb & 1
    bands = jnp.stack([b + core * (3 - 2 * b) for b in (2, 0, 1, 3)])
    holder = (z == 2 - core).astype(jnp.int32)
    goals = jnp.stack([k + core * (3 - 2 * k) for k in (0, 1, 3)] + [z, holder])
    targets = jnp.stack([chip ^ flip for flip in FLIPS])
    return bands, goals, targets, core[None]


def by_symmetry(hi, lo, old, order, tables):
    bands, goals, targets, core = tables

    def one(x, halo, v=None, turned=False):
        return apply_step(core, hi, lo, halo, x, v, turned)

    v0, v1, v2 = old
    hv = [neighbours(x) for x in old]
    f0 = one(v0, hv[0])
    hf0 = neighbours(f0)
    f1 = one(v1, hv[1])
    hf1 = neighbours(f1)
    f2 = one(v2, hv[2])
    hf2 = neighbours(f2)
    g0 = one(f0, hf0, v0)
    z0 = gather_bands(g0)
    g1 = one(after_that(f1, g0), hf1, v1)
    z1 = gather_bands(g1)
    c0, upper = chunk(bands, targets, [after_that(z0[0], g1)] + z0[1:], [], ALL)
    g2 = one(after_that(f2, upper[0]), hf2, v2, turned=True)
    z2 = gather_bands(g2)
    c1, early = chunk(bands, targets, [after_that(z1[0], g2)] + z1[1:], [c0], ALL, upper)
    early[0] = send(early[0], over_chips(FLIPS[0]))
    early[1] = send(early[1], over_chips(FLIPS[1]))
    c2, late = chunk(bands, targets, [after_that(z2[0], c1[0])] + z2[1:], [c0, c1], (0,))
    early[2] = send(after_that(early[2], late[0]), over_chips(FLIPS[2]))
    late.append(product(after_that(targets, late[0], early[0], early[1]), 1, [c0, c1, c2]))
    late.append(product(after_that(targets, late[1]), 2, [c0, c1, c2]))

    def deliver(parts):
        moved = pick(goals, parts)
        return [moved[3]] + [send(x, mirrored([(2, k)])) for k, x in zip((0, 1, 3), moved)]

    late[0] = send(late[0], over_chips(FLIPS[0]))
    arrived = [deliver([after_that(early[0], late[2], late[0])] + early[1:])]
    late[1:] = [send(x, over_chips(flip)) for x, flip in zip(late[1:], FLIPS[1:])]
    late.append(product(after_that(targets, arrived[0][0], late[1]), 3, [c0, c1, c2]))
    arrived.append(deliver(late))
    filtered = jnp.concatenate([g0, g1, after_that(g2, late[3])], axis=1)
    piece = jnp.concatenate([(x[0] + x[1]) + (x[2] + x[3]) for x in arrived], axis=0)
    piece = piece + send(piece, SWAP)
    w = v0.shape[1]
    turn_e = send(piece[w : 2 * w], TURN)
    turn_l = send(piece[3 * w : 5 * w], TURN_UP)
    return filtered, assemble(core, [piece, turn_e, turn_l], order)


def body(blocks, columns, counts, vectors, symmetric):
    rows, width = vectors.shape
    order = rows * lax.axis_size("orb")
    slot_of = slot_table(columns, counts)
    later = vectors
    if symmetric:
        tables = index_tables()
        slot_of, tables, later = lax.optimization_barrier((slot_of, tables, vectors))
    old = [
        (later if c else vectors)[:, c : min(c + LANES, width)] for c in range(0, width, LANES)
    ]
    hi, lo = densify(slot_of, blocks)
    if symmetric:
        return by_symmetry(hi, lo, old, order, tables)
    return in_turn(hi, lo, old, order)


def solution(mesh):
    placed = (P("orb", None, None, None), P("orb", None), P("orb"), P("orb", "band"))

    def whole(blocks, columns, counts, vectors):
        symmetric = (
            mesh.shape["orb"] == 8 and mesh.shape["band"] == 4 and vectors.shape[1] == 3 * LANES
        )
        return body(blocks, columns, counts, vectors, symmetric)

    return jax.shard_map(
        whole,
        mesh=mesh,
        in_specs=placed,
        out_specs=(P("orb", "band"), P("band", "orb")),
        check_vma=False,
    )
```

```python
import functools

import jax
import jax.numpy as jnp
from jax import lax
from jax.experimental import pallas as pl
from jax.experimental.pallas import tpu as pltpu
from jax.sharding import PartitionSpec as P

GROUP = 4
LANES = 128
MIB = 1024 * 1024
APPLY_MIB = 10


def split(x):
    hi = x.astype(jnp.bfloat16)
    lo = (x - hi.astype(jnp.float32)).astype(jnp.bfloat16)
    return hi, lo


def densify_kernel(slot_ref, blocks_ref, hi_ref, lo_ref, *, spread, reach):
    blk = blocks_ref.shape[2]
    step = pl.program_id(0)
    tile = (blk, 2 * blk)
    shift = lax.broadcasted_iota(jnp.int32, tile, 1) - lax.broadcasted_iota(jnp.int32, tile, 0)

    def one_row(i, carry):
        row = step * GROUP + i
        start = pl.multiple_of(i * blk, blk)
        for pair in range(spread // 2):
            left = slot_ref[row, 2 * pair]
            right = slot_ref[row, 2 * pair + 1]
            lblk = jnp.where(left >= 0, blocks_ref[i, jnp.maximum(left, 0)], 0.0)
            rblk = jnp.where(right >= 0, blocks_ref[i, jnp.maximum(right, 0)], 0.0)
            both = jnp.concatenate([lblk, rblk], axis=1)
            if reach <= 2 * pair + 1 and 2 * pair < reach + GROUP:
                both = both - jnp.where(shift == (reach + i - 2 * pair) * blk, 0.1, 0.0)
            hi, lo = split(both / 0.9)
            hi_ref[pl.ds(start, blk), pl.ds(pair * 2 * blk, 2 * blk)] = hi
            lo_ref[pl.ds(start, blk), pl.ds(pair * 2 * blk, 2 * blk)] = lo
        return carry

    lax.fori_loop(0, GROUP, one_row, 0)


def densify(slot_of, blocks):
    rows, slots, blk, _ = blocks.shape
    spread = slot_of.shape[1]
    shape = pltpu.VMEM((rows * blk, spread * blk), jnp.bfloat16)
    out = pl.BlockSpec((GROUP * blk, spread * blk), lambda g, _: (g, 0))
    return pl.pallas_call(
        functools.partial(densify_kernel, spread=spread, reach=rows),
        grid_spec=pltpu.PrefetchScalarGridSpec(
            num_scalar_prefetch=1,
            grid=(rows // GROUP,),
            in_specs=[pl.BlockSpec((GROUP, slots, blk, blk), lambda g, _: (g, 0, 0, 0))],
            out_specs=[out, out],
        ),
        out_shape=[shape, shape],
        compiler_params=pltpu.CompilerParams(vmem_limit_bytes=20 * MIB),
        cost_estimate=pl.CostEstimate(flops=0, bytes_accessed=60_000_000, transcendentals=0),
    )(slot_of, blocks)


def apply_kernel(core_ref, hi_ref, lo_ref, near_ref, far_ref, own_ref, *rest, second, turned):
    inside_ref, across_ref = (far_ref, near_ref) if turned else (near_ref, far_ref)
    old_ref = rest[0] if second else None
    out_ref, parts = rest[-2:]
    rows, width = own_ref.shape
    wide = hi_ref.shape[1]
    tall = wide - 2 * rows
    core = core_ref[0]
    for place, ref in ((1, own_ref), (2 - 2 * core, inside_ref), (2 * core, across_ref)):
        there = pl.ds(pl.multiple_of(place * rows, rows), rows)
        parts[there, pl.ds(0, width)], parts[there, pl.ds(width, width)] = split(ref[...])

    def one_group(step, carry):
        start = pl.multiple_of(step * tall, tall)
        here = pl.ds(start, tall)
        reached = pl.ds(start, wide)
        both = jnp.dot(hi_ref[here, :], parts[reached, :], preferred_element_type=jnp.float32)
        other = jnp.dot(
            lo_ref[here, :], parts[reached, pl.ds(0, width)], preferred_element_type=jnp.float32
        )
        product = both[:, :width] + (both[:, width:] + other)
        if second:
            product = 2.0 * product - old_ref[here, :]
        out_ref[here, :] = product
        return carry

    lax.fori_loop(0, rows // tall, one_group, 0)


def apply_step(core, hi, lo, halo, own, old=None, turned=False):
    rows, width = own.shape
    wide = hi.shape[1]
    second = old is not None
    hi, lo = (pltpu.with_memory_space_constraint(x, pltpu.VMEM) for x in (hi, lo))
    vmem = pl.BlockSpec(memory_space=pltpu.VMEM)
    return pl.pallas_call(
        functools.partial(apply_kernel, second=second, turned=turned),
        in_specs=[pl.BlockSpec(memory_space=pltpu.SMEM)] + [vmem] * (6 if second else 5),
        out_specs=vmem,
        out_shape=jax.ShapeDtypeStruct((rows, width), jnp.float32),
        scratch_shapes=[pltpu.VMEM((3 * rows, 2 * width), jnp.bfloat16)],
        compiler_params=pltpu.CompilerParams(vmem_limit_bytes=APPLY_MIB * MIB),
        cost_estimate=pl.CostEstimate(
            flops=8 * rows * wide * width, bytes_accessed=4 * rows * wide, transcendentals=0
        ),
    )(core, hi, lo, *(halo[::-1] if turned else halo), own, *([old] if second else []))


def slot_table(columns, counts):
    rows, slots = columns.shape
    total = rows * lax.axis_size("orb")
    spread = GROUP + 2 * rows
    ids = jnp.arange(rows, dtype=jnp.int32)
    offset = lax.axis_index("orb") * rows - rows
    place = (columns - offset) % total - (ids // GROUP * GROUP)[:, None]
    number = jnp.arange(slots, dtype=jnp.int32)
    place = jnp.where(number[None, :] < counts[:, None], place, -1)
    hit = place[:, :, None] == jnp.arange(spread, dtype=jnp.int32)[None, None, :]
    return jnp.max(jnp.where(hit, number[None, :, None], -1), axis=1)


def neighbours(x):
    size = lax.axis_size("orb")
    inside = [(i, i ^ 1) for i in range(size)]
    across = [(i, (i + 1 if i % 2 else i - 1) % size) for i in range(size)]
    return lax.ppermute(x, "orb", inside), lax.ppermute(x, "orb", across)


def after_that(x, *done):
    return lax.optimization_barrier((x, done))[0]


def store_parts(band_ref, ins, outs):
    hi_ref, lo_ref, thi_ref, tlo_ref = outs
    for place, ref in enumerate(ins):
        x = ref[...]
        width = x.shape[1]
        there = pl.ds(pl.multiple_of(band_ref[place] * width, width), width)
        hi_ref[:, there], lo_ref[:, there] = split(x)
        thi_ref[there, :], tlo_ref[there, :] = split(x.T)


def block_row(target, turned, right):
    rows = turned[0][0].shape[0] // 4
    there = pl.ds(pl.multiple_of(target * rows, rows), rows)
    thi = jnp.concatenate([hi[there, :] for hi, lo in turned], axis=0)
    tlo = jnp.concatenate([lo[there, :] for hi, lo in turned], axis=0)
    hi_ref, lo_ref = right
    total = jnp.dot(thi, lo_ref[...], preferred_element_type=jnp.float32)
    total += jnp.dot(tlo, hi_ref[...], preferred_element_type=jnp.float32)
    return total + jnp.dot(thi, hi_ref[...], preferred_element_type=jnp.float32)


def chunk_kernel(band_ref, target_ref, *refs, before, places, upper):
    ins, refs = refs[:4], refs[4:]
    olds, refs = [refs[4 * k : 4 * k + 4] for k in range(before)], refs[4 * before :]
    old_products, refs = (refs[: len(places)], refs[len(places) :]) if upper else ((), refs)
    new, outs = refs[:4], refs[4:]
    store_parts(band_ref, ins, new)
    turned = [x[2:] for x in olds] + [new[2:]]
    for k, place in enumerate(places):
        total = block_row(target_ref[place], turned, new[:2])
        if upper:
            high = old_products[k].shape[0]
            outs[k][pl.ds(0, high), :] = old_products[k][...]
            outs[k][pl.ds(high, total.shape[0]), :] = total
        else:
            outs[k][...] = total


def chunk(bands, targets, parts, olds, places, old_products=()):
    rows, width = parts[0].shape
    plain = pltpu.VMEM((rows, 4 * width), jnp.bfloat16)
    turned = pltpu.VMEM((4 * width, rows), jnp.bfloat16)
    high = width * (len(olds) + 1) + (old_products[0].shape[0] if old_products else 0)
    product = jax.ShapeDtypeStruct((high, 4 * width), jnp.float32)
    olds = [pltpu.with_memory_space_constraint(x, pltpu.VMEM) for old in olds for x in old]
    ins = [*parts, *olds, *old_products]
    vmem, smem = pl.BlockSpec(memory_space=pltpu.VMEM), pl.BlockSpec(memory_space=pltpu.SMEM)
    out = pl.pallas_call(
        functools.partial(
            chunk_kernel, before=len(olds) // 4, places=places, upper=bool(old_products)
        ),
        in_specs=[smem, smem] + [vmem] * len(ins),
        out_specs=[vmem] * (4 + len(places)),
        out_shape=[plain, plain, turned, turned] + [product] * len(places),
        compiler_params=pltpu.CompilerParams(vmem_limit_bytes=14 * MIB),
        cost_estimate=pl.CostEstimate(
            flops=24 * len(places) * high * width * rows, bytes_accessed=8_000_000, transcendentals=0
        ),
    )(bands, targets, *ins)
    return out[:4], list(out[4:])


def product_kernel(target_ref, *refs, place):
    out_ref = refs[-1]
    out_ref[...] = block_row(target_ref[place], [refs[k : k + 2] for k in range(2, len(refs) - 1, 2)], refs[:2])


def product(targets, place, chunks):
    rows, wide = chunks[-1][0].shape
    ins = [*chunks[-1][:2]] + [x for c in chunks for x in c[2:]]
    ins = [pltpu.with_memory_space_constraint(x, pltpu.VMEM) for x in ins]
    high = wide // 4 * len(chunks)
    vmem = pl.BlockSpec(memory_space=pltpu.VMEM)
    return pl.pallas_call(
        functools.partial(product_kernel, place=place),
        in_specs=[pl.BlockSpec(memory_space=pltpu.SMEM)] + [vmem] * len(ins),
        out_specs=vmem,
        out_shape=jax.ShapeDtypeStruct((high, wide), jnp.float32),
        compiler_params=pltpu.CompilerParams(vmem_limit_bytes=16 * MIB),
        cost_estimate=pl.CostEstimate(
            flops=6 * high * wide * rows, bytes_accessed=4_000_000, transcendentals=0
        ),
    )(targets, *ins)


def pick_kernel(goal_ref, *refs):
    ins, outs = refs[:4], refs[4:]
    width = ins[0].shape[1] // 4
    for k, out in enumerate(outs):
        there = pl.ds(pl.multiple_of(goal_ref[k] * width, width), width)
        x, y, u, v = (ref[:, there] for ref in ins)
        total = (x + y) + (u + v)
        out[...] = jnp.where(goal_ref[4] > 0, total, 0.0) if k == 3 else total


def pick(goals, parts):
    rows, size = parts[0].shape
    shape = jax.ShapeDtypeStruct((rows, size // 4), jnp.float32)
    vmem = pl.BlockSpec(memory_space=pltpu.VMEM)
    return pl.pallas_call(
        pick_kernel,
        in_specs=[pl.BlockSpec(memory_space=pltpu.SMEM)] + [vmem] * 4,
        out_specs=[vmem] * 4,
        out_shape=[shape] * 4,
        compiler_params=pltpu.CompilerParams(vmem_limit_bytes=8 * MIB),
        cost_estimate=pl.CostEstimate(flops=0, bytes_accessed=3_000_000, transcendentals=0),
    )(goals, *parts)


def assemble_kernel(core_ref, piece_ref, turn_e_ref, turn_l_ref, out_ref, *, scale):
    w = piece_ref.shape[1]
    first = jnp.concatenate([piece_ref[:w, :], turn_e_ref[...].T, turn_l_ref[:w, :].T], axis=0)
    second = jnp.concatenate([piece_ref[w : 3 * w, :], turn_l_ref[w:, :].T], axis=0)
    last = piece_ref[3 * w :, :]
    half = out_ref.shape[0]
    is_first = core_ref[0] == 0
    for k, x in enumerate((first, second, last)):
        out_ref[:, pl.ds(k * w, w)] = jnp.where(is_first, x[:half], x[half:]) * scale


def assemble(core, parts, order):
    w = parts[0].shape[1]
    vmem = pl.BlockSpec(memory_space=pltpu.VMEM)
    return pl.pallas_call(
        functools.partial(assemble_kernel, scale=1.0 / order),
        in_specs=[pl.BlockSpec(memory_space=pltpu.SMEM)] + [vmem] * len(parts),
        out_specs=vmem,
        out_shape=jax.ShapeDtypeStruct((3 * w // 2, 3 * w), jnp.float32),
        compiler_params=pltpu.CompilerParams(vmem_limit_bytes=12 * MIB),
        cost_estimate=pl.CostEstimate(flops=0, bytes_accessed=2_000_000, transcendentals=0),
    )(core, *parts).T


def linear(chip, core, z):
    return (chip * 2 + core) * 4 + z


def send(x, pairs):
    return lax.ppermute(x, ("orb", "band"), pairs)


def mirrored(pairs):
    out = []
    for chip in range(4):
        for a, b in pairs:
            out.append((linear(chip, 0, a), linear(chip, 0, b)))
            out.append((linear(chip, 1, 3 - a), linear(chip, 1, 3 - b)))
    return out


def gather_bands(x):
    return [x] + [send(x, mirrored([(source, 2)])) for source in (0, 1, 3)]


def over_chips(flip):
    return [
        (linear(chip, core, 2 - core), linear(chip ^ flip, core, 2 - core))
        for chip in range(4)
        for core in range(2)
    ]


FLIPS = (3, 1, 2, 0)
ALL = (0, 1, 2, 3)
EVERY = [(q, c, z) for q in range(4) for c in range(2) for z in range(4)]
SWAP = [(linear(q, c, z), linear(q, 1 - c, z)) for q, c, z in EVERY]
TURN = [(linear(q, c, z), linear(z, c, q)) for q, c, z in EVERY]
TURN_UP = [pair for pair in TURN if pair[0] // 4 % 2 == 1]


def simple_gram(filtered):
    partial_gram = jnp.dot(
        filtered.T,
        lax.all_gather(filtered, "band", axis=1, tiled=True),
        precision=lax.Precision.HIGH,
        preferred_element_type=jnp.float32,
    )
    return lax.psum_scatter(partial_gram, "orb", scatter_dimension=1, tiled=True)


def in_turn(hi, lo, old, order):
    core = (lax.axis_index("orb") & 1)[None]
    first = [apply_step(core, hi, lo, neighbours(x), x) for x in old]
    filtered = [apply_step(core, hi, lo, neighbours(x), x, v) for x, v in zip(first, old)]
    filtered = jnp.concatenate(filtered, axis=1)
    return filtered, simple_gram(filtered) / order


def index_tables():
    orb, z = lax.axis_index("orb"), lax.axis_index("band")
    chip, core = orb >> 1, orb & 1
    bands = jnp.stack([b + core * (3 - 2 * b) for b in (2, 0, 1, 3)])
    holder = (z == 2 - core).astype(jnp.int32)
    goals = jnp.stack([k + core * (3 - 2 * k) for k in (0, 1, 3)] + [z, holder])
    targets = jnp.stack([chip ^ flip for flip in FLIPS])
    return bands, goals, targets, core[None]


def by_symmetry(hi, lo, old, order, tables):
    bands, goals, targets, core = tables

    def one(x, halo, v=None, turned=False):
        return apply_step(core, hi, lo, halo, x, v, turned)

    v0, v1, v2 = old
    hv = [neighbours(x) for x in old]
    f0 = one(v0, hv[0])
    hf0 = neighbours(f0)
    f1 = one(v1, hv[1])
    hf1 = neighbours(f1)
    f2 = one(v2, hv[2])
    hf2 = neighbours(f2)
    g0 = one(f0, hf0, v0)
    z0 = gather_bands(g0)
    g1 = one(after_that(f1, g0), hf1, v1)
    z1 = gather_bands(g1)
    c0, upper = chunk(bands, targets, [after_that(z0[0], g1)] + z0[1:], [], ALL)
    g2 = one(after_that(f2, upper[0]), hf2, v2, turned=True)
    z2 = gather_bands(g2)
    c1, early = chunk(bands, targets, [after_that(z1[0], g2)] + z1[1:], [c0], ALL, upper)
    early = [send(x, over_chips(flip)) if flip else x for x, flip in zip(early, FLIPS)]
    c2, late = chunk(bands, targets, [after_that(z2[0], c1[0])] + z2[1:], [c0, c1], (0,))
    for k in (1, 2):
        late.append(product(after_that(targets, late[-1]), k, [c0, c1, c2]))
    last = late[-1]
    late = [send(x, over_chips(flip)) for x, flip in zip(late, FLIPS)]

    def deliver(parts):
        moved = pick(goals, parts)
        return [moved[3]] + [send(x, mirrored([(2, k)])) for k, x in zip((0, 1, 3), moved)]

    arrived = [deliver([after_that(early[0], last)] + early[1:])]
    late.append(product(after_that(targets, arrived[0][0], late[0]), 3, [c0, c1, c2]))
    arrived.append(deliver(late))
    filtered = jnp.concatenate([g0, g1, after_that(g2, late[3])], axis=1)
    piece = jnp.concatenate([(x[0] + x[1]) + (x[2] + x[3]) for x in arrived], axis=0)
    piece = piece + send(piece, SWAP)
    w = v0.shape[1]
    turn_e = send(piece[w : 2 * w], TURN)
    turn_l = send(piece[3 * w : 5 * w], TURN_UP)
    return filtered, assemble(core, [piece, turn_e, turn_l], order)


def body(blocks, columns, counts, vectors, symmetric):
    rows, width = vectors.shape
    order = rows * lax.axis_size("orb")
    slot_of = slot_table(columns, counts)
    later = vectors
    if symmetric:
        tables = index_tables()
        slot_of, tables, later = lax.optimization_barrier((slot_of, tables, vectors))
    old = [
        (later if c else vectors)[:, c : min(c + LANES, width)] for c in range(0, width, LANES)
    ]
    hi, lo = densify(slot_of, blocks)
    if symmetric:
        return by_symmetry(hi, lo, old, order, tables)
    return in_turn(hi, lo, old, order)


def solution(mesh):
    placed = (P("orb", None, None, None), P("orb", None), P("orb"), P("orb", "band"))

    def whole(blocks, columns, counts, vectors):
        symmetric = (
            mesh.shape["orb"] == 8 and mesh.shape["band"] == 4 and vectors.shape[1] == 3 * LANES
        )
        return body(blocks, columns, counts, vectors, symmetric)

    return jax.shard_map(
        whole,
        mesh=mesh,
        in_specs=placed,
        out_specs=(P("orb", "band"), P("band", "orb")),
        check_vma=False,
    )
```

```python
import functools

import jax
import jax.numpy as jnp
from jax import lax
from jax.experimental import pallas as pl
from jax.experimental.pallas import tpu as pltpu
from jax.sharding import PartitionSpec as P

GROUP = 4
LANES = 128
MIB = 1024 * 1024
APPLY_MIB = 10


def split(x):
    hi = x.astype(jnp.bfloat16)
    lo = (x - hi.astype(jnp.float32)).astype(jnp.bfloat16)
    return hi, lo


def densify_kernel(slot_ref, blocks_ref, hi_ref, lo_ref, *, spread, reach):
    blk = blocks_ref.shape[2]
    step = pl.program_id(0)
    tile = (blk, 2 * blk)
    shift = lax.broadcasted_iota(jnp.int32, tile, 1) - lax.broadcasted_iota(jnp.int32, tile, 0)

    def one_row(i, carry):
        row = step * GROUP + i
        start = pl.multiple_of(i * blk, blk)
        for pair in range(spread // 2):
            left = slot_ref[row, 2 * pair]
            right = slot_ref[row, 2 * pair + 1]
            lblk = jnp.where(left >= 0, blocks_ref[i, jnp.maximum(left, 0)], 0.0)
            rblk = jnp.where(right >= 0, blocks_ref[i, jnp.maximum(right, 0)], 0.0)
            both = jnp.concatenate([lblk, rblk], axis=1)
            if reach <= 2 * pair + 1 and 2 * pair < reach + GROUP:
                both = both - jnp.where(shift == (reach + i - 2 * pair) * blk, 0.1, 0.0)
            hi, lo = split(both / 0.9)
            hi_ref[pl.ds(start, blk), pl.ds(pair * 2 * blk, 2 * blk)] = hi
            lo_ref[pl.ds(start, blk), pl.ds(pair * 2 * blk, 2 * blk)] = lo
        return carry

    lax.fori_loop(0, GROUP, one_row, 0)


def densify(slot_of, blocks):
    rows, slots, blk, _ = blocks.shape
    spread = slot_of.shape[1]
    shape = pltpu.VMEM((rows * blk, spread * blk), jnp.bfloat16)
    out = pl.BlockSpec((GROUP * blk, spread * blk), lambda g, _: (g, 0))
    return pl.pallas_call(
        functools.partial(densify_kernel, spread=spread, reach=rows),
        grid_spec=pltpu.PrefetchScalarGridSpec(
            num_scalar_prefetch=1,
            grid=(rows // GROUP,),
            in_specs=[pl.BlockSpec((GROUP, slots, blk, blk), lambda g, _: (g, 0, 0, 0))],
            out_specs=[out, out],
        ),
        out_shape=[shape, shape],
        compiler_params=pltpu.CompilerParams(vmem_limit_bytes=20 * MIB),
        cost_estimate=pl.CostEstimate(flops=0, bytes_accessed=60_000_000, transcendentals=0),
    )(slot_of, blocks)


def apply_kernel(core_ref, hi_ref, lo_ref, near_ref, far_ref, own_ref, *rest, second, turned):
    inside_ref, across_ref = (far_ref, near_ref) if turned else (near_ref, far_ref)
    old_ref = rest[0] if second else None
    out_ref, parts = rest[-2:]
    rows, width = own_ref.shape
    wide = hi_ref.shape[1]
    tall = wide - 2 * rows
    core = core_ref[0]
    for place, ref in ((1, own_ref), (2 - 2 * core, inside_ref), (2 * core, across_ref)):
        there = pl.ds(pl.multiple_of(place * rows, rows), rows)
        parts[there, pl.ds(0, width)], parts[there, pl.ds(width, width)] = split(ref[...])

    def one_group(step, carry):
        start = pl.multiple_of(step * tall, tall)
        here = pl.ds(start, tall)
        reached = pl.ds(start, wide)
        both = jnp.dot(hi_ref[here, :], parts[reached, :], preferred_element_type=jnp.float32)
        other = jnp.dot(
            lo_ref[here, :], parts[reached, pl.ds(0, width)], preferred_element_type=jnp.float32
        )
        product = both[:, :width] + (both[:, width:] + other)
        if second:
            product = 2.0 * product - old_ref[here, :]
        out_ref[here, :] = product
        return carry

    lax.fori_loop(0, rows // tall, one_group, 0)


def apply_step(core, hi, lo, halo, own, old=None, turned=False):
    rows, width = own.shape
    wide = hi.shape[1]
    second = old is not None
    hi, lo = (pltpu.with_memory_space_constraint(x, pltpu.VMEM) for x in (hi, lo))
    vmem = pl.BlockSpec(memory_space=pltpu.VMEM)
    return pl.pallas_call(
        functools.partial(apply_kernel, second=second, turned=turned),
        in_specs=[pl.BlockSpec(memory_space=pltpu.SMEM)] + [vmem] * (6 if second else 5),
        out_specs=vmem,
        out_shape=jax.ShapeDtypeStruct((rows, width), jnp.float32),
        scratch_shapes=[pltpu.VMEM((3 * rows, 2 * width), jnp.bfloat16)],
        compiler_params=pltpu.CompilerParams(vmem_limit_bytes=APPLY_MIB * MIB),
        cost_estimate=pl.CostEstimate(
            flops=8 * rows * wide * width, bytes_accessed=4 * rows * wide, transcendentals=0
        ),
    )(core, hi, lo, *(halo[::-1] if turned else halo), own, *([old] if second else []))


def part_kernel(core_ref, hi_ref, lo_ref, *refs, late):
    out_ref, parts = refs[-2:]
    blocks = refs[:1] if late else refs[:2]
    rows, width = blocks[0].shape
    wide = hi_ref.shape[1]
    tall = wide - 2 * rows
    core = core_ref[0]
    for k, ref in enumerate(blocks):
        place = 0 if late else (core if k == 0 else 1 - core)
        there = pl.ds(pl.multiple_of(place * rows, rows), rows)
        parts[there, pl.ds(0, width)], parts[there, pl.ds(width, width)] = split(ref[...])
    for which in range(2):

        @pl.when(core == which)
        def _():
            for step in range(rows // tall):
                start = step * tall
                low, high = (rows, 3 * rows) if which == 0 else (0, 2 * rows)
                if late:
                    low, high = (0, rows) if which == 0 else (2 * rows, 3 * rows)
                first, last = max(low, start), min(high, start + wide)
                size, column, row = last - first, first - start, first - low
                here = pl.ds(start, tall)
                reached = pl.ds(row, size)
                both = jnp.dot(
                    hi_ref[here, pl.ds(column, size)],
                    parts[reached, :],
                    preferred_element_type=jnp.float32,
                )
                other = jnp.dot(
                    lo_ref[here, pl.ds(column, size)],
                    parts[reached, pl.ds(0, width)],
                    preferred_element_type=jnp.float32,
                )
                product = both[:, :width] + (both[:, width:] + other)
                if late:
                    product = 2.0 * (refs[1][here, :] + product) - refs[2][here, :]
                out_ref[here, :] = product


def apply_part(core, hi, lo, *ins, late):
    rows, width = ins[0].shape
    hi, lo = (pltpu.with_memory_space_constraint(x, pltpu.VMEM) for x in (hi, lo))
    vmem = pl.BlockSpec(memory_space=pltpu.VMEM)
    return pl.pallas_call(
        functools.partial(part_kernel, late=late),
        in_specs=[pl.BlockSpec(memory_space=pltpu.SMEM)] + [vmem] * (2 + len(ins)),
        out_specs=vmem,
        out_shape=jax.ShapeDtypeStruct((rows, width), jnp.float32),
        scratch_shapes=[pltpu.VMEM(((1 if late else 2) * rows, 2 * width), jnp.bfloat16)],
        compiler_params=pltpu.CompilerParams(vmem_limit_bytes=APPLY_MIB * MIB),
        cost_estimate=pl.CostEstimate(
            flops=(2 if late else 6) * rows * hi.shape[1] * width,
            bytes_accessed=4 * rows * hi.shape[1],
            transcendentals=0,
        ),
    )(core, hi, lo, *ins)


def slot_table(columns, counts):
    rows, slots = columns.shape
    total = rows * lax.axis_size("orb")
    spread = GROUP + 2 * rows
    ids = jnp.arange(rows, dtype=jnp.int32)
    offset = lax.axis_index("orb") * rows - rows
    place = (columns - offset) % total - (ids // GROUP * GROUP)[:, None]
    number = jnp.arange(slots, dtype=jnp.int32)
    place = jnp.where(number[None, :] < counts[:, None], place, -1)
    hit = place[:, :, None] == jnp.arange(spread, dtype=jnp.int32)[None, None, :]
    return jnp.max(jnp.where(hit, number[None, :, None], -1), axis=1)


def neighbours(x):
    size = lax.axis_size("orb")
    inside = [(i, i ^ 1) for i in range(size)]
    across = [(i, (i + 1 if i % 2 else i - 1) % size) for i in range(size)]
    return lax.ppermute(x, "orb", inside), lax.ppermute(x, "orb", across)


def after_that(x, *done):
    return lax.optimization_barrier((x, done))[0]


def store_parts(band_ref, ins, outs):
    hi_ref, lo_ref, thi_ref, tlo_ref = outs
    for place, ref in enumerate(ins):
        x = ref[...]
        width = x.shape[1]
        there = pl.ds(pl.multiple_of(band_ref[place] * width, width), width)
        hi_ref[:, there], lo_ref[:, there] = split(x)
        thi_ref[there, :], tlo_ref[there, :] = split(x.T)


def block_row(target, turned, right):
    rows = turned[0][0].shape[0] // 4
    there = pl.ds(pl.multiple_of(target * rows, rows), rows)
    thi = jnp.concatenate([hi[there, :] for hi, lo in turned], axis=0)
    tlo = jnp.concatenate([lo[there, :] for hi, lo in turned], axis=0)
    hi_ref, lo_ref = right
    total = jnp.dot(thi, lo_ref[...], preferred_element_type=jnp.float32)
    total += jnp.dot(tlo, hi_ref[...], preferred_element_type=jnp.float32)
    return total + jnp.dot(thi, hi_ref[...], preferred_element_type=jnp.float32)


def chunk_kernel(band_ref, target_ref, *refs, before, places, upper):
    ins, refs = refs[:4], refs[4:]
    olds, refs = [refs[4 * k : 4 * k + 4] for k in range(before)], refs[4 * before :]
    old_products, refs = (refs[: len(places)], refs[len(places) :]) if upper else ((), refs)
    new, outs = refs[:4], refs[4:]
    store_parts(band_ref, ins, new)
    turned = [x[2:] for x in olds] + [new[2:]]
    for k, place in enumerate(places):
        total = block_row(target_ref[place], turned, new[:2])
        if upper:
            high = old_products[k].shape[0]
            outs[k][pl.ds(0, high), :] = old_products[k][...]
            outs[k][pl.ds(high, total.shape[0]), :] = total
        else:
            outs[k][...] = total


def chunk(bands, targets, parts, olds, places, old_products=()):
    rows, width = parts[0].shape
    plain = pltpu.VMEM((rows, 4 * width), jnp.bfloat16)
    turned = pltpu.VMEM((4 * width, rows), jnp.bfloat16)
    high = width * (len(olds) + 1) + (old_products[0].shape[0] if old_products else 0)
    product = jax.ShapeDtypeStruct((high, 4 * width), jnp.float32)
    olds = [pltpu.with_memory_space_constraint(x, pltpu.VMEM) for old in olds for x in old]
    ins = [*parts, *olds, *old_products]
    vmem, smem = pl.BlockSpec(memory_space=pltpu.VMEM), pl.BlockSpec(memory_space=pltpu.SMEM)
    out = pl.pallas_call(
        functools.partial(
            chunk_kernel, before=len(olds) // 4, places=places, upper=bool(old_products)
        ),
        in_specs=[smem, smem] + [vmem] * len(ins),
        out_specs=[vmem] * (4 + len(places)),
        out_shape=[plain, plain, turned, turned] + [product] * len(places),
        compiler_params=pltpu.CompilerParams(vmem_limit_bytes=14 * MIB),
        cost_estimate=pl.CostEstimate(
            flops=24 * len(places) * high * width * rows, bytes_accessed=8_000_000, transcendentals=0
        ),
    )(bands, targets, *ins)
    return out[:4], list(out[4:])


def product_kernel(target_ref, *refs, place):
    out_ref = refs[-1]
    out_ref[...] = block_row(target_ref[place], [refs[k : k + 2] for k in range(2, len(refs) - 1, 2)], refs[:2])


def product(targets, place, chunks):
    rows, wide = chunks[-1][0].shape
    ins = [*chunks[-1][:2]] + [x for c in chunks for x in c[2:]]
    ins = [pltpu.with_memory_space_constraint(x, pltpu.VMEM) for x in ins]
    high = wide // 4 * len(chunks)
    vmem = pl.BlockSpec(memory_space=pltpu.VMEM)
    return pl.pallas_call(
        functools.partial(product_kernel, place=place),
        in_specs=[pl.BlockSpec(memory_space=pltpu.SMEM)] + [vmem] * len(ins),
        out_specs=vmem,
        out_shape=jax.ShapeDtypeStruct((high, wide), jnp.float32),
        compiler_params=pltpu.CompilerParams(vmem_limit_bytes=16 * MIB),
        cost_estimate=pl.CostEstimate(
            flops=6 * high * wide * rows, bytes_accessed=4_000_000, transcendentals=0
        ),
    )(targets, *ins)


def pick_kernel(goal_ref, *refs):
    ins, outs = refs[:4], refs[4:]
    width = ins[0].shape[1] // 4
    for k, out in enumerate(outs):
        there = pl.ds(pl.multiple_of(goal_ref[k] * width, width), width)
        x, y, u, v = (ref[:, there] for ref in ins)
        total = (x + y) + (u + v)
        out[...] = jnp.where(goal_ref[4] > 0, total, 0.0) if k == 3 else total


def pick(goals, parts):
    rows, size = parts[0].shape
    shape = jax.ShapeDtypeStruct((rows, size // 4), jnp.float32)
    vmem = pl.BlockSpec(memory_space=pltpu.VMEM)
    return pl.pallas_call(
        pick_kernel,
        in_specs=[pl.BlockSpec(memory_space=pltpu.SMEM)] + [vmem] * 4,
        out_specs=[vmem] * 4,
        out_shape=[shape] * 4,
        compiler_params=pltpu.CompilerParams(vmem_limit_bytes=8 * MIB),
        cost_estimate=pl.CostEstimate(flops=0, bytes_accessed=3_000_000, transcendentals=0),
    )(goals, *parts)


def assemble_kernel(core_ref, piece_ref, turn_e_ref, turn_l_ref, out_ref, *, scale):
    w = piece_ref.shape[1]
    first = jnp.concatenate([piece_ref[:w, :], turn_e_ref[...].T, turn_l_ref[:w, :].T], axis=0)
    second = jnp.concatenate([piece_ref[w : 3 * w, :], turn_l_ref[w:, :].T], axis=0)
    last = piece_ref[3 * w :, :]
    half = out_ref.shape[0]
    is_first = core_ref[0] == 0
    for k, x in enumerate((first, second, last)):
        out_ref[:, pl.ds(k * w, w)] = jnp.where(is_first, x[:half], x[half:]) * scale


def assemble(core, parts, order):
    w = parts[0].shape[1]
    vmem = pl.BlockSpec(memory_space=pltpu.VMEM)
    return pl.pallas_call(
        functools.partial(assemble_kernel, scale=1.0 / order),
        in_specs=[pl.BlockSpec(memory_space=pltpu.SMEM)] + [vmem] * len(parts),
        out_specs=vmem,
        out_shape=jax.ShapeDtypeStruct((3 * w // 2, 3 * w), jnp.float32),
        compiler_params=pltpu.CompilerParams(vmem_limit_bytes=12 * MIB),
        cost_estimate=pl.CostEstimate(flops=0, bytes_accessed=2_000_000, transcendentals=0),
    )(core, *parts).T


def linear(chip, core, z):
    return (chip * 2 + core) * 4 + z


def send(x, pairs):
    return lax.ppermute(x, ("orb", "band"), pairs)


def mirrored(pairs):
    out = []
    for chip in range(4):
        for a, b in pairs:
            out.append((linear(chip, 0, a), linear(chip, 0, b)))
            out.append((linear(chip, 1, 3 - a), linear(chip, 1, 3 - b)))
    return out


def gather_bands(x):
    return [x] + [send(x, mirrored([(source, 2)])) for source in (0, 1, 3)]


def over_chips(flip):
    return [
        (linear(chip, core, 2 - core), linear(chip ^ flip, core, 2 - core))
        for chip in range(4)
        for core in range(2)
    ]


FLIPS = (3, 1, 2, 0)
ALL = (0, 1, 2, 3)
EVERY = [(q, c, z) for q in range(4) for c in range(2) for z in range(4)]
SWAP = [(linear(q, c, z), linear(q, 1 - c, z)) for q, c, z in EVERY]
TURN = [(linear(q, c, z), linear(z, c, q)) for q, c, z in EVERY]
TURN_UP = [pair for pair in TURN if pair[0] // 4 % 2 == 1]


def simple_gram(filtered):
    partial_gram = jnp.dot(
        filtered.T,
        lax.all_gather(filtered, "band", axis=1, tiled=True),
        precision=lax.Precision.HIGH,
        preferred_element_type=jnp.float32,
    )
    return lax.psum_scatter(partial_gram, "orb", scatter_dimension=1, tiled=True)


def in_turn(hi, lo, old, order):
    core = (lax.axis_index("orb") & 1)[None]
    first = [apply_step(core, hi, lo, neighbours(x), x) for x in old]
    filtered = [apply_step(core, hi, lo, neighbours(x), x, v) for x, v in zip(first, old)]
    filtered = jnp.concatenate(filtered, axis=1)
    return filtered, simple_gram(filtered) / order


def index_tables():
    orb, z = lax.axis_index("orb"), lax.axis_index("band")
    chip, core = orb >> 1, orb & 1
    bands = jnp.stack([b + core * (3 - 2 * b) for b in (2, 0, 1, 3)])
    holder = (z == 2 - core).astype(jnp.int32)
    goals = jnp.stack([k + core * (3 - 2 * k) for k in (0, 1, 3)] + [z, holder])
    targets = jnp.stack([chip ^ flip for flip in FLIPS])
    return bands, goals, targets, core[None]


def by_symmetry(hi, lo, old, order, tables):
    bands, goals, targets, core = tables

    def one(x, halo, v=None, turned=False):
        return apply_step(core, hi, lo, halo, x, v, turned)

    v0, v1, v2 = old
    hv = [neighbours(x) for x in old]
    f0 = one(v0, hv[0])
    hf0 = neighbours(f0)
    f1 = one(v1, hv[1])
    hf1 = neighbours(f1)
    g0 = one(f0, hf0, v0)
    z0 = gather_bands(g0)
    f2 = one(after_that(v2, g0), hv[2])
    hf2 = neighbours(f2)
    e1 = apply_part(core, hi, lo, after_that(f1, g0, f2), hf1[0], late=False)
    g1 = apply_part(core, hi, lo, hf1[1], after_that(e1, *z0[1:]), v1, late=True)
    z1 = gather_bands(g1)
    e2 = apply_part(core, hi, lo, after_that(f2, g1), hf2[0], late=False)
    g2 = apply_part(core, hi, lo, hf2[1], e2, v2, late=True)
    z2 = gather_bands(g2)
    c0, upper = chunk(bands, targets, [after_that(z0[0], g2)] + z0[1:], [], ALL)
    c1, early = chunk(bands, targets, [after_that(z1[0], upper[0])] + z1[1:], [c0], ALL, upper)
    early = [send(x, over_chips(flip)) if flip else x for x, flip in zip(early, FLIPS)]
    c2, late = chunk(bands, targets, [after_that(z2[0], c1[0])] + z2[1:], [c0, c1], (0,))
    late.append(product(after_that(targets, late[0], early[1], early[2]), 1, [c0, c1, c2]))
    late.append(product(after_that(targets, late[1]), 2, [c0, c1, c2]))
    last = late[-1]
    late = [send(x, over_chips(flip)) for x, flip in zip(late, FLIPS)]

    def deliver(parts):
        moved = pick(goals, parts)
        return [moved[3]] + [send(x, mirrored([(2, k)])) for k, x in zip((0, 1, 3), moved)]

    arrived = [deliver([after_that(early[0], last)] + early[1:])]
    late.append(product(after_that(targets, arrived[0][0], late[0]), 3, [c0, c1, c2]))
    arrived.append(deliver(late))
    filtered = jnp.concatenate([g0, g1, after_that(g2, late[3])], axis=1)
    piece = jnp.concatenate([(x[0] + x[1]) + (x[2] + x[3]) for x in arrived], axis=0)
    piece = piece + send(piece, SWAP)
    w = v0.shape[1]
    turn_e = send(piece[w : 2 * w], TURN)
    turn_l = send(piece[3 * w : 5 * w], TURN_UP)
    return filtered, assemble(core, [piece, turn_e, turn_l], order)


def body(blocks, columns, counts, vectors, symmetric):
    rows, width = vectors.shape
    order = rows * lax.axis_size("orb")
    slot_of = slot_table(columns, counts)
    later = vectors
    if symmetric:
        tables = index_tables()
        slot_of, tables, later = lax.optimization_barrier((slot_of, tables, vectors))
    old = [
        (later if c else vectors)[:, c : min(c + LANES, width)] for c in range(0, width, LANES)
    ]
    hi, lo = densify(slot_of, blocks)
    if symmetric:
        return by_symmetry(hi, lo, old, order, tables)
    return in_turn(hi, lo, old, order)


def solution(mesh):
    placed = (P("orb", None, None, None), P("orb", None), P("orb"), P("orb", "band"))

    def whole(blocks, columns, counts, vectors):
        symmetric = (
            mesh.shape["orb"] == 8 and mesh.shape["band"] == 4 and vectors.shape[1] == 3 * LANES
        )
        return body(blocks, columns, counts, vectors, symmetric)

    return jax.shard_map(
        whole,
        mesh=mesh,
        in_specs=placed,
        out_specs=(P("orb", "band"), P("band", "orb")),
        check_vma=False,
    )
```

```python
import functools

import jax
import jax.numpy as jnp
from jax import lax
from jax.experimental import pallas as pl
from jax.experimental.pallas import tpu as pltpu
from jax.sharding import PartitionSpec as P

GROUP = 4
LANES = 128
MIB = 1024 * 1024
APPLY_MIB = 10


def split(x):
    hi = x.astype(jnp.bfloat16)
    lo = (x - hi.astype(jnp.float32)).astype(jnp.bfloat16)
    return hi, lo


def densify_kernel(slot_ref, blocks_ref, hi_ref, lo_ref, *, spread, reach):
    blk = blocks_ref.shape[2]
    step = pl.program_id(0)
    tile = (blk, 2 * blk)
    shift = lax.broadcasted_iota(jnp.int32, tile, 1) - lax.broadcasted_iota(jnp.int32, tile, 0)

    def one_row(i, carry):
        row = step * GROUP + i
        start = pl.multiple_of(i * blk, blk)
        for pair in range(spread // 2):
            left = slot_ref[row, 2 * pair]
            right = slot_ref[row, 2 * pair + 1]
            lblk = jnp.where(left >= 0, blocks_ref[i, jnp.maximum(left, 0)], 0.0)
            rblk = jnp.where(right >= 0, blocks_ref[i, jnp.maximum(right, 0)], 0.0)
            both = jnp.concatenate([lblk, rblk], axis=1)
            if reach <= 2 * pair + 1 and 2 * pair < reach + GROUP:
                both = both - jnp.where(shift == (reach + i - 2 * pair) * blk, 0.1, 0.0)
            hi, lo = split(both / 0.9)
            hi_ref[pl.ds(start, blk), pl.ds(pair * 2 * blk, 2 * blk)] = hi
            lo_ref[pl.ds(start, blk), pl.ds(pair * 2 * blk, 2 * blk)] = lo
        return carry

    lax.fori_loop(0, GROUP, one_row, 0)


def densify(slot_of, blocks):
    rows, slots, blk, _ = blocks.shape
    spread = slot_of.shape[1]
    shape = pltpu.VMEM((rows * blk, spread * blk), jnp.bfloat16)
    out = pl.BlockSpec((GROUP * blk, spread * blk), lambda g, _: (g, 0))
    return pl.pallas_call(
        functools.partial(densify_kernel, spread=spread, reach=rows),
        grid_spec=pltpu.PrefetchScalarGridSpec(
            num_scalar_prefetch=1,
            grid=(rows // GROUP,),
            in_specs=[pl.BlockSpec((GROUP, slots, blk, blk), lambda g, _: (g, 0, 0, 0))],
            out_specs=[out, out],
        ),
        out_shape=[shape, shape],
        compiler_params=pltpu.CompilerParams(vmem_limit_bytes=20 * MIB),
        cost_estimate=pl.CostEstimate(flops=0, bytes_accessed=60_000_000, transcendentals=0),
    )(slot_of, blocks)


def apply_kernel(core_ref, hi_ref, lo_ref, near_ref, far_ref, own_ref, *rest, second, turned):
    inside_ref, across_ref = (far_ref, near_ref) if turned else (near_ref, far_ref)
    old_ref = rest[0] if second else None
    out_ref, parts = rest[-2:]
    rows, width = own_ref.shape
    wide = hi_ref.shape[1]
    tall = wide - 2 * rows
    core = core_ref[0]
    for place, ref in ((1, own_ref), (2 - 2 * core, inside_ref), (2 * core, across_ref)):
        there = pl.ds(pl.multiple_of(place * rows, rows), rows)
        parts[there, pl.ds(0, width)], parts[there, pl.ds(width, width)] = split(ref[...])

    def one_group(step, carry):
        start = pl.multiple_of(step * tall, tall)
        here = pl.ds(start, tall)
        reached = pl.ds(start, wide)
        both = jnp.dot(hi_ref[here, :], parts[reached, :], preferred_element_type=jnp.float32)
        other = jnp.dot(
            lo_ref[here, :], parts[reached, pl.ds(0, width)], preferred_element_type=jnp.float32
        )
        product = both[:, :width] + (both[:, width:] + other)
        if second:
            product = 2.0 * product - old_ref[here, :]
        out_ref[here, :] = product
        return carry

    lax.fori_loop(0, rows // tall, one_group, 0)


def apply_step(core, hi, lo, halo, own, old=None, turned=False):
    rows, width = own.shape
    wide = hi.shape[1]
    second = old is not None
    hi, lo = (pltpu.with_memory_space_constraint(x, pltpu.VMEM) for x in (hi, lo))
    vmem = pl.BlockSpec(memory_space=pltpu.VMEM)
    return pl.pallas_call(
        functools.partial(apply_kernel, second=second, turned=turned),
        in_specs=[pl.BlockSpec(memory_space=pltpu.SMEM)] + [vmem] * (6 if second else 5),
        out_specs=vmem,
        out_shape=jax.ShapeDtypeStruct((rows, width), jnp.float32),
        scratch_shapes=[pltpu.VMEM((3 * rows, 2 * width), jnp.bfloat16)],
        compiler_params=pltpu.CompilerParams(vmem_limit_bytes=APPLY_MIB * MIB),
        cost_estimate=pl.CostEstimate(
            flops=8 * rows * wide * width, bytes_accessed=4 * rows * wide, transcendentals=0
        ),
    )(core, hi, lo, *(halo[::-1] if turned else halo), own, *([old] if second else []))


def part_kernel(core_ref, hi_ref, lo_ref, *refs, late):
    out_ref, parts = refs[-2:]
    blocks = refs[:1] if late else refs[:2]
    rows, width = blocks[0].shape
    wide = hi_ref.shape[1]
    tall = wide - 2 * rows
    core = core_ref[0]
    for k, ref in enumerate(blocks):
        place = 0 if late else (core if k == 0 else 1 - core)
        there = pl.ds(pl.multiple_of(place * rows, rows), rows)
        parts[there, pl.ds(0, width)], parts[there, pl.ds(width, width)] = split(ref[...])
    for which in range(2):

        @pl.when(core == which)
        def _():
            for step in range(rows // tall):
                start = step * tall
                low, high = (rows, 3 * rows) if which == 0 else (0, 2 * rows)
                if late:
                    low, high = (0, rows) if which == 0 else (2 * rows, 3 * rows)
                first, last = max(low, start), min(high, start + wide)
                size, column, row = last - first, first - start, first - low
                here = pl.ds(start, tall)
                reached = pl.ds(row, size)
                both = jnp.dot(
                    hi_ref[here, pl.ds(column, size)],
                    parts[reached, :],
                    preferred_element_type=jnp.float32,
                )
                other = jnp.dot(
                    lo_ref[here, pl.ds(column, size)],
                    parts[reached, pl.ds(0, width)],
                    preferred_element_type=jnp.float32,
                )
                product = both[:, :width] + (both[:, width:] + other)
                if late:
                    product = 2.0 * (refs[1][here, :] + product) - refs[2][here, :]
                out_ref[here, :] = product


def apply_part(core, hi, lo, *ins, late):
    rows, width = ins[0].shape
    hi, lo = (pltpu.with_memory_space_constraint(x, pltpu.VMEM) for x in (hi, lo))
    vmem = pl.BlockSpec(memory_space=pltpu.VMEM)
    return pl.pallas_call(
        functools.partial(part_kernel, late=late),
        in_specs=[pl.BlockSpec(memory_space=pltpu.SMEM)] + [vmem] * (2 + len(ins)),
        out_specs=vmem,
        out_shape=jax.ShapeDtypeStruct((rows, width), jnp.float32),
        scratch_shapes=[pltpu.VMEM(((1 if late else 2) * rows, 2 * width), jnp.bfloat16)],
        compiler_params=pltpu.CompilerParams(vmem_limit_bytes=APPLY_MIB * MIB),
        cost_estimate=pl.CostEstimate(
            flops=(2 if late else 6) * rows * hi.shape[1] * width,
            bytes_accessed=4 * rows * hi.shape[1],
            transcendentals=0,
        ),
    )(core, hi, lo, *ins)


def slot_table(columns, counts):
    rows, slots = columns.shape
    total = rows * lax.axis_size("orb")
    spread = GROUP + 2 * rows
    ids = jnp.arange(rows, dtype=jnp.int32)
    offset = lax.axis_index("orb") * rows - rows
    place = (columns - offset) % total - (ids // GROUP * GROUP)[:, None]
    number = jnp.arange(slots, dtype=jnp.int32)
    place = jnp.where(number[None, :] < counts[:, None], place, -1)
    hit = place[:, :, None] == jnp.arange(spread, dtype=jnp.int32)[None, None, :]
    return jnp.max(jnp.where(hit, number[None, :, None], -1), axis=1)


def neighbours(x):
    size = lax.axis_size("orb")
    inside = [(i, i ^ 1) for i in range(size)]
    across = [(i, (i + 1 if i % 2 else i - 1) % size) for i in range(size)]
    return lax.ppermute(x, "orb", inside), lax.ppermute(x, "orb", across)


def after_that(x, *done):
    return lax.optimization_barrier((x, done))[0]


def store_parts(band_ref, ins, outs):
    hi_ref, lo_ref, thi_ref, tlo_ref = outs
    for place, ref in enumerate(ins):
        x = ref[...]
        width = x.shape[1]
        there = pl.ds(pl.multiple_of(band_ref[place] * width, width), width)
        hi_ref[:, there], lo_ref[:, there] = split(x)
        thi_ref[there, :], tlo_ref[there, :] = split(x.T)


def block_row(target, turned, right):
    rows = turned[0][0].shape[0] // 4
    there = pl.ds(pl.multiple_of(target * rows, rows), rows)
    thi = jnp.concatenate([hi[there, :] for hi, lo in turned], axis=0)
    tlo = jnp.concatenate([lo[there, :] for hi, lo in turned], axis=0)
    hi_ref, lo_ref = right
    total = jnp.dot(thi, lo_ref[...], preferred_element_type=jnp.float32)
    total += jnp.dot(tlo, hi_ref[...], preferred_element_type=jnp.float32)
    return total + jnp.dot(thi, hi_ref[...], preferred_element_type=jnp.float32)


def chunk_kernel(band_ref, target_ref, *refs, before, places, upper):
    ins, refs = refs[:4], refs[4:]
    olds, refs = [refs[4 * k : 4 * k + 4] for k in range(before)], refs[4 * before :]
    old_products, refs = (refs[: len(places)], refs[len(places) :]) if upper else ((), refs)
    new, outs = refs[:4], refs[4:]
    store_parts(band_ref, ins, new)
    turned = [x[2:] for x in olds] + [new[2:]]
    for k, place in enumerate(places):
        total = block_row(target_ref[place], turned, new[:2])
        if upper:
            high = old_products[k].shape[0]
            outs[k][pl.ds(0, high), :] = old_products[k][...]
            outs[k][pl.ds(high, total.shape[0]), :] = total
        else:
            outs[k][...] = total


def chunk(bands, targets, parts, olds, places, old_products=()):
    rows, width = parts[0].shape
    plain = pltpu.VMEM((rows, 4 * width), jnp.bfloat16)
    turned = pltpu.VMEM((4 * width, rows), jnp.bfloat16)
    high = width * (len(olds) + 1) + (old_products[0].shape[0] if old_products else 0)
    product = jax.ShapeDtypeStruct((high, 4 * width), jnp.float32)
    olds = [pltpu.with_memory_space_constraint(x, pltpu.VMEM) for old in olds for x in old]
    ins = [*parts, *olds, *old_products]
    vmem, smem = pl.BlockSpec(memory_space=pltpu.VMEM), pl.BlockSpec(memory_space=pltpu.SMEM)
    out = pl.pallas_call(
        functools.partial(
            chunk_kernel, before=len(olds) // 4, places=places, upper=bool(old_products)
        ),
        in_specs=[smem, smem] + [vmem] * len(ins),
        out_specs=[vmem] * (4 + len(places)),
        out_shape=[plain, plain, turned, turned] + [product] * len(places),
        compiler_params=pltpu.CompilerParams(vmem_limit_bytes=14 * MIB),
        cost_estimate=pl.CostEstimate(
            flops=24 * len(places) * high * width * rows, bytes_accessed=8_000_000, transcendentals=0
        ),
    )(bands, targets, *ins)
    return out[:4], list(out[4:])


def product_kernel(target_ref, *refs, place):
    out_ref = refs[-1]
    out_ref[...] = block_row(target_ref[place], [refs[k : k + 2] for k in range(2, len(refs) - 1, 2)], refs[:2])


def product(targets, place, chunks):
    rows, wide = chunks[-1][0].shape
    ins = [*chunks[-1][:2]] + [x for c in chunks for x in c[2:]]
    ins = [pltpu.with_memory_space_constraint(x, pltpu.VMEM) for x in ins]
    high = wide // 4 * len(chunks)
    vmem = pl.BlockSpec(memory_space=pltpu.VMEM)
    return pl.pallas_call(
        functools.partial(product_kernel, place=place),
        in_specs=[pl.BlockSpec(memory_space=pltpu.SMEM)] + [vmem] * len(ins),
        out_specs=vmem,
        out_shape=jax.ShapeDtypeStruct((high, wide), jnp.float32),
        compiler_params=pltpu.CompilerParams(vmem_limit_bytes=16 * MIB),
        cost_estimate=pl.CostEstimate(
            flops=6 * high * wide * rows, bytes_accessed=4_000_000, transcendentals=0
        ),
    )(targets, *ins)


def pick_kernel(goal_ref, *refs):
    ins, outs = refs[:4], refs[4:]
    width = ins[0].shape[1] // 4
    for k, out in enumerate(outs):
        there = pl.ds(pl.multiple_of(goal_ref[k] * width, width), width)
        x, y, u, v = (ref[:, there] for ref in ins)
        total = (x + y) + (u + v)
        out[...] = jnp.where(goal_ref[4] > 0, total, 0.0) if k == 3 else total


def pick(goals, parts):
    rows, size = parts[0].shape
    shape = jax.ShapeDtypeStruct((rows, size // 4), jnp.float32)
    vmem = pl.BlockSpec(memory_space=pltpu.VMEM)
    return pl.pallas_call(
        pick_kernel,
        in_specs=[pl.BlockSpec(memory_space=pltpu.SMEM)] + [vmem] * 4,
        out_specs=[vmem] * 4,
        out_shape=[shape] * 4,
        compiler_params=pltpu.CompilerParams(vmem_limit_bytes=8 * MIB),
        cost_estimate=pl.CostEstimate(flops=0, bytes_accessed=3_000_000, transcendentals=0),
    )(goals, *parts)


def assemble_kernel(core_ref, piece_ref, turn_e_ref, turn_l_ref, out_ref, *, scale):
    w = piece_ref.shape[1]
    first = jnp.concatenate([piece_ref[:w, :], turn_e_ref[...].T, turn_l_ref[:w, :].T], axis=0)
    second = jnp.concatenate([piece_ref[w : 3 * w, :], turn_l_ref[w:, :].T], axis=0)
    last = piece_ref[3 * w :, :]
    half = out_ref.shape[0]
    is_first = core_ref[0] == 0
    for k, x in enumerate((first, second, last)):
        out_ref[:, pl.ds(k * w, w)] = jnp.where(is_first, x[:half], x[half:]) * scale


def assemble(core, parts, order):
    w = parts[0].shape[1]
    vmem = pl.BlockSpec(memory_space=pltpu.VMEM)
    return pl.pallas_call(
        functools.partial(assemble_kernel, scale=1.0 / order),
        in_specs=[pl.BlockSpec(memory_space=pltpu.SMEM)] + [vmem] * len(parts),
        out_specs=vmem,
        out_shape=jax.ShapeDtypeStruct((3 * w // 2, 3 * w), jnp.float32),
        compiler_params=pltpu.CompilerParams(vmem_limit_bytes=12 * MIB),
        cost_estimate=pl.CostEstimate(flops=0, bytes_accessed=2_000_000, transcendentals=0),
    )(core, *parts).T


def linear(chip, core, z):
    return (chip * 2 + core) * 4 + z


def send(x, pairs):
    return lax.ppermute(x, ("orb", "band"), pairs)


def mirrored(pairs):
    out = []
    for chip in range(4):
        for a, b in pairs:
            out.append((linear(chip, 0, a), linear(chip, 0, b)))
            out.append((linear(chip, 1, 3 - a), linear(chip, 1, 3 - b)))
    return out


def gather_bands(x):
    return [x] + [send(x, mirrored([(source, 2)])) for source in (0, 1, 3)]


def over_chips(flip):
    return [
        (linear(chip, core, 2 - core), linear(chip ^ flip, core, 2 - core))
        for chip in range(4)
        for core in range(2)
    ]


FLIPS = (3, 1, 2, 0)
ALL = (0, 1, 2, 3)
EVERY = [(q, c, z) for q in range(4) for c in range(2) for z in range(4)]
SWAP = [(linear(q, c, z), linear(q, 1 - c, z)) for q, c, z in EVERY]
TURN = [(linear(q, c, z), linear(z, c, q)) for q, c, z in EVERY]
TURN_UP = [pair for pair in TURN if pair[0] // 4 % 2 == 1]


def simple_gram(filtered):
    partial_gram = jnp.dot(
        filtered.T,
        lax.all_gather(filtered, "band", axis=1, tiled=True),
        precision=lax.Precision.HIGH,
        preferred_element_type=jnp.float32,
    )
    return lax.psum_scatter(partial_gram, "orb", scatter_dimension=1, tiled=True)


def in_turn(hi, lo, old, order):
    core = (lax.axis_index("orb") & 1)[None]
    first = [apply_step(core, hi, lo, neighbours(x), x) for x in old]
    filtered = [apply_step(core, hi, lo, neighbours(x), x, v) for x, v in zip(first, old)]
    filtered = jnp.concatenate(filtered, axis=1)
    return filtered, simple_gram(filtered) / order


def index_tables():
    orb, z = lax.axis_index("orb"), lax.axis_index("band")
    chip, core = orb >> 1, orb & 1
    bands = jnp.stack([b + core * (3 - 2 * b) for b in (2, 0, 1, 3)])
    holder = (z == 2 - core).astype(jnp.int32)
    goals = jnp.stack([k + core * (3 - 2 * k) for k in (0, 1, 3)] + [z, holder])
    targets = jnp.stack([chip ^ flip for flip in FLIPS])
    return bands, goals, targets, core[None]


def by_symmetry(hi, lo, old, order, tables):
    bands, goals, targets, core = tables

    def one(x, halo, v=None, turned=False):
        return apply_step(core, hi, lo, halo, x, v, turned)

    v0, v1, v2 = old
    hv = [neighbours(x) for x in old]
    f0 = one(v0, hv[0])
    hf0 = neighbours(f0)
    f1 = one(v1, hv[1])
    hf1 = neighbours(f1)
    g0 = one(f0, hf0, v0)
    z0 = gather_bands(g0)
    f2 = one(after_that(v2, g0), hv[2])
    hf2 = neighbours(f2)
    e1 = apply_part(core, hi, lo, after_that(f1, g0, f2), hf1[0], late=False)
    g1 = apply_part(core, hi, lo, hf1[1], after_that(e1, *z0[1:]), v1, late=True)
    z1 = gather_bands(g1)
    e2 = apply_part(core, hi, lo, after_that(f2, g1), hf2[0], late=False)
    g2 = apply_part(core, hi, lo, hf2[1], e2, v2, late=True)
    z2 = gather_bands(g2)
    c0, upper = chunk(bands, targets, [after_that(z0[0], g2)] + z0[1:], [], ALL)
    c1, early = chunk(bands, targets, [after_that(z1[0], upper[0])] + z1[1:], [c0], ALL, upper)
    early = [send(x, over_chips(flip)) if flip else x for x, flip in zip(early, FLIPS)]
    c2, late = chunk(bands, targets, [after_that(z2[0], c1[0])] + z2[1:], [c0, c1], (0,))
    late.append(product(after_that(targets, late[0], early[1]), 1, [c0, c1, c2]))
    late.append(product(after_that(targets, late[1]), 2, [c0, c1, c2]))
    last = late[-1]
    late = [send(x, over_chips(flip)) for x, flip in zip(late, FLIPS)]

    def deliver(parts):
        moved = pick(goals, parts)
        return [moved[3]] + [send(x, mirrored([(2, k)])) for k, x in zip((0, 1, 3), moved)]

    arrived = [deliver([after_that(early[0], last)] + early[1:])]
    late.append(product(after_that(targets, arrived[0][0], late[0]), 3, [c0, c1, c2]))
    arrived.append(deliver(late))
    filtered = jnp.concatenate([g0, g1, after_that(g2, late[3])], axis=1)
    piece = jnp.concatenate([(x[0] + x[1]) + (x[2] + x[3]) for x in arrived], axis=0)
    piece = piece + send(piece, SWAP)
    w = v0.shape[1]
    turn_e = send(piece[w : 2 * w], TURN)
    turn_l = send(piece[3 * w : 5 * w], TURN_UP)
    return filtered, assemble(core, [piece, turn_e, turn_l], order)


def body(blocks, columns, counts, vectors, symmetric):
    rows, width = vectors.shape
    order = rows * lax.axis_size("orb")
    slot_of = slot_table(columns, counts)
    later = vectors
    if symmetric:
        tables = index_tables()
        slot_of, tables, later = lax.optimization_barrier((slot_of, tables, vectors))
    old = [
        (later if c else vectors)[:, c : min(c + LANES, width)] for c in range(0, width, LANES)
    ]
    hi, lo = densify(slot_of, blocks)
    if symmetric:
        return by_symmetry(hi, lo, old, order, tables)
    return in_turn(hi, lo, old, order)


def solution(mesh):
    placed = (P("orb", None, None, None), P("orb", None), P("orb"), P("orb", "band"))

    def whole(blocks, columns, counts, vectors):
        symmetric = (
            mesh.shape["orb"] == 8 and mesh.shape["band"] == 4 and vectors.shape[1] == 3 * LANES
        )
        return body(blocks, columns, counts, vectors, symmetric)

    return jax.shard_map(
        whole,
        mesh=mesh,
        in_specs=placed,
        out_specs=(P("orb", "band"), P("band", "orb")),
        check_vma=False,
    )
```

```python
import functools

import jax
import jax.numpy as jnp
from jax import lax
from jax.experimental import pallas as pl
from jax.experimental.pallas import tpu as pltpu
from jax.sharding import PartitionSpec as P

GROUP = 4
LANES = 128
MIB = 1024 * 1024
APPLY_MIB = 10


def split(x):
    hi = x.astype(jnp.bfloat16)
    lo = (x - hi.astype(jnp.float32)).astype(jnp.bfloat16)
    return hi, lo


def densify_kernel(slot_ref, blocks_ref, hi_ref, lo_ref, *, spread, reach):
    blk = blocks_ref.shape[2]
    step = pl.program_id(0)
    tile = (blk, 2 * blk)
    shift = lax.broadcasted_iota(jnp.int32, tile, 1) - lax.broadcasted_iota(jnp.int32, tile, 0)

    def one_row(i, carry):
        row = step * GROUP + i
        start = pl.multiple_of(i * blk, blk)
        for pair in range(spread // 2):
            left = slot_ref[row, 2 * pair]
            right = slot_ref[row, 2 * pair + 1]
            lblk = jnp.where(left >= 0, blocks_ref[i, jnp.maximum(left, 0)], 0.0)
            rblk = jnp.where(right >= 0, blocks_ref[i, jnp.maximum(right, 0)], 0.0)
            both = jnp.concatenate([lblk, rblk], axis=1)
            if reach <= 2 * pair + 1 and 2 * pair < reach + GROUP:
                both = both - jnp.where(shift == (reach + i - 2 * pair) * blk, 0.1, 0.0)
            hi, lo = split(both / 0.9)
            hi_ref[pl.ds(start, blk), pl.ds(pair * 2 * blk, 2 * blk)] = hi
            lo_ref[pl.ds(start, blk), pl.ds(pair * 2 * blk, 2 * blk)] = lo
        return carry

    lax.fori_loop(0, GROUP, one_row, 0)


def densify(slot_of, blocks):
    rows, slots, blk, _ = blocks.shape
    spread = slot_of.shape[1]
    shape = pltpu.VMEM((rows * blk, spread * blk), jnp.bfloat16)
    out = pl.BlockSpec((GROUP * blk, spread * blk), lambda g, _: (g, 0))
    return pl.pallas_call(
        functools.partial(densify_kernel, spread=spread, reach=rows),
        grid_spec=pltpu.PrefetchScalarGridSpec(
            num_scalar_prefetch=1,
            grid=(rows // GROUP,),
            in_specs=[pl.BlockSpec((GROUP, slots, blk, blk), lambda g, _: (g, 0, 0, 0))],
            out_specs=[out, out],
        ),
        out_shape=[shape, shape],
        compiler_params=pltpu.CompilerParams(vmem_limit_bytes=20 * MIB),
        cost_estimate=pl.CostEstimate(flops=0, bytes_accessed=60_000_000, transcendentals=0),
    )(slot_of, blocks)


def apply_kernel(core_ref, hi_ref, lo_ref, near_ref, far_ref, own_ref, *rest, second, turned):
    inside_ref, across_ref = (far_ref, near_ref) if turned else (near_ref, far_ref)
    old_ref = rest[0] if second else None
    out_ref, parts = rest[-2:]
    rows, width = own_ref.shape
    wide = hi_ref.shape[1]
    tall = wide - 2 * rows
    core = core_ref[0]
    for place, ref in ((1, own_ref), (2 - 2 * core, inside_ref), (2 * core, across_ref)):
        there = pl.ds(pl.multiple_of(place * rows, rows), rows)
        parts[there, pl.ds(0, width)], parts[there, pl.ds(width, width)] = split(ref[...])

    def one_group(step, carry):
        start = pl.multiple_of(step * tall, tall)
        here = pl.ds(start, tall)
        reached = pl.ds(start, wide)
        both = jnp.dot(hi_ref[here, :], parts[reached, :], preferred_element_type=jnp.float32)
        other = jnp.dot(
            lo_ref[here, :], parts[reached, pl.ds(0, width)], preferred_element_type=jnp.float32
        )
        product = both[:, :width] + (both[:, width:] + other)
        if second:
            product = 2.0 * product - old_ref[here, :]
        out_ref[here, :] = product
        return carry

    lax.fori_loop(0, rows // tall, one_group, 0)


def apply_step(core, hi, lo, halo, own, old=None, turned=False):
    rows, width = own.shape
    wide = hi.shape[1]
    second = old is not None
    hi, lo = (pltpu.with_memory_space_constraint(x, pltpu.VMEM) for x in (hi, lo))
    vmem = pl.BlockSpec(memory_space=pltpu.VMEM)
    return pl.pallas_call(
        functools.partial(apply_kernel, second=second, turned=turned),
        in_specs=[pl.BlockSpec(memory_space=pltpu.SMEM)] + [vmem] * (6 if second else 5),
        out_specs=vmem,
        out_shape=jax.ShapeDtypeStruct((rows, width), jnp.float32),
        scratch_shapes=[pltpu.VMEM((3 * rows, 2 * width), jnp.bfloat16)],
        compiler_params=pltpu.CompilerParams(vmem_limit_bytes=APPLY_MIB * MIB),
        cost_estimate=pl.CostEstimate(
            flops=8 * rows * wide * width, bytes_accessed=4 * rows * wide, transcendentals=0
        ),
    )(core, hi, lo, *(halo[::-1] if turned else halo), own, *([old] if second else []))


def part_kernel(core_ref, hi_ref, lo_ref, *refs, late):
    out_ref, parts = refs[-2:]
    rows, width = refs[0].shape
    wide = hi_ref.shape[1]
    tall = wide - 2 * rows
    core = core_ref[0]
    places = (core,) if late else (1, 2 - 2 * core)
    for place, ref in zip(places, refs):
        there = pl.ds(pl.multiple_of(place * rows, rows), rows)
        parts[there, pl.ds(0, width)], parts[there, pl.ds(width, width)] = split(ref[...])
    empty = 1 - core if late else 2 * core
    parts[pl.ds(pl.multiple_of(empty * rows, rows), rows), :] = jnp.zeros((rows, 2 * width), jnp.bfloat16)
    size = rows if late else wide - tall
    column = core * (wide - rows) if late else (1 - core) * tall
    shift = core * tall if late else (1 - core) * tall

    def one_group(step, carry):
        here = pl.ds(pl.multiple_of(step * tall, tall), tall)
        reached = pl.ds(pl.multiple_of(step * tall + shift, tall), size)
        columns = pl.ds(pl.multiple_of(column, tall), size)
        both = jnp.dot(hi_ref[here, columns], parts[reached, :], preferred_element_type=jnp.float32)
        other = jnp.dot(
            lo_ref[here, columns], parts[reached, pl.ds(0, width)], preferred_element_type=jnp.float32
        )
        product = both[:, :width] + (both[:, width:] + other)
        if late:
            product = 2.0 * (refs[1][here, :] + product) - refs[2][here, :]
        out_ref[here, :] = product
        return carry

    lax.fori_loop(0, rows // tall, one_group, 0)


def apply_part(core, hi, lo, *ins, late):
    rows, width = ins[0].shape
    hi, lo = (pltpu.with_memory_space_constraint(x, pltpu.VMEM) for x in (hi, lo))
    vmem = pl.BlockSpec(memory_space=pltpu.VMEM)
    return pl.pallas_call(
        functools.partial(part_kernel, late=late),
        in_specs=[pl.BlockSpec(memory_space=pltpu.SMEM)] + [vmem] * (2 + len(ins)),
        out_specs=vmem,
        out_shape=jax.ShapeDtypeStruct((rows, width), jnp.float32),
        scratch_shapes=[pltpu.VMEM(((2 if late else 3) * rows, 2 * width), jnp.bfloat16)],
        compiler_params=pltpu.CompilerParams(vmem_limit_bytes=APPLY_MIB * MIB),
        cost_estimate=pl.CostEstimate(
            flops=(2 if late else 6) * rows * hi.shape[1] * width,
            bytes_accessed=4 * rows * hi.shape[1],
            transcendentals=0,
        ),
    )(core, hi, lo, *ins)


def slot_table(columns, counts):
    rows, slots = columns.shape
    total = rows * lax.axis_size("orb")
    spread = GROUP + 2 * rows
    ids = jnp.arange(rows, dtype=jnp.int32)
    offset = lax.axis_index("orb") * rows - rows
    place = (columns - offset) % total - (ids // GROUP * GROUP)[:, None]
    number = jnp.arange(slots, dtype=jnp.int32)
    place = jnp.where(number[None, :] < counts[:, None], place, -1)
    hit = place[:, :, None] == jnp.arange(spread, dtype=jnp.int32)[None, None, :]
    return jnp.max(jnp.where(hit, number[None, :, None], -1), axis=1)


def neighbours(x):
    size = lax.axis_size("orb")
    inside = [(i, i ^ 1) for i in range(size)]
    across = [(i, (i + 1 if i % 2 else i - 1) % size) for i in range(size)]
    return lax.ppermute(x, "orb", inside), lax.ppermute(x, "orb", across)


def after_that(x, *done):
    return lax.optimization_barrier((x, done))[0]


def store_parts(band_ref, ins, outs):
    hi_ref, lo_ref, thi_ref, tlo_ref = outs
    for place, ref in enumerate(ins):
        x = ref[...]
        width = x.shape[1]
        there = pl.ds(pl.multiple_of(band_ref[place] * width, width), width)
        hi_ref[:, there], lo_ref[:, there] = split(x)
        thi_ref[there, :], tlo_ref[there, :] = split(x.T)


def block_row(target, turned, right, part):
    rows = turned[0][0].shape[0] // 4
    there = pl.ds(pl.multiple_of(target * rows, rows), rows)
    thi = jnp.concatenate([hi[there, :] for hi, lo in turned], axis=0)
    tlo = jnp.concatenate([lo[there, :] for hi, lo in turned], axis=0)
    if part is not None:
        half = thi.shape[0] // 2
        thi, tlo = (x[part * half : (part + 1) * half] for x in (thi, tlo))
    hi_ref, lo_ref = right
    total = jnp.dot(thi, lo_ref[...], preferred_element_type=jnp.float32)
    total += jnp.dot(tlo, hi_ref[...], preferred_element_type=jnp.float32)
    return total + jnp.dot(thi, hi_ref[...], preferred_element_type=jnp.float32)


def rows_of(target_ref, turned, right, outs, plan, old_products=()):
    for place, parts in plan:
        wanted = [part for part, _, _ in parts]
        if old_products:
            total = block_row(target_ref[place], turned, right, None)
            total = jnp.concatenate([old_products[place][...], total], axis=0)
        else:
            total = block_row(target_ref[place], turned, right, wanted[0] if len(wanted) == 1 else None)
        half = total.shape[0] // 2
        for part, out, slot in parts:
            if old_products or len(wanted) == 2:
                outs[out][slot] = total[part * half : (part + 1) * half]
            else:
                outs[out][slot] = total


def chunk_kernel(band_ref, target_ref, *refs, before, upper, plan):
    ins, refs = refs[:4], refs[4:]
    olds, refs = [refs[4 * k : 4 * k + 4] for k in range(before)], refs[4 * before :]
    old_products, refs = (refs[:4], refs[4:]) if upper else ((), refs)
    new, outs = refs[:4], refs[4:]
    store_parts(band_ref, ins, new)
    turned = [x[2:] for x in olds] + [new[2:]]
    if plan is None:
        for place, out in enumerate(outs):
            out[...] = block_row(target_ref[place], turned, new[:2], None)
    else:
        rows_of(target_ref, turned, new[:2], outs, plan, old_products)


def chunk(bands, targets, parts, olds, plan=None, old_products=()):
    rows, width = parts[0].shape
    plain = pltpu.VMEM((rows, 4 * width), jnp.bfloat16)
    turned = pltpu.VMEM((4 * width, rows), jnp.bfloat16)
    high = width * (len(olds) + 1) + (old_products[0].shape[0] if old_products else 0)
    count = 4 if plan is None else 1 + max(out for _, x in plan for _, out, _ in x)
    shape = (high, 4 * width) if plan is None else (2, high // 2, 4 * width)
    product = jax.ShapeDtypeStruct(shape, jnp.float32)
    olds = [pltpu.with_memory_space_constraint(x, pltpu.VMEM) for old in olds for x in old]
    ins = [*parts, *olds, *old_products]
    vmem, smem = pl.BlockSpec(memory_space=pltpu.VMEM), pl.BlockSpec(memory_space=pltpu.SMEM)
    out = pl.pallas_call(
        functools.partial(chunk_kernel, before=len(olds) // 4, upper=bool(old_products), plan=plan),
        in_specs=[smem, smem] + [vmem] * len(ins),
        out_specs=[vmem] * (4 + count),
        out_shape=[plain, plain, turned, turned] + [product] * count,
        compiler_params=pltpu.CompilerParams(vmem_limit_bytes=14 * MIB),
        cost_estimate=pl.CostEstimate(
            flops=96 * high * width * rows, bytes_accessed=8_000_000, transcendentals=0
        ),
    )(bands, targets, *ins)
    return out[:4], list(out[4:])


def product_kernel(target_ref, *refs, plan):
    ins, outs = refs[:-2], refs[-2:]
    rows_of(target_ref, [ins[k : k + 2] for k in range(2, len(ins), 2)], ins[:2], outs, plan)


def product(targets, chunks, plan):
    rows, wide = chunks[-1][0].shape
    ins = [*chunks[-1][:2]] + [x for c in chunks for x in c[2:]]
    ins = [pltpu.with_memory_space_constraint(x, pltpu.VMEM) for x in ins]
    high = wide // 4 * len(chunks)
    vmem = pl.BlockSpec(memory_space=pltpu.VMEM)
    return pl.pallas_call(
        functools.partial(product_kernel, plan=plan),
        in_specs=[pl.BlockSpec(memory_space=pltpu.SMEM)] + [vmem] * len(ins),
        out_specs=[vmem] * 2,
        out_shape=[jax.ShapeDtypeStruct((2, high // 2, wide), jnp.float32)] * 2,
        compiler_params=pltpu.CompilerParams(vmem_limit_bytes=16 * MIB),
        cost_estimate=pl.CostEstimate(
            flops=12 * high * wide * rows, bytes_accessed=4_000_000, transcendentals=0
        ),
    )(targets, *ins)


def middle_kernel(got_a, got_b, ours_a, ours_b, send_a, keep_a, send_b, keep_b):
    for got, ours, send_ref, keep in ((got_a, ours_a, send_a, keep_a), (got_b, ours_b, send_b, keep_b)):
        keep[...] = got[0] + ours[0]
        send_ref[...] = got[1] + ours[1]


def middle(*parts):
    shape = jax.ShapeDtypeStruct(parts[0].shape[1:], jnp.float32)
    vmem = pl.BlockSpec(memory_space=pltpu.VMEM)
    return pl.pallas_call(
        middle_kernel,
        in_specs=[vmem] * 4,
        out_specs=[vmem] * 4,
        out_shape=[shape] * 4,
        compiler_params=pltpu.CompilerParams(vmem_limit_bytes=8 * MIB),
        cost_estimate=pl.CostEstimate(flops=0, bytes_accessed=5_000_000, transcendentals=0),
    )(*parts)


def pick_kernel(goal_ref, *refs):
    ins, outs = refs[:4], refs[4:]
    width = ins[0].shape[1] // 4
    for k, out in enumerate(outs):
        there = pl.ds(pl.multiple_of(goal_ref[k] * width, width), width)
        x, y, u, v = (ref[:, there] for ref in ins)
        total = jnp.concatenate([x + y, u + v], axis=0)
        out[...] = jnp.where(goal_ref[4] > 0, total, 0.0) if k == 3 else total


def pick(goals, parts):
    rows, size = parts[0].shape
    shape = jax.ShapeDtypeStruct((2 * rows, size // 4), jnp.float32)
    vmem = pl.BlockSpec(memory_space=pltpu.VMEM)
    return pl.pallas_call(
        pick_kernel,
        in_specs=[pl.BlockSpec(memory_space=pltpu.SMEM)] + [vmem] * 4,
        out_specs=[vmem] * 4,
        out_shape=[shape] * 4,
        compiler_params=pltpu.CompilerParams(vmem_limit_bytes=8 * MIB),
        cost_estimate=pl.CostEstimate(flops=0, bytes_accessed=3_000_000, transcendentals=0),
    )(goals, *parts)


def assemble_kernel(core_ref, piece_ref, turn_e_ref, turn_l_ref, out_ref, *, scale):
    w = piece_ref.shape[1]
    first = jnp.concatenate([piece_ref[:w, :], turn_e_ref[...].T, turn_l_ref[:w, :].T], axis=0)
    second = jnp.concatenate([piece_ref[w : 3 * w, :], turn_l_ref[w:, :].T], axis=0)
    last = piece_ref[3 * w :, :]
    half = out_ref.shape[0]
    is_first = core_ref[0] == 0
    for k, x in enumerate((first, second, last)):
        out_ref[:, pl.ds(k * w, w)] = jnp.where(is_first, x[:half], x[half:]) * scale


def assemble(core, parts, order):
    w = parts[0].shape[1]
    vmem = pl.BlockSpec(memory_space=pltpu.VMEM)
    return pl.pallas_call(
        functools.partial(assemble_kernel, scale=1.0 / order),
        in_specs=[pl.BlockSpec(memory_space=pltpu.SMEM)] + [vmem] * len(parts),
        out_specs=vmem,
        out_shape=jax.ShapeDtypeStruct((3 * w // 2, 3 * w), jnp.float32),
        compiler_params=pltpu.CompilerParams(vmem_limit_bytes=12 * MIB),
        cost_estimate=pl.CostEstimate(flops=0, bytes_accessed=2_000_000, transcendentals=0),
    )(core, *parts).T


def linear(chip, core, z):
    return (chip * 2 + core) * 4 + z


def send(x, pairs):
    return lax.ppermute(x, ("orb", "band"), pairs)


def mirrored(pairs):
    out = []
    for chip in range(4):
        for a, b in pairs:
            out.append((linear(chip, 0, a), linear(chip, 0, b)))
            out.append((linear(chip, 1, 3 - a), linear(chip, 1, 3 - b)))
    return out


def gather_bands(x):
    return [x] + [send(x, mirrored([(source, 2)])) for source in (0, 1, 3)]


def over_chips(flip):
    return [
        (linear(chip, core, 2 - core), linear(chip ^ flip, core, 2 - core))
        for chip in range(4)
        for core in range(2)
    ]


FLIPS = (3, 1, 2, 0)
FAR = ((0, ((0, 0, 1), (1, 1, 1))), (1, ((1, 1, 0),)), (2, ((0, 0, 0),)))
NEAR = ((1, ((0, 0, 1),)), (2, ((1, 1, 1),)), (3, ((0, 0, 0), (1, 1, 0))))
BOTH = (
    (0, ((0, 0, 1), (1, 1, 1))),
    (1, ((0, 2, 1), (1, 1, 0))),
    (2, ((0, 0, 0), (1, 3, 1))),
    (3, ((0, 2, 0), (1, 3, 0))),
)
EVERY = [(q, c, z) for q in range(4) for c in range(2) for z in range(4)]
SWAP = [(linear(q, c, z), linear(q, 1 - c, z)) for q, c, z in EVERY]
TURN = [(linear(q, c, z), linear(z, c, q)) for q, c, z in EVERY]
TURN_UP = [pair for pair in TURN if pair[0] // 4 % 2 == 1]


def simple_gram(filtered):
    partial_gram = jnp.dot(
        filtered.T,
        lax.all_gather(filtered, "band", axis=1, tiled=True),
        precision=lax.Precision.HIGH,
        preferred_element_type=jnp.float32,
    )
    return lax.psum_scatter(partial_gram, "orb", scatter_dimension=1, tiled=True)


def in_turn(hi, lo, old, order):
    core = (lax.axis_index("orb") & 1)[None]
    first = [apply_step(core, hi, lo, neighbours(x), x) for x in old]
    filtered = [apply_step(core, hi, lo, neighbours(x), x, v) for x, v in zip(first, old)]
    filtered = jnp.concatenate(filtered, axis=1)
    return filtered, simple_gram(filtered) / order


def index_tables():
    orb, z = lax.axis_index("orb"), lax.axis_index("band")
    chip, core = orb >> 1, orb & 1
    bands = jnp.stack([b + core * (3 - 2 * b) for b in (2, 0, 1, 3)])
    holder = (z == 2 - core).astype(jnp.int32)
    goals = jnp.stack([k + core * (3 - 2 * k) for k in (0, 1, 3)] + [z, holder])
    targets = jnp.stack([chip ^ flip for flip in FLIPS])
    return bands, goals, targets, core[None]


def by_symmetry(hi, lo, old, order, tables):
    bands, goals, targets, core = tables

    def one(x, halo, v=None, turned=False):
        return apply_step(core, hi, lo, halo, x, v, turned)

    v0, v1, v2 = old
    hv = [neighbours(x) for x in old]
    f0 = one(v0, hv[0])
    hf0 = neighbours(f0)
    f1 = one(v1, hv[1])
    hf1 = neighbours(f1)
    g0 = one(after_that(f0, f1), hf0, v0)
    z0 = gather_bands(g0)
    f2 = one(after_that(v2, g0), hv[2])
    hf2 = neighbours(f2)
    e1 = apply_part(core, hi, lo, after_that(f1, g0, f2, z0[1]), hf1[0], late=False)
    g1 = apply_part(core, hi, lo, hf1[1], after_that(e1, *z0[1:]), v1, late=True)
    z1 = gather_bands(g1)
    e2 = apply_part(core, hi, lo, after_that(f2, g1), hf2[0], late=False)
    g2 = apply_part(core, hi, lo, hf2[1], e2, v2, late=True)
    z2 = gather_bands(g2)
    c0, upper = chunk(bands, targets, [after_that(z0[0], g2)] + z0[1:], [])
    c1, early = chunk(bands, targets, [after_that(z1[0], upper[0])] + z1[1:], [c0], BOTH, upper)

    def first_step(parts):
        return [send(x, over_chips(flip)) for x, flip in zip(parts, (2, 1))]

    def second_step(got, ours):
        send_a, keep_a, send_b, keep_b = middle(*got, *ours)
        return [keep_a, send(send_a, over_chips(1)), keep_b, send(send_b, over_chips(2))]

    def deliver(parts):
        moved = pick(goals, parts)
        return [moved[3]] + [send(x, mirrored([(2, k)])) for k, x in zip((0, 1, 3), moved)]

    got_e = first_step(early[:2])
    c2, far = chunk(bands, targets, [after_that(z2[0], c1[0])] + z2[1:], [c0, c1], FAR)
    got_l = first_step(far)
    sums_e = second_step([after_that(got_e[0], far[0]), got_e[1]], early[2:])
    near = product(after_that(targets, sums_e[0]), [c0, c1, c2], NEAR)
    sums_l = second_step(got_l, near)
    arrived = [deliver([after_that(sums_e[0], sums_l[0])] + sums_e[1:])]
    sums_l[2] = after_that(sums_l[2], arrived[0][0])
    arrived.append(deliver(sums_l))
    filtered = jnp.concatenate([g0, g1, after_that(g2, near[0])], axis=1)
    piece = jnp.concatenate([(x[0] + x[1]) + (x[2] + x[3]) for x in arrived], axis=0)
    piece = piece + send(piece, SWAP)
    w = v0.shape[1]
    turn_e = send(piece[w : 2 * w], TURN)
    turn_l = send(piece[3 * w : 5 * w], TURN_UP)
    return filtered, assemble(core, [piece, turn_e, turn_l], order)


def body(blocks, columns, counts, vectors, symmetric):
    rows, width = vectors.shape
    order = rows * lax.axis_size("orb")
    slot_of = slot_table(columns, counts)
    later = vectors
    if symmetric:
        tables = index_tables()
        slot_of, tables, later = lax.optimization_barrier((slot_of, tables, vectors))
    old = [
        (later if c else vectors)[:, c : min(c + LANES, width)] for c in range(0, width, LANES)
    ]
    hi, lo = densify(slot_of, blocks)
    if symmetric:
        return by_symmetry(hi, lo, old, order, tables)
    return in_turn(hi, lo, old, order)


def solution(mesh):
    placed = (P("orb", None, None, None), P("orb", None), P("orb"), P("orb", "band"))

    def whole(blocks, columns, counts, vectors):
        symmetric = (
            mesh.shape["orb"] == 8 and mesh.shape["band"] == 4 and vectors.shape[1] == 3 * LANES
        )
        return body(blocks, columns, counts, vectors, symmetric)

    return jax.shard_map(
        whole,
        mesh=mesh,
        in_specs=placed,
        out_specs=(P("orb", "band"), P("band", "orb")),
        check_vma=False,
    )
```

```python
import functools

import jax
import jax.numpy as jnp
from jax import lax
from jax.experimental import pallas as pl
from jax.experimental.pallas import tpu as pltpu
from jax.sharding import PartitionSpec as P

GROUP = 4
LANES = 128
MIB = 1024 * 1024
APPLY_MIB = 10


def split(x):
    hi = x.astype(jnp.bfloat16)
    lo = (x - hi.astype(jnp.float32)).astype(jnp.bfloat16)
    return hi, lo


def densify_kernel(slot_ref, blocks_ref, hi_ref, lo_ref, *, spread, reach):
    blk = blocks_ref.shape[2]
    step = pl.program_id(0)
    tile = (blk, 2 * blk)
    shift = lax.broadcasted_iota(jnp.int32, tile, 1) - lax.broadcasted_iota(jnp.int32, tile, 0)

    def one_row(i, carry):
        row = step * GROUP + i
        start = pl.multiple_of(i * blk, blk)
        for pair in range(spread // 2):
            left = slot_ref[row, 2 * pair]
            right = slot_ref[row, 2 * pair + 1]
            lblk = jnp.where(left >= 0, blocks_ref[i, jnp.maximum(left, 0)], 0.0)
            rblk = jnp.where(right >= 0, blocks_ref[i, jnp.maximum(right, 0)], 0.0)
            both = jnp.concatenate([lblk, rblk], axis=1)
            if reach <= 2 * pair + 1 and 2 * pair < reach + GROUP:
                both = both - jnp.where(shift == (reach + i - 2 * pair) * blk, 0.1, 0.0)
            hi, lo = split(both / 0.9)
            hi_ref[pl.ds(start, blk), pl.ds(pair * 2 * blk, 2 * blk)] = hi
            lo_ref[pl.ds(start, blk), pl.ds(pair * 2 * blk, 2 * blk)] = lo
        return carry

    lax.fori_loop(0, GROUP, one_row, 0)


def densify(slot_of, blocks):
    rows, slots, blk, _ = blocks.shape
    spread = slot_of.shape[1]
    shape = pltpu.VMEM((rows * blk, spread * blk), jnp.bfloat16)
    out = pl.BlockSpec((GROUP * blk, spread * blk), lambda g, _: (g, 0))
    return pl.pallas_call(
        functools.partial(densify_kernel, spread=spread, reach=rows),
        grid_spec=pltpu.PrefetchScalarGridSpec(
            num_scalar_prefetch=1,
            grid=(rows // GROUP,),
            in_specs=[pl.BlockSpec((GROUP, slots, blk, blk), lambda g, _: (g, 0, 0, 0))],
            out_specs=[out, out],
        ),
        out_shape=[shape, shape],
        compiler_params=pltpu.CompilerParams(vmem_limit_bytes=20 * MIB),
        cost_estimate=pl.CostEstimate(flops=0, bytes_accessed=60_000_000, transcendentals=0),
    )(slot_of, blocks)


def apply_kernel(core_ref, hi_ref, lo_ref, near_ref, far_ref, own_ref, *rest, second, turned):
    inside_ref, across_ref = (far_ref, near_ref) if turned else (near_ref, far_ref)
    old_ref = rest[0] if second else None
    out_ref, parts = rest[-2:]
    rows, width = own_ref.shape
    wide = hi_ref.shape[1]
    tall = wide - 2 * rows
    core = core_ref[0]
    for place, ref in ((1, own_ref), (2 - 2 * core, inside_ref), (2 * core, across_ref)):
        there = pl.ds(pl.multiple_of(place * rows, rows), rows)
        parts[there, pl.ds(0, width)], parts[there, pl.ds(width, width)] = split(ref[...])

    def one_group(step, carry):
        start = pl.multiple_of(step * tall, tall)
        here = pl.ds(start, tall)
        reached = pl.ds(start, wide)
        both = jnp.dot(hi_ref[here, :], parts[reached, :], preferred_element_type=jnp.float32)
        other = jnp.dot(
            lo_ref[here, :], parts[reached, pl.ds(0, width)], preferred_element_type=jnp.float32
        )
        product = both[:, :width] + (both[:, width:] + other)
        if second:
            product = 2.0 * product - old_ref[here, :]
        out_ref[here, :] = product
        return carry

    lax.fori_loop(0, rows // tall, one_group, 0)


def apply_step(core, hi, lo, halo, own, old=None, turned=False):
    rows, width = own.shape
    wide = hi.shape[1]
    second = old is not None
    hi, lo = (pltpu.with_memory_space_constraint(x, pltpu.VMEM) for x in (hi, lo))
    vmem = pl.BlockSpec(memory_space=pltpu.VMEM)
    return pl.pallas_call(
        functools.partial(apply_kernel, second=second, turned=turned),
        in_specs=[pl.BlockSpec(memory_space=pltpu.SMEM)] + [vmem] * (6 if second else 5),
        out_specs=vmem,
        out_shape=jax.ShapeDtypeStruct((rows, width), jnp.float32),
        scratch_shapes=[pltpu.VMEM((3 * rows, 2 * width), jnp.bfloat16)],
        compiler_params=pltpu.CompilerParams(vmem_limit_bytes=APPLY_MIB * MIB),
        cost_estimate=pl.CostEstimate(
            flops=8 * rows * wide * width, bytes_accessed=4 * rows * wide, transcendentals=0
        ),
    )(core, hi, lo, *(halo[::-1] if turned else halo), own, *([old] if second else []))


def part_kernel(core_ref, hi_ref, lo_ref, *refs, late):
    out_ref, parts = refs[-2:]
    rows, width = refs[0].shape
    wide = hi_ref.shape[1]
    tall = wide - 2 * rows
    core = core_ref[0]
    places = (core,) if late else (1, 2 - 2 * core)
    for place, ref in zip(places, refs):
        there = pl.ds(pl.multiple_of(place * rows, rows), rows)
        parts[there, pl.ds(0, width)], parts[there, pl.ds(width, width)] = split(ref[...])
    empty = 1 - core if late else 2 * core
    parts[pl.ds(pl.multiple_of(empty * rows, rows), rows), :] = jnp.zeros((rows, 2 * width), jnp.bfloat16)
    size = rows if late else wide - tall
    column = core * (wide - rows) if late else (1 - core) * tall
    shift = core * tall if late else (1 - core) * tall

    def one_group(step, carry):
        here = pl.ds(pl.multiple_of(step * tall, tall), tall)
        reached = pl.ds(pl.multiple_of(step * tall + shift, tall), size)
        columns = pl.ds(pl.multiple_of(column, tall), size)
        both = jnp.dot(hi_ref[here, columns], parts[reached, :], preferred_element_type=jnp.float32)
        other = jnp.dot(
            lo_ref[here, columns], parts[reached, pl.ds(0, width)], preferred_element_type=jnp.float32
        )
        product = both[:, :width] + (both[:, width:] + other)
        if late:
            product = 2.0 * (refs[1][here, :] + product) - refs[2][here, :]
        out_ref[here, :] = product
        return carry

    lax.fori_loop(0, rows // tall, one_group, 0)


def apply_part(core, hi, lo, *ins, late):
    rows, width = ins[0].shape
    hi, lo = (pltpu.with_memory_space_constraint(x, pltpu.VMEM) for x in (hi, lo))
    vmem = pl.BlockSpec(memory_space=pltpu.VMEM)
    return pl.pallas_call(
        functools.partial(part_kernel, late=late),
        in_specs=[pl.BlockSpec(memory_space=pltpu.SMEM)] + [vmem] * (2 + len(ins)),
        out_specs=vmem,
        out_shape=jax.ShapeDtypeStruct((rows, width), jnp.float32),
        scratch_shapes=[pltpu.VMEM(((2 if late else 3) * rows, 2 * width), jnp.bfloat16)],
        compiler_params=pltpu.CompilerParams(vmem_limit_bytes=APPLY_MIB * MIB),
        cost_estimate=pl.CostEstimate(
            flops=(2 if late else 6) * rows * hi.shape[1] * width,
            bytes_accessed=4 * rows * hi.shape[1],
            transcendentals=0,
        ),
    )(core, hi, lo, *ins)


def slot_table(columns, counts):
    rows, slots = columns.shape
    total = rows * lax.axis_size("orb")
    spread = GROUP + 2 * rows
    ids = jnp.arange(rows, dtype=jnp.int32)
    offset = lax.axis_index("orb") * rows - rows
    place = (columns - offset) % total - (ids // GROUP * GROUP)[:, None]
    number = jnp.arange(slots, dtype=jnp.int32)
    place = jnp.where(number[None, :] < counts[:, None], place, -1)
    hit = place[:, :, None] == jnp.arange(spread, dtype=jnp.int32)[None, None, :]
    return jnp.max(jnp.where(hit, number[None, :, None], -1), axis=1)


def neighbours(x):
    size = lax.axis_size("orb")
    inside = [(i, i ^ 1) for i in range(size)]
    across = [(i, (i + 1 if i % 2 else i - 1) % size) for i in range(size)]
    return lax.ppermute(x, "orb", inside), lax.ppermute(x, "orb", across)


def after_that(x, *done):
    return lax.optimization_barrier((x, done))[0]


def store_parts(band_ref, ins, outs):
    hi_ref, lo_ref, thi_ref, tlo_ref = outs
    for place, ref in enumerate(ins):
        x = ref[...]
        width = x.shape[1]
        there = pl.ds(pl.multiple_of(band_ref[place] * width, width), width)
        hi_ref[:, there], lo_ref[:, there] = split(x)
        thi_ref[there, :], tlo_ref[there, :] = split(x.T)


def block_row(target, turned, right, part):
    rows = turned[0][0].shape[0] // 4
    there = pl.ds(pl.multiple_of(target * rows, rows), rows)
    thi = jnp.concatenate([hi[there, :] for hi, lo in turned], axis=0)
    tlo = jnp.concatenate([lo[there, :] for hi, lo in turned], axis=0)
    if part is not None:
        half = thi.shape[0] // 2
        thi, tlo = (x[part * half : (part + 1) * half] for x in (thi, tlo))
    hi_ref, lo_ref = right
    total = jnp.dot(thi, lo_ref[...], preferred_element_type=jnp.float32)
    total += jnp.dot(tlo, hi_ref[...], preferred_element_type=jnp.float32)
    return total + jnp.dot(thi, hi_ref[...], preferred_element_type=jnp.float32)


def rows_of(target_ref, turned, right, outs, plan, old_products=()):
    for place, parts in plan:
        wanted = [part for part, _, _ in parts]
        if old_products:
            total = block_row(target_ref[place], turned, right, None)
            total = jnp.concatenate([old_products[place][...], total], axis=0)
        else:
            total = block_row(target_ref[place], turned, right, wanted[0] if len(wanted) == 1 else None)
        half = total.shape[0] // 2
        for part, out, slot in parts:
            if old_products or len(wanted) == 2:
                outs[out][slot] = total[part * half : (part + 1) * half]
            else:
                outs[out][slot] = total


def chunk_kernel(band_ref, target_ref, *refs, before, upper, plan):
    ins, refs = refs[:4], refs[4:]
    olds, refs = [refs[4 * k : 4 * k + 4] for k in range(before)], refs[4 * before :]
    old_products, refs = (refs[:4], refs[4:]) if upper else ((), refs)
    new, outs = refs[:4], refs[4:]
    store_parts(band_ref, ins, new)
    turned = [x[2:] for x in olds] + [new[2:]]
    if plan is None:
        for place, out in enumerate(outs):
            out[...] = block_row(target_ref[place], turned, new[:2], None)
    else:
        rows_of(target_ref, turned, new[:2], outs, plan, old_products)


def chunk(bands, targets, parts, olds, plan=None, old_products=()):
    rows, width = parts[0].shape
    plain = pltpu.VMEM((rows, 4 * width), jnp.bfloat16)
    turned = pltpu.VMEM((4 * width, rows), jnp.bfloat16)
    high = width * (len(olds) + 1) + (old_products[0].shape[0] if old_products else 0)
    count = 4 if plan is None else 1 + max(out for _, x in plan for _, out, _ in x)
    shape = (high, 4 * width) if plan is None else (2, high // 2, 4 * width)
    product = jax.ShapeDtypeStruct(shape, jnp.float32)
    olds = [pltpu.with_memory_space_constraint(x, pltpu.VMEM) for old in olds for x in old]
    ins = [*parts, *olds, *old_products]
    vmem, smem = pl.BlockSpec(memory_space=pltpu.VMEM), pl.BlockSpec(memory_space=pltpu.SMEM)
    out = pl.pallas_call(
        functools.partial(chunk_kernel, before=len(olds) // 4, upper=bool(old_products), plan=plan),
        in_specs=[smem, smem] + [vmem] * len(ins),
        out_specs=[vmem] * (4 + count),
        out_shape=[plain, plain, turned, turned] + [product] * count,
        compiler_params=pltpu.CompilerParams(vmem_limit_bytes=14 * MIB),
        cost_estimate=pl.CostEstimate(
            flops=96 * high * width * rows, bytes_accessed=8_000_000, transcendentals=0
        ),
    )(bands, targets, *ins)
    return out[:4], list(out[4:])


def product_kernel(target_ref, *refs, plan):
    ins, outs = refs[:-2], refs[-2:]
    rows_of(target_ref, [ins[k : k + 2] for k in range(2, len(ins), 2)], ins[:2], outs, plan)


def product(targets, chunks, plan):
    rows, wide = chunks[-1][0].shape
    ins = [*chunks[-1][:2]] + [x for c in chunks for x in c[2:]]
    ins = [pltpu.with_memory_space_constraint(x, pltpu.VMEM) for x in ins]
    high = wide // 4 * len(chunks)
    vmem = pl.BlockSpec(memory_space=pltpu.VMEM)
    return pl.pallas_call(
        functools.partial(product_kernel, plan=plan),
        in_specs=[pl.BlockSpec(memory_space=pltpu.SMEM)] + [vmem] * len(ins),
        out_specs=[vmem] * 2,
        out_shape=[jax.ShapeDtypeStruct((2, high // 2, wide), jnp.float32)] * 2,
        compiler_params=pltpu.CompilerParams(vmem_limit_bytes=16 * MIB),
        cost_estimate=pl.CostEstimate(
            flops=12 * high * wide * rows, bytes_accessed=4_000_000, transcendentals=0
        ),
    )(targets, *ins)


def middle_kernel(got_a, got_b, ours_a, ours_b, send_a, keep_a, send_b, keep_b):
    for got, ours, send_ref, keep in ((got_a, ours_a, send_a, keep_a), (got_b, ours_b, send_b, keep_b)):
        keep[...] = got[0] + ours[0]
        send_ref[...] = got[1] + ours[1]


def middle(*parts):
    shape = jax.ShapeDtypeStruct(parts[0].shape[1:], jnp.float32)
    vmem = pl.BlockSpec(memory_space=pltpu.VMEM)
    return pl.pallas_call(
        middle_kernel,
        in_specs=[vmem] * 4,
        out_specs=[vmem] * 4,
        out_shape=[shape] * 4,
        compiler_params=pltpu.CompilerParams(vmem_limit_bytes=8 * MIB),
        cost_estimate=pl.CostEstimate(flops=0, bytes_accessed=5_000_000, transcendentals=0),
    )(*parts)


def pick_kernel(goal_ref, *refs):
    ins, outs = refs[:4], refs[4:]
    width = ins[0].shape[1] // 4
    for k, out in enumerate(outs):
        there = pl.ds(pl.multiple_of(goal_ref[k] * width, width), width)
        x, y, u, v = (ref[:, there] for ref in ins)
        total = jnp.concatenate([x + y, u + v], axis=0)
        out[...] = jnp.where(goal_ref[4] > 0, total, 0.0) if k == 3 else total


def pick(goals, parts):
    rows, size = parts[0].shape
    shape = jax.ShapeDtypeStruct((2 * rows, size // 4), jnp.float32)
    vmem = pl.BlockSpec(memory_space=pltpu.VMEM)
    return pl.pallas_call(
        pick_kernel,
        in_specs=[pl.BlockSpec(memory_space=pltpu.SMEM)] + [vmem] * 4,
        out_specs=[vmem] * 4,
        out_shape=[shape] * 4,
        compiler_params=pltpu.CompilerParams(vmem_limit_bytes=8 * MIB),
        cost_estimate=pl.CostEstimate(flops=0, bytes_accessed=3_000_000, transcendentals=0),
    )(goals, *parts)


def assemble_kernel(core_ref, piece_ref, turn_e_ref, turn_l_ref, out_ref, *, scale):
    w = piece_ref.shape[1]
    first = jnp.concatenate([piece_ref[:w, :], turn_e_ref[...].T, turn_l_ref[:w, :].T], axis=0)
    second = jnp.concatenate([piece_ref[w : 3 * w, :], turn_l_ref[w:, :].T], axis=0)
    last = piece_ref[3 * w :, :]
    half = out_ref.shape[0]
    is_first = core_ref[0] == 0
    for k, x in enumerate((first, second, last)):
        out_ref[:, pl.ds(k * w, w)] = jnp.where(is_first, x[:half], x[half:]) * scale


def assemble(core, parts, order):
    w = parts[0].shape[1]
    vmem = pl.BlockSpec(memory_space=pltpu.VMEM)
    return pl.pallas_call(
        functools.partial(assemble_kernel, scale=1.0 / order),
        in_specs=[pl.BlockSpec(memory_space=pltpu.SMEM)] + [vmem] * len(parts),
        out_specs=vmem,
        out_shape=jax.ShapeDtypeStruct((3 * w // 2, 3 * w), jnp.float32),
        compiler_params=pltpu.CompilerParams(vmem_limit_bytes=12 * MIB),
        cost_estimate=pl.CostEstimate(flops=0, bytes_accessed=2_000_000, transcendentals=0),
    )(core, *parts).T


def linear(chip, core, z):
    return (chip * 2 + core) * 4 + z


def send(x, pairs):
    return lax.ppermute(x, ("orb", "band"), pairs)


def mirrored(pairs):
    out = []
    for chip in range(4):
        for a, b in pairs:
            out.append((linear(chip, 0, a), linear(chip, 0, b)))
            out.append((linear(chip, 1, 3 - a), linear(chip, 1, 3 - b)))
    return out


def gather_bands(x, later=None):
    last = x if later is None else later
    return [x] + [send(y, mirrored([(source, 2)])) for source, y in ((0, x), (1, x), (3, last))]


def over_chips(flip):
    return [
        (linear(chip, core, 2 - core), linear(chip ^ flip, core, 2 - core))
        for chip in range(4)
        for core in range(2)
    ]


FLIPS = (3, 1, 2, 0)
FAR = ((0, ((0, 0, 1), (1, 1, 1))), (1, ((1, 1, 0),)), (2, ((0, 0, 0),)))
NEAR = ((1, ((0, 0, 1),)), (2, ((1, 1, 1),)), (3, ((0, 0, 0), (1, 1, 0))))
BOTH = (
    (0, ((0, 0, 1), (1, 1, 1))),
    (1, ((0, 2, 1), (1, 1, 0))),
    (2, ((0, 0, 0), (1, 3, 1))),
    (3, ((0, 2, 0), (1, 3, 0))),
)
EVERY = [(q, c, z) for q in range(4) for c in range(2) for z in range(4)]
SWAP = [(linear(q, c, z), linear(q, 1 - c, z)) for q, c, z in EVERY]
TURN = [(linear(q, c, z), linear(z, c, q)) for q, c, z in EVERY]
TURN_UP = [pair for pair in TURN if pair[0] // 4 % 2 == 1]


def simple_gram(filtered):
    partial_gram = jnp.dot(
        filtered.T,
        lax.all_gather(filtered, "band", axis=1, tiled=True),
        precision=lax.Precision.HIGH,
        preferred_element_type=jnp.float32,
    )
    return lax.psum_scatter(partial_gram, "orb", scatter_dimension=1, tiled=True)


def in_turn(hi, lo, old, order):
    core = (lax.axis_index("orb") & 1)[None]
    first = [apply_step(core, hi, lo, neighbours(x), x) for x in old]
    filtered = [apply_step(core, hi, lo, neighbours(x), x, v) for x, v in zip(first, old)]
    filtered = jnp.concatenate(filtered, axis=1)
    return filtered, simple_gram(filtered) / order


def index_tables():
    orb, z = lax.axis_index("orb"), lax.axis_index("band")
    chip, core = orb >> 1, orb & 1
    bands = jnp.stack([b + core * (3 - 2 * b) for b in (2, 0, 1, 3)])
    holder = (z == 2 - core).astype(jnp.int32)
    goals = jnp.stack([k + core * (3 - 2 * k) for k in (0, 1, 3)] + [z, holder])
    targets = jnp.stack([chip ^ flip for flip in FLIPS])
    return bands, goals, targets, core[None]


def by_symmetry(hi, lo, old, order, tables):
    bands, goals, targets, core = tables

    def one(x, halo, v=None, turned=False):
        return apply_step(core, hi, lo, halo, x, v, turned)

    v0, v1, v2 = old
    hv = [neighbours(x) for x in old]
    f0 = one(v0, hv[0])
    hf0 = neighbours(f0)
    f1 = one(v1, hv[1])
    hf1 = neighbours(f1)
    g0 = one(after_that(f0, f1), hf0, v0)
    z0 = gather_bands(g0)
    e1 = apply_part(core, hi, lo, after_that(f1, g0), hf1[0], late=False)
    f2 = one(after_that(v2, e1), hv[2])
    hf2 = neighbours(f2)
    g1 = apply_part(core, hi, lo, hf1[1], after_that(e1, *z0[1:]), v1, late=True)
    z1 = gather_bands(g1)
    e2 = apply_part(core, hi, lo, after_that(f2, g1), hf2[0], late=False)
    g2 = apply_part(core, hi, lo, hf2[1], e2, v2, late=True)
    c0, upper = chunk(bands, targets, [after_that(z0[0], g2)] + z0[1:], [])
    z2 = gather_bands(g2, after_that(g2, upper[0]))
    c1, early = chunk(bands, targets, [after_that(z1[0], upper[0])] + z1[1:], [c0], BOTH, upper)

    def first_step(parts):
        return [send(x, over_chips(flip)) for x, flip in zip(parts, (2, 1))]

    def second_step(got, ours):
        send_a, keep_a, send_b, keep_b = middle(*got, *ours)
        return [keep_a, send(send_a, over_chips(1)), keep_b, send(send_b, over_chips(2))]

    def deliver(parts):
        moved = pick(goals, parts)
        return [moved[3]] + [send(x, mirrored([(2, k)])) for k, x in zip((0, 1, 3), moved)]

    got_e = first_step(early[:2])
    c2, far = chunk(bands, targets, [after_that(z2[0], c1[0])] + z2[1:], [c0, c1], FAR)
    got_l = first_step(far)
    sums_e = second_step([after_that(got_e[0], far[0]), got_e[1]], early[2:])
    near = product(after_that(targets, sums_e[0]), [c0, c1, c2], NEAR)
    sums_l = second_step(got_l, near)
    arrived = [deliver([after_that(sums_e[0], sums_l[0])] + sums_e[1:])]
    sums_l[2] = after_that(sums_l[2], arrived[0][0])
    arrived.append(deliver(sums_l))
    filtered = jnp.concatenate([g0, g1, after_that(g2, near[0])], axis=1)
    piece = jnp.concatenate([(x[0] + x[1]) + (x[2] + x[3]) for x in arrived], axis=0)
    piece = piece + send(piece, SWAP)
    w = v0.shape[1]
    turn_e = send(piece[w : 2 * w], TURN)
    turn_l = send(piece[3 * w : 5 * w], TURN_UP)
    return filtered, assemble(core, [piece, turn_e, turn_l], order)


def body(blocks, columns, counts, vectors, symmetric):
    rows, width = vectors.shape
    order = rows * lax.axis_size("orb")
    slot_of = slot_table(columns, counts)
    later = vectors
    if symmetric:
        tables = index_tables()
        slot_of, tables, later = lax.optimization_barrier((slot_of, tables, vectors))
    old = [
        (later if c else vectors)[:, c : min(c + LANES, width)] for c in range(0, width, LANES)
    ]
    hi, lo = densify(slot_of, blocks)
    if symmetric:
        return by_symmetry(hi, lo, old, order, tables)
    return in_turn(hi, lo, old, order)


def solution(mesh):
    placed = (P("orb", None, None, None), P("orb", None), P("orb"), P("orb", "band"))

    def whole(blocks, columns, counts, vectors):
        symmetric = (
            mesh.shape["orb"] == 8 and mesh.shape["band"] == 4 and vectors.shape[1] == 3 * LANES
        )
        return body(blocks, columns, counts, vectors, symmetric)

    return jax.shard_map(
        whole,
        mesh=mesh,
        in_specs=placed,
        out_specs=(P("orb", "band"), P("band", "orb")),
        check_vma=False,
    )
```

```python
import functools

import jax
import jax.numpy as jnp
from jax import lax
from jax.experimental import pallas as pl
from jax.experimental.pallas import tpu as pltpu
from jax.sharding import PartitionSpec as P

GROUP = 4
LANES = 128
MIB = 1024 * 1024
APPLY_MIB = 10


def split(x):
    hi = x.astype(jnp.bfloat16)
    lo = (x - hi.astype(jnp.float32)).astype(jnp.bfloat16)
    return hi, lo


def densify_kernel(slot_ref, blocks_ref, hi_ref, lo_ref, *, spread, reach):
    blk = blocks_ref.shape[2]
    step = pl.program_id(0)
    tile = (blk, 2 * blk)
    shift = lax.broadcasted_iota(jnp.int32, tile, 1) - lax.broadcasted_iota(jnp.int32, tile, 0)

    def one_row(i, carry):
        row = step * GROUP + i
        start = pl.multiple_of(i * blk, blk)
        for pair in range(spread // 2):
            left = slot_ref[row, 2 * pair]
            right = slot_ref[row, 2 * pair + 1]
            lblk = jnp.where(left >= 0, blocks_ref[i, jnp.maximum(left, 0)], 0.0)
            rblk = jnp.where(right >= 0, blocks_ref[i, jnp.maximum(right, 0)], 0.0)
            both = jnp.concatenate([lblk, rblk], axis=1)
            if reach <= 2 * pair + 1 and 2 * pair < reach + GROUP:
                both = both - jnp.where(shift == (reach + i - 2 * pair) * blk, 0.1, 0.0)
            hi, lo = split(both / 0.9)
            hi_ref[pl.ds(start, blk), pl.ds(pair * 2 * blk, 2 * blk)] = hi
            lo_ref[pl.ds(start, blk), pl.ds(pair * 2 * blk, 2 * blk)] = lo
        return carry

    lax.fori_loop(0, GROUP, one_row, 0)


def densify(slot_of, blocks):
    rows, slots, blk, _ = blocks.shape
    spread = slot_of.shape[1]
    shape = pltpu.VMEM((rows * blk, spread * blk), jnp.bfloat16)
    out = pl.BlockSpec((GROUP * blk, spread * blk), lambda g, _: (g, 0))
    return pl.pallas_call(
        functools.partial(densify_kernel, spread=spread, reach=rows),
        grid_spec=pltpu.PrefetchScalarGridSpec(
            num_scalar_prefetch=1,
            grid=(rows // GROUP,),
            in_specs=[pl.BlockSpec((GROUP, slots, blk, blk), lambda g, _: (g, 0, 0, 0))],
            out_specs=[out, out],
        ),
        out_shape=[shape, shape],
        compiler_params=pltpu.CompilerParams(vmem_limit_bytes=20 * MIB),
        cost_estimate=pl.CostEstimate(flops=0, bytes_accessed=60_000_000, transcendentals=0),
    )(slot_of, blocks)


def apply_kernel(core_ref, hi_ref, lo_ref, near_ref, far_ref, own_ref, *rest, second, turned):
    inside_ref, across_ref = (far_ref, near_ref) if turned else (near_ref, far_ref)
    old_ref = rest[0] if second else None
    out_ref, parts = rest[-2:]
    rows, width = own_ref.shape
    wide = hi_ref.shape[1]
    tall = wide - 2 * rows
    core = core_ref[0]
    for place, ref in ((1, own_ref), (2 - 2 * core, inside_ref), (2 * core, across_ref)):
        there = pl.ds(pl.multiple_of(place * rows, rows), rows)
        parts[there, pl.ds(0, width)], parts[there, pl.ds(width, width)] = split(ref[...])

    def one_group(step, carry):
        start = pl.multiple_of(step * tall, tall)
        here = pl.ds(start, tall)
        reached = pl.ds(start, wide)
        both = jnp.dot(hi_ref[here, :], parts[reached, :], preferred_element_type=jnp.float32)
        other = jnp.dot(
            lo_ref[here, :], parts[reached, pl.ds(0, width)], preferred_element_type=jnp.float32
        )
        product = both[:, :width] + (both[:, width:] + other)
        if second:
            product = 2.0 * product - old_ref[here, :]
        out_ref[here, :] = product
        return carry

    lax.fori_loop(0, rows // tall, one_group, 0)


def apply_step(core, hi, lo, halo, own, old=None, turned=False):
    rows, width = own.shape
    wide = hi.shape[1]
    second = old is not None
    hi, lo = (pltpu.with_memory_space_constraint(x, pltpu.VMEM) for x in (hi, lo))
    vmem = pl.BlockSpec(memory_space=pltpu.VMEM)
    return pl.pallas_call(
        functools.partial(apply_kernel, second=second, turned=turned),
        in_specs=[pl.BlockSpec(memory_space=pltpu.SMEM)] + [vmem] * (6 if second else 5),
        out_specs=vmem,
        out_shape=jax.ShapeDtypeStruct((rows, width), jnp.float32),
        scratch_shapes=[pltpu.VMEM((3 * rows, 2 * width), jnp.bfloat16)],
        compiler_params=pltpu.CompilerParams(vmem_limit_bytes=APPLY_MIB * MIB),
        cost_estimate=pl.CostEstimate(
            flops=8 * rows * wide * width, bytes_accessed=4 * rows * wide, transcendentals=0
        ),
    )(core, hi, lo, *(halo[::-1] if turned else halo), own, *([old] if second else []))


def part_kernel(core_ref, hi_ref, lo_ref, *refs, late):
    out_ref, parts = refs[-2:]
    rows, width = refs[0].shape
    wide = hi_ref.shape[1]
    tall = wide - 2 * rows
    core = core_ref[0]
    places = (core,) if late else (1, 2 - 2 * core)
    for place, ref in zip(places, refs):
        there = pl.ds(pl.multiple_of(place * rows, rows), rows)
        parts[there, pl.ds(0, width)], parts[there, pl.ds(width, width)] = split(ref[...])
    steps = rows // tall
    half = steps // 2
    if late:
        few = (half - 1) * tall
        empty = pl.ds(pl.multiple_of(rows - core * few, tall), few)
        runs = (
            (rows, half * core, core * (wide - rows), core * tall),
            (half * tall, half * (1 - core), core * (wide - half * tall), core * (half + 1) * tall),
        )
    else:
        few = rows
        empty = pl.ds(pl.multiple_of(2 * core * rows, rows), few)
        runs = ((wide - tall, 0, (1 - core) * tall, (1 - core) * tall),)
    parts[empty, :] = jnp.zeros((few, 2 * width), jnp.bfloat16)
    for size, first, column, shift in runs:

        def one_group(k, carry, size=size, first=first, column=column, shift=shift):
            start = pl.multiple_of((k + first) * tall, tall)
            here = pl.ds(start, tall)
            reached = pl.ds(pl.multiple_of(start + shift, tall), size)
            columns = pl.ds(pl.multiple_of(column, tall), size)
            both = jnp.dot(hi_ref[here, columns], parts[reached, :], preferred_element_type=jnp.float32)
            other = jnp.dot(
                lo_ref[here, columns],
                parts[reached, pl.ds(0, width)],
                preferred_element_type=jnp.float32,
            )
            product = both[:, :width] + (both[:, width:] + other)
            if late:
                product = 2.0 * (refs[1][here, :] + product) - refs[2][here, :]
            out_ref[here, :] = product
            return carry

        lax.fori_loop(0, half if late else steps, one_group, 0)


def apply_part(core, hi, lo, *ins, late):
    rows, width = ins[0].shape
    hi, lo = (pltpu.with_memory_space_constraint(x, pltpu.VMEM) for x in (hi, lo))
    vmem = pl.BlockSpec(memory_space=pltpu.VMEM)
    return pl.pallas_call(
        functools.partial(part_kernel, late=late),
        in_specs=[pl.BlockSpec(memory_space=pltpu.SMEM)] + [vmem] * (2 + len(ins)),
        out_specs=vmem,
        out_shape=jax.ShapeDtypeStruct((rows, width), jnp.float32),
        scratch_shapes=[pltpu.VMEM(((2 if late else 3) * rows, 2 * width), jnp.bfloat16)],
        compiler_params=pltpu.CompilerParams(vmem_limit_bytes=APPLY_MIB * MIB),
        cost_estimate=pl.CostEstimate(
            flops=(2 if late else 6) * rows * hi.shape[1] * width,
            bytes_accessed=4 * rows * hi.shape[1],
            transcendentals=0,
        ),
    )(core, hi, lo, *ins)


def slot_table(columns, counts):
    rows, slots = columns.shape
    total = rows * lax.axis_size("orb")
    spread = GROUP + 2 * rows
    ids = jnp.arange(rows, dtype=jnp.int32)
    offset = lax.axis_index("orb") * rows - rows
    place = (columns - offset) % total - (ids // GROUP * GROUP)[:, None]
    number = jnp.arange(slots, dtype=jnp.int32)
    place = jnp.where(number[None, :] < counts[:, None], place, -1)
    hit = place[:, :, None] == jnp.arange(spread, dtype=jnp.int32)[None, None, :]
    return jnp.max(jnp.where(hit, number[None, :, None], -1), axis=1)


def neighbours(x):
    size = lax.axis_size("orb")
    inside = [(i, i ^ 1) for i in range(size)]
    across = [(i, (i + 1 if i % 2 else i - 1) % size) for i in range(size)]
    return lax.ppermute(x, "orb", inside), lax.ppermute(x, "orb", across)


def after_that(x, *done):
    return lax.optimization_barrier((x, done))[0]


def store_parts(band_ref, ins, outs):
    hi_ref, lo_ref, thi_ref, tlo_ref = outs
    for place, ref in enumerate(ins):
        x = ref[...]
        width = x.shape[1]
        there = pl.ds(pl.multiple_of(band_ref[place] * width, width), width)
        hi_ref[:, there], lo_ref[:, there] = split(x)
        thi_ref[there, :], tlo_ref[there, :] = split(x.T)


def block_row(target, turned, right, part):
    rows = turned[0][0].shape[0] // 4
    there = pl.ds(pl.multiple_of(target * rows, rows), rows)
    thi = jnp.concatenate([hi[there, :] for hi, lo in turned], axis=0)
    tlo = jnp.concatenate([lo[there, :] for hi, lo in turned], axis=0)
    if part is not None:
        half = thi.shape[0] // 2
        thi, tlo = (x[part * half : (part + 1) * half] for x in (thi, tlo))
    hi_ref, lo_ref = right
    total = jnp.dot(thi, lo_ref[...], preferred_element_type=jnp.float32)
    total += jnp.dot(tlo, hi_ref[...], preferred_element_type=jnp.float32)
    return total + jnp.dot(thi, hi_ref[...], preferred_element_type=jnp.float32)


def rows_of(target_ref, turned, right, outs, plan, old_products=()):
    for place, parts in plan:
        wanted = [part for part, _, _ in parts]
        if old_products:
            total = block_row(target_ref[place], turned, right, None)
            total = jnp.concatenate([old_products[place][...], total], axis=0)
        else:
            total = block_row(target_ref[place], turned, right, wanted[0] if len(wanted) == 1 else None)
        half = total.shape[0] // 2
        for part, out, slot in parts:
            if old_products or len(wanted) == 2:
                outs[out][slot] = total[part * half : (part + 1) * half]
            else:
                outs[out][slot] = total


def chunk_kernel(band_ref, target_ref, *refs, before, upper, plan):
    ins, refs = refs[:4], refs[4:]
    olds, refs = [refs[4 * k : 4 * k + 4] for k in range(before)], refs[4 * before :]
    old_products, refs = (refs[:4], refs[4:]) if upper else ((), refs)
    new, outs = refs[:4], refs[4:]
    store_parts(band_ref, ins, new)
    turned = [x[2:] for x in olds] + [new[2:]]
    if plan is None:
        for place, out in enumerate(outs):
            out[...] = block_row(target_ref[place], turned, new[:2], None)
    else:
        rows_of(target_ref, turned, new[:2], outs, plan, old_products)


def chunk(bands, targets, parts, olds, plan=None, old_products=()):
    rows, width = parts[0].shape
    plain = pltpu.VMEM((rows, 4 * width), jnp.bfloat16)
    turned = pltpu.VMEM((4 * width, rows), jnp.bfloat16)
    high = width * (len(olds) + 1) + (old_products[0].shape[0] if old_products else 0)
    count = 4 if plan is None else 1 + max(out for _, x in plan for _, out, _ in x)
    shape = (high, 4 * width) if plan is None else (2, high // 2, 4 * width)
    product = jax.ShapeDtypeStruct(shape, jnp.float32)
    olds = [pltpu.with_memory_space_constraint(x, pltpu.VMEM) for old in olds for x in old]
    ins = [*parts, *olds, *old_products]
    vmem, smem = pl.BlockSpec(memory_space=pltpu.VMEM), pl.BlockSpec(memory_space=pltpu.SMEM)
    out = pl.pallas_call(
        functools.partial(chunk_kernel, before=len(olds) // 4, upper=bool(old_products), plan=plan),
        in_specs=[smem, smem] + [vmem] * len(ins),
        out_specs=[vmem] * (4 + count),
        out_shape=[plain, plain, turned, turned] + [product] * count,
        compiler_params=pltpu.CompilerParams(vmem_limit_bytes=14 * MIB),
        cost_estimate=pl.CostEstimate(
            flops=96 * high * width * rows, bytes_accessed=8_000_000, transcendentals=0
        ),
    )(bands, targets, *ins)
    return out[:4], list(out[4:])


def product_kernel(target_ref, *refs, plan):
    ins, outs = refs[:-2], refs[-2:]
    rows_of(target_ref, [ins[k : k + 2] for k in range(2, len(ins), 2)], ins[:2], outs, plan)


def product(targets, chunks, plan):
    rows, wide = chunks[-1][0].shape
    ins = [*chunks[-1][:2]] + [x for c in chunks for x in c[2:]]
    ins = [pltpu.with_memory_space_constraint(x, pltpu.VMEM) for x in ins]
    high = wide // 4 * len(chunks)
    vmem = pl.BlockSpec(memory_space=pltpu.VMEM)
    return pl.pallas_call(
        functools.partial(product_kernel, plan=plan),
        in_specs=[pl.BlockSpec(memory_space=pltpu.SMEM)] + [vmem] * len(ins),
        out_specs=[vmem] * 2,
        out_shape=[jax.ShapeDtypeStruct((2, high // 2, wide), jnp.float32)] * 2,
        compiler_params=pltpu.CompilerParams(vmem_limit_bytes=16 * MIB),
        cost_estimate=pl.CostEstimate(
            flops=12 * high * wide * rows, bytes_accessed=4_000_000, transcendentals=0
        ),
    )(targets, *ins)


def middle_kernel(got_a, got_b, ours_a, ours_b, send_a, keep_a, send_b, keep_b):
    for got, ours, send_ref, keep in ((got_a, ours_a, send_a, keep_a), (got_b, ours_b, send_b, keep_b)):
        keep[...] = got[0] + ours[0]
        send_ref[...] = got[1] + ours[1]


def middle(*parts):
    shape = jax.ShapeDtypeStruct(parts[0].shape[1:], jnp.float32)
    vmem = pl.BlockSpec(memory_space=pltpu.VMEM)
    return pl.pallas_call(
        middle_kernel,
        in_specs=[vmem] * 4,
        out_specs=[vmem] * 4,
        out_shape=[shape] * 4,
        compiler_params=pltpu.CompilerParams(vmem_limit_bytes=8 * MIB),
        cost_estimate=pl.CostEstimate(flops=0, bytes_accessed=5_000_000, transcendentals=0),
    )(*parts)


def pick_kernel(goal_ref, *refs):
    ins, outs = refs[:4], refs[4:]
    width = ins[0].shape[1] // 4
    for k, out in enumerate(outs):
        there = pl.ds(pl.multiple_of(goal_ref[k] * width, width), width)
        x, y, u, v = (ref[:, there] for ref in ins)
        total = jnp.concatenate([x + y, u + v], axis=0)
        out[...] = jnp.where(goal_ref[4] > 0, total, 0.0) if k == 3 else total


def pick(goals, parts):
    rows, size = parts[0].shape
    shape = jax.ShapeDtypeStruct((2 * rows, size // 4), jnp.float32)
    vmem = pl.BlockSpec(memory_space=pltpu.VMEM)
    return pl.pallas_call(
        pick_kernel,
        in_specs=[pl.BlockSpec(memory_space=pltpu.SMEM)] + [vmem] * 4,
        out_specs=[vmem] * 4,
        out_shape=[shape] * 4,
        compiler_params=pltpu.CompilerParams(vmem_limit_bytes=8 * MIB),
        cost_estimate=pl.CostEstimate(flops=0, bytes_accessed=3_000_000, transcendentals=0),
    )(goals, *parts)


def assemble_kernel(core_ref, piece_ref, turn_e_ref, turn_l_ref, out_ref, *, scale):
    w = piece_ref.shape[1]
    first = jnp.concatenate([piece_ref[:w, :], turn_e_ref[...].T, turn_l_ref[:w, :].T], axis=0)
    second = jnp.concatenate([piece_ref[w : 3 * w, :], turn_l_ref[w:, :].T], axis=0)
    last = piece_ref[3 * w :, :]
    half = out_ref.shape[0]
    is_first = core_ref[0] == 0
    for k, x in enumerate((first, second, last)):
        out_ref[:, pl.ds(k * w, w)] = jnp.where(is_first, x[:half], x[half:]) * scale


def assemble(core, parts, order):
    w = parts[0].shape[1]
    vmem = pl.BlockSpec(memory_space=pltpu.VMEM)
    return pl.pallas_call(
        functools.partial(assemble_kernel, scale=1.0 / order),
        in_specs=[pl.BlockSpec(memory_space=pltpu.SMEM)] + [vmem] * len(parts),
        out_specs=vmem,
        out_shape=jax.ShapeDtypeStruct((3 * w // 2, 3 * w), jnp.float32),
        compiler_params=pltpu.CompilerParams(vmem_limit_bytes=12 * MIB),
        cost_estimate=pl.CostEstimate(flops=0, bytes_accessed=2_000_000, transcendentals=0),
    )(core, *parts).T


def linear(chip, core, z):
    return (chip * 2 + core) * 4 + z


def send(x, pairs):
    return lax.ppermute(x, ("orb", "band"), pairs)


def mirrored(pairs):
    out = []
    for chip in range(4):
        for a, b in pairs:
            out.append((linear(chip, 0, a), linear(chip, 0, b)))
            out.append((linear(chip, 1, 3 - a), linear(chip, 1, 3 - b)))
    return out


def gather_bands(x):
    return [x] + [send(x, mirrored([(source, 2)])) for source in (0, 1, 3)]


def over_chips(flip):
    return [
        (linear(chip, core, 2 - core), linear(chip ^ flip, core, 2 - core))
        for chip in range(4)
        for core in range(2)
    ]


FLIPS = (3, 1, 2, 0)
FAR = ((0, ((0, 0, 1), (1, 1, 1))), (1, ((1, 1, 0),)), (2, ((0, 0, 0),)))
NEAR = ((1, ((0, 0, 1),)), (2, ((1, 1, 1),)), (3, ((0, 0, 0), (1, 1, 0))))
BOTH = (
    (0, ((0, 0, 1), (1, 1, 1))),
    (1, ((0, 2, 1), (1, 1, 0))),
    (2, ((0, 0, 0), (1, 3, 1))),
    (3, ((0, 2, 0), (1, 3, 0))),
)
EVERY = [(q, c, z) for q in range(4) for c in range(2) for z in range(4)]
SWAP = [(linear(q, c, z), linear(q, 1 - c, z)) for q, c, z in EVERY]
TURN = [(linear(q, c, z), linear(z, c, q)) for q, c, z in EVERY]
TURN_UP = [pair for pair in TURN if pair[0] // 4 % 2 == 1]


def simple_gram(filtered):
    partial_gram = jnp.dot(
        filtered.T,
        lax.all_gather(filtered, "band", axis=1, tiled=True),
        precision=lax.Precision.HIGH,
        preferred_element_type=jnp.float32,
    )
    return lax.psum_scatter(partial_gram, "orb", scatter_dimension=1, tiled=True)


def in_turn(hi, lo, old, order):
    core = (lax.axis_index("orb") & 1)[None]
    first = [apply_step(core, hi, lo, neighbours(x), x) for x in old]
    filtered = [apply_step(core, hi, lo, neighbours(x), x, v) for x, v in zip(first, old)]
    filtered = jnp.concatenate(filtered, axis=1)
    return filtered, simple_gram(filtered) / order


def index_tables():
    orb, z = lax.axis_index("orb"), lax.axis_index("band")
    chip, core = orb >> 1, orb & 1
    bands = jnp.stack([b + core * (3 - 2 * b) for b in (2, 0, 1, 3)])
    holder = (z == 2 - core).astype(jnp.int32)
    goals = jnp.stack([k + core * (3 - 2 * k) for k in (0, 1, 3)] + [z, holder])
    targets = jnp.stack([chip ^ flip for flip in FLIPS])
    return bands, goals, targets, core[None]


def by_symmetry(hi, lo, old, order, tables):
    bands, goals, targets, core = tables

    def one(x, halo, v=None, turned=False):
        return apply_step(core, hi, lo, halo, x, v, turned)

    v0, v1, v2 = old
    hv = [neighbours(x) for x in old]
    f0 = one(v0, hv[0])
    hf0 = neighbours(f0)
    f1 = one(v1, hv[1])
    hf1 = neighbours(f1)
    g0 = one(after_that(f0, f1), hf0, v0)
    z0 = gather_bands(g0)
    f2 = one(after_that(v2, g0), hv[2])
    hf2 = neighbours(f2)
    e1 = apply_part(core, hi, lo, after_that(f1, g0, f2, z0[1]), hf1[0], late=False)
    g1 = apply_part(core, hi, lo, hf1[1], after_that(e1, *z0[1:]), v1, late=True)
    z1 = gather_bands(g1)
    e2 = apply_part(core, hi, lo, after_that(f2, g1), hf2[0], late=False)
    g2 = apply_part(core, hi, lo, hf2[1], e2, v2, late=True)
    z2 = gather_bands(g2)
    c0, upper = chunk(bands, targets, [after_that(z0[0], g2)] + z0[1:], [])
    c1, early = chunk(bands, targets, [after_that(z1[0], upper[0])] + z1[1:], [c0], BOTH, upper)

    def first_step(parts):
        return [send(x, over_chips(flip)) for x, flip in zip(parts, (2, 1))]

    def second_step(got, ours):
        send_a, keep_a, send_b, keep_b = middle(*got, *ours)
        return [keep_a, send(send_a, over_chips(1)), keep_b, send(send_b, over_chips(2))]

    def deliver(parts):
        moved = pick(goals, parts)
        return [moved[3]] + [send(x, mirrored([(2, k)])) for k, x in zip((0, 1, 3), moved)]

    got_e = first_step(early[:2])
    c2, far = chunk(bands, targets, [after_that(z2[0], c1[0])] + z2[1:], [c0, c1], FAR)
    got_l = first_step(far)
    sums_e = second_step([after_that(got_e[0], far[0]), got_e[1]], early[2:])
    near = product(after_that(targets, sums_e[0]), [c0, c1, c2], NEAR)
    sums_l = second_step(got_l, near)
    arrived = [deliver([after_that(sums_e[0], sums_l[0])] + sums_e[1:])]
    sums_l[2] = after_that(sums_l[2], arrived[0][0])
    arrived.append(deliver(sums_l))
    filtered = jnp.concatenate([g0, g1, after_that(g2, near[0])], axis=1)
    piece = jnp.concatenate([(x[0] + x[1]) + (x[2] + x[3]) for x in arrived], axis=0)
    piece = piece + send(piece, SWAP)
    w = v0.shape[1]
    turn_e = send(piece[w : 2 * w], TURN)
    turn_l = send(piece[3 * w : 5 * w], TURN_UP)
    return filtered, assemble(core, [piece, turn_e, turn_l], order)


def body(blocks, columns, counts, vectors, symmetric):
    rows, width = vectors.shape
    order = rows * lax.axis_size("orb")
    slot_of = slot_table(columns, counts)
    later = vectors
    if symmetric:
        tables = index_tables()
        slot_of, tables, later = lax.optimization_barrier((slot_of, tables, vectors))
    old = [
        (later if c else vectors)[:, c : min(c + LANES, width)] for c in range(0, width, LANES)
    ]
    hi, lo = densify(slot_of, blocks)
    if symmetric:
        return by_symmetry(hi, lo, old, order, tables)
    return in_turn(hi, lo, old, order)


def solution(mesh):
    placed = (P("orb", None, None, None), P("orb", None), P("orb"), P("orb", "band"))

    def whole(blocks, columns, counts, vectors):
        symmetric = (
            mesh.shape["orb"] == 8 and mesh.shape["band"] == 4 and vectors.shape[1] == 3 * LANES
        )
        return body(blocks, columns, counts, vectors, symmetric)

    return jax.shard_map(
        whole,
        mesh=mesh,
        in_specs=placed,
        out_specs=(P("orb", "band"), P("band", "orb")),
        check_vma=False,
    )
```
